32 devices in a mesh: seq: 8 (over y, x, core), batch: 4 (over z).
Axes of the slice: x: 2, y: 2, z: 4, core: 2. Of those that a mesh axis runs over, the one named last changes fastest.
Arguments:
- tokens: bfloat16 [8, 512, 2048], P('batch', 'seq'), may hold values from -6 to 6
- grad_out: bfloat16 [8, 512, 2048], P('batch', 'seq'), may hold values from -6 to 6
- resets: int32 [8], P('batch'), may hold values from 1 to 512, as said below
- w_proj: bfloat16 [2048, 12288], P(('seq', 'batch')), may hold values from -0.125 to 0.125
- w_small: bfloat16 [2048, 32], P(('seq', 'batch')), may hold values from -0.125 to 0.125
- w_out: bfloat16 [4096, 2048], P(('seq', 'batch')), may hold values from -0.1875 to 0.1875
- w_gu: bfloat16 [2048, 11264], P(('seq', 'batch')), may hold values from -0.125 to 0.125
- w_down: bfloat16 [5632, 2048], P(('seq', 'batch')), may hold values from -0.078125 to 0.078125
- norm_in: float32 [2048], replicated, may hold values from 0.5 to 1.5
- norm_ff: float32 [2048], replicated, may hold values from 0.5 to 1.5
- norm_head: float32 [256], replicated, may hold values from 0.5 to 1.5
- conv_w: float32 [4, 8192], replicated, may hold values from -2.5 to 2.5
- a_log: float32 [16], replicated, may hold values from 0 to 2.77
- dt_bias: float32 [16], replicated, may hold values from -8 to -3
Outputs:
- block_out: bfloat16 [8, 512, 2048], P('batch', 'seq')
- d_tokens: bfloat16 [8, 512, 2048], P('batch', 'seq')
- g_proj: float32 [2048, 12288], P(('seq', 'batch'))
- g_small: float32 [2048, 32], P(('seq', 'batch'))
- g_out: float32 [4096, 2048], P(None, ('seq', 'batch'))
- g_gu: float32 [2048, 11264], P(('seq', 'batch'))
- g_down: float32 [5632, 2048], P(None, ('seq', 'batch'))
- g_norm_in: float32 [2048], replicated
- g_norm_ff: float32 [2048], replicated
- g_norm_head: float32 [256], replicated
- g_conv: float32 [4, 8192], replicated
- g_alog: float32 [16], replicated
- g_dt: float32 [16], replicated
The draws below stay inside these ranges and needn't reach their ends.
Inputs may be any that keep to these rules, and one draw needn't show every extreme that they name: resets[r] is the position in row r where a second sequence begins, where the state and the short convolution restart; it lies within the first or the last 64 positions of its row, and exactly one row has resets = 512, that row being a single sequence.
All inputs are finite; a program needn't handle non-finite values.
Results may differ from the reference program's by a relative error of at most 0.014.
Values may be sent and summed in bfloat16 or wider, within the bound.
No kernel may reach another device: no remote copies, remote signals or barrier semaphores. Data moves between devices by JAX's collectives and lax.ppermute only.
A program may use at most 960 MiB of HBM per device.

```python
from functools import partial
import jax
import jax.numpy as jnp
from jax import lax

D = 2048
H = 16
DK = 128
DV = 256
FF = 5632
CONV = 4
CH = 64
SPAN = 64
KW = 2048
VW = 4096
CW = 8192
ROWS = 8
L = 512


def draw_resets(key, part):
    key = jax.random.fold_in(key, 7)
    pick_key, side_key, chosen_key = jax.random.split(key, 3)
    nearby = jax.random.randint(pick_key, (ROWS,), 1, SPAN)
    at_end = jax.random.randint(side_key, (ROWS,), 0, 2)
    located = jnp.where(at_end == 1, L - nearby, nearby)
    single_row = jax.random.randint(chosen_key, (), 0, ROWS)
    return jnp.where(jnp.arange(ROWS) == single_row, L, located).astype(jnp.int32)


def level_of(stream_key, shape, shards, low, largest):
    factor_of, own = 1.0, jax.random.fold_in(stream_key, 6)
    for position, parts in shards:
        draws = jnp.exp(jax.random.uniform(jax.random.fold_in(own, position), (parts,), jnp.float32, low / len(shards), largest / len(shards)))
        factor_of = factor_of * jnp.repeat(draws, shape[position] // parts).reshape([-1 if axis == position else 1 for axis in range(len(shape))])
    return factor_of


def normal_values(stream_key, extent, width, reach, cuts=(), held_as=jnp.bfloat16):
    values = jax.random.normal(stream_key, extent, jnp.float32) * width
    if len(cuts) > 0:
        values = level_of(stream_key, extent, cuts, -0.22, 0.18) * values
    return jnp.clip(values, min=-reach, max=reach).astype(held_as)


def setup_inputs(seed: int = 0) -> dict:
    key_of = jax.random.split(jax.random.key(seed), 15)
    return {
        "tokens": normal_values(key_of[0], (ROWS, L, D), 1.0, 6.0, ((0, 4), (1, 8))),
        "grad_out": normal_values(key_of[1], (ROWS, L, D), 1.0, 6.0, ((0, 4), (1, 8))),
        "resets": draw_resets(jax.random.fold_in(key_of[14], 71), 0),
        "w_proj": normal_values(key_of[3], (D, CW + VW), D ** -0.5, 0.125, ((0, 32),)),
        "w_small": normal_values(key_of[4], (D, 2 * H), D ** -0.5, 0.125, ((0, 32),)),
        "w_out": normal_values(key_of[5], (VW, D), (VW // 4) ** -0.5, 0.1875, ((0, 32),)),
        "w_gu": normal_values(key_of[6], (D, 2 * FF), D ** -0.5, 0.125, ((0, 32),)),
        "w_down": normal_values(key_of[7], (FF, D), FF ** -0.5, 0.078125, ((0, 32),)),
        "norm_in": jnp.clip(1.0 + 0.1 * jax.random.normal(key_of[8], (D,), jnp.float32), 0.5, 1.5),
        "norm_ff": jnp.clip(1.0 + 0.1 * jax.random.normal(key_of[9], (D,), jnp.float32), 0.5, 1.5),
        "norm_head": jnp.clip(1.0 + 0.1 * jax.random.normal(key_of[10], (DV,), jnp.float32), 0.5, 1.5),
        "conv_w": normal_values(key_of[11], (CONV, CW), 0.5, 2.5, (), jnp.float32),
        "a_log": jnp.clip(jax.random.uniform(key_of[12], (H,), jnp.float32, 0.0, 2.77), 0.0, 2.77),
        "dt_bias": jnp.clip(jax.random.uniform(key_of[13], (H,), jnp.float32, -8.0, -3.0), -8.0, -3.0),
    }


EPS_NORM = 1e-06
EPS_HEAD = 1e-05
EPS_UNIT = 1e-06
highest = lax.Precision.HIGHEST

@jax.custom_vjp
def low(v):
    return lax.optimization_barrier(v.astype(jnp.bfloat16)).astype(jnp.float32)

@jax.custom_vjp
def low_back(v):
    return v

def low_keep(v):
    return (low(v), None)

def low_pass(kept, grad):
    return (grad,)

def back_keep(v):
    return (v, None)

def back_low(kept, grad):
    return (low(grad),)
low.defvjp(low_keep, low_pass)
low_back.defvjp(back_keep, back_low)

def matmul_high(left_op, right_op):
    return jnp.matmul(left_op, right_op, precision=highest)

def rms_scale(values, scale_gain):
    return values * lax.rsqrt(lax.optimization_barrier(jnp.mean(values * values, axis=-1, keepdims=True)) + EPS_NORM) * scale_gain

def unit_rows(values):
    return values * lax.rsqrt(lax.optimization_barrier(jnp.sum(values * values, axis=-1, keepdims=True)) + EPS_UNIT)

def delta_rule(query_rows, key_rows, value_rows, beta_gate, keep_rate):
    row_count = query_rows.shape[0]

    def token_step(state, inputs):
        query_t, key_t, value_t, beta_t, keep_t = inputs
        recall = jnp.einsum('rhk,rhkv->rhv', key_t, state, precision=highest)
        erased = state - beta_t[..., None, None] * key_t[..., :, None] * recall[..., None, :]
        state = keep_t[..., None, None] * erased + beta_t[..., None, None] * key_t[..., :, None] * value_t[..., None, :]
        return (state, jnp.einsum('rhk,rhkv->rhv', query_t, state, precision=highest))

    def block_step(state, inputs):
        return lax.scan(token_step, state, inputs)

    def arrange(array):
        moved = jnp.moveaxis(array, 1, 0)
        return moved.reshape((L // CH, CH) + moved.shape[1:])
    start_state = jnp.zeros((row_count, H, DK, DV), jnp.float32)
    stacked_in = tuple((arrange(item) for item in (query_rows, key_rows, value_rows, beta_gate, keep_rate)))
    final_state, outputs = lax.scan(jax.checkpoint(block_step), start_state, stacked_in)
    return jnp.moveaxis(outputs.reshape((L,) + outputs.shape[2:]), 0, 1)

def forward(tokens, w_proj, w_small, w_out, w_gu, w_down, norm_in, norm_ff, norm_head, conv_w, a_log, dt_bias, resets):
    row_count = tokens.shape[0]
    h_in = low(rms_scale(tokens, norm_in))
    projected = matmul_high(h_in, w_proj)
    conv_in = low_back(low(projected[..., :CW]))
    gate_head = low_back(projected[..., CW:])
    small_pre = matmul_high(h_in, w_small)
    padded = jnp.pad(conv_in, ((0, 0), (CONV - 1, 0), (0, 0)))
    positions = jnp.arange(L, dtype=jnp.int32)[None, :]
    starts = resets.astype(jnp.int32)[:, None]
    seg_start = jnp.where(positions >= starts, starts, 0)
    conv_out = jnp.zeros((row_count, L, CW), jnp.float32)
    for tap_pos in range(CONV):
        valid_tap = (positions - (CONV - 1) + tap_pos >= seg_start).astype(jnp.float32)
        conv_out = conv_out + conv_w[tap_pos] * padded[:, tap_pos:tap_pos + L] * valid_tap[..., None]
    active = jax.nn.silu(conv_out)
    query_rows = unit_rows(active[..., :KW].reshape(row_count, L, H, DK)) * DK ** (-0.5)
    key_rows = unit_rows(active[..., KW:2 * KW].reshape(row_count, L, H, DK))
    value_rows = active[..., 2 * KW:].reshape(row_count, L, H, DV)
    beta_gate = jax.nn.sigmoid(small_pre[..., :H])
    log_decay = -jnp.exp(a_log) * jax.nn.softplus(small_pre[..., H:] + dt_bias)
    keep_rate = jnp.exp(log_decay) * (positions != starts).astype(jnp.float32)[..., None]
    mixer_out = delta_rule(query_rows, key_rows, value_rows, beta_gate, keep_rate)
    scaled = mixer_out * lax.rsqrt(lax.optimization_barrier(jnp.mean(mixer_out * mixer_out, axis=-1, keepdims=True)) + EPS_HEAD) * norm_head
    gated = scaled * jax.nn.silu(gate_head.reshape(row_count, L, H, DV))
    z_rows = low(gated.reshape(row_count, L, VW))
    residual = tokens + low_back(matmul_high(z_rows, w_out))
    h_ff = low(rms_scale(residual, norm_ff))
    gate_up = low_back(matmul_high(h_ff, w_gu))
    hidden = low(jax.nn.silu(gate_up[..., :FF]) * gate_up[..., FF:])
    return residual + low_back(matmul_high(hidden, w_down))

def reference(tokens, grad_out, resets, w_proj, w_small, w_out, w_gu, w_down, norm_in, norm_ff, norm_head, conv_w, a_log, dt_bias):
    floats = tuple((item.astype(jnp.float32) for item in (tokens, w_proj, w_small, w_out, w_gu, w_down)))
    result, pull_back = jax.vjp(partial(forward, resets=resets), *floats, norm_in, norm_ff, norm_head, conv_w, a_log, dt_bias)
    grads = pull_back(grad_out.astype(jnp.float32))
    return (result.astype(jnp.bfloat16), grads[0].astype(jnp.bfloat16), grads[1], grads[2], grads[3], grads[4], grads[5], grads[6], grads[7], grads[8], grads[9], grads[10], grads[11])
```

```python
from functools import partial

import jax
import jax.numpy as jnp
from jax import lax
from jax.experimental import pallas as pl
from jax.experimental.pallas import tpu as pltpu
from jax.sharding import PartitionSpec as P

D = 2048
H = 16
DK = 128
DV = 256
FF = 5632
CH = 64
KW = 2048
VW = 4096
CW = 8192
TAPS = 4
LANES = 128

EPS_NORM = 1e-06
EPS_HEAD = 1e-05
EPS_UNIT = 1e-06
f32 = jnp.float32
bf16 = jnp.bfloat16
VMEM_BYTES = 32 * 1024 * 1024
KERNEL_COST = pl.CostEstimate(flops=60_000_000_000, bytes_accessed=40_000_000, transcendentals=0)


def dot_in(left, right, contract, precision):
    return lax.dot_general(
        left,
        right,
        (((contract[0],), (contract[1],)), ((), ())),
        precision=precision,
        preferred_element_type=f32,
    )


def fine(left, right, contract=(1, 0)):
    return dot_in(left, right, contract, lax.Precision.HIGHEST)


def coarse(left, right, contract=(1, 0)):
    return dot_in(left, right, contract, lax.Precision.HIGHEST)


def position_masks(reset, chunk):
    rows = lax.broadcasted_iota(jnp.int32, (CH, CH), 0)
    cols = lax.broadcasted_iota(jnp.int32, (CH, CH), 1)
    time = lax.broadcasted_iota(jnp.int32, (CH, 1), 0)
    offset = reset - chunk * CH
    cut = jnp.where(offset < 0, CH, offset)
    apart = (rows >= cut) & (cols < cut)
    causal = jnp.where((rows >= cols) & ~apart, 1.0, 0.0)
    strict = jnp.where((rows > cols) & ~apart, 1.0, 0.0)
    in_first = jnp.where(time < cut, 1.0, 0.0)
    last_first = jnp.where(CH - 1 < cut, 1.0, 0.0)
    in_last = jnp.where((time >= cut) | (cut > CH - 1), 1.0, 0.0)
    begin = jnp.where(time >= offset, offset, -chunk * CH)
    taps = [jnp.where(time - (TAPS - 1) + j >= begin, 1.0, 0.0) for j in range(TAPS)]
    return causal, strict, in_first, last_first, in_last, taps


def gates(small, aux):
    beta = jax.nn.sigmoid(small)
    shifted = small + aux[1:2]
    soft = jnp.maximum(shifted, 0.0) + jnp.log1p(jnp.exp(-jnp.abs(shifted)))
    return beta, -aux[0:1] * soft, shifted


def running(values, reverse=False):
    rows = lax.broadcasted_iota(jnp.int32, (CH, CH), 0)
    cols = lax.broadcasted_iota(jnp.int32, (CH, CH), 1)
    keep = (cols >= rows) if reverse else (cols <= rows)
    return fine(jnp.where(keep, 1.0, 0.0), values)


def as_rows(total):
    pick_row = lax.broadcasted_iota(jnp.int32, (LANES, LANES), 0)
    pick_col = lax.broadcasted_iota(jnp.int32, (LANES, LANES), 1)
    return fine(jnp.where(pick_row == pick_col, 1.0, 0.0), total, (1, 1))


def inverse_unit_lower(strict_part):
    rows = lax.broadcasted_iota(jnp.int32, (CH, CH), 0)
    cols = lax.broadcasted_iota(jnp.int32, (CH, CH), 1)
    eye = jnp.where(rows == cols, 1.0, 0.0)
    diag = jnp.where(rows // 16 == cols // 16, strict_part, 0.0)
    inv = eye - diag
    power = diag
    for _ in range(3):
        power = fine(power, power)
        inv = inv + fine(inv, power)
    for size in (16, 32):
        off = jnp.where((rows // size != cols // size) & (rows // (2 * size) == cols // (2 * size)), strict_part, 0.0)
        inv = inv - fine(fine(inv, off), inv)
    return inv


def conv_taps(ext_ref, row, conv_w, taps):
    out = None
    for j in range(TAPS):
        part = conv_w[j : j + 1] * (ext_ref[row, 8 - (TAPS - 1) + j : 8 - (TAPS - 1) + j + CH, :] * taps[j])
        out = part if out is None else out + part
    return out


def unit(values):
    return lax.rsqrt(jnp.sum(values * values, axis=-1, keepdims=True) + EPS_UNIT)


def head_parts(active, head, heads):
    q = active[:, head * DK : (head + 1) * DK]
    k = active[:, heads * DK + head * DK : heads * DK + (head + 1) * DK]
    v = active[:, 2 * heads * DK + head * DV : 2 * heads * DK + (head + 1) * DV]
    return q, k, v


def decay_terms(total, total_rows, head, heads, masks):
    causal, strict, in_first, last_first, in_last, _ = masks
    lane = heads + head
    col = total[:, lane : lane + 1]
    row = total_rows[lane : lane + 1, :]
    ratios = jnp.exp(jnp.where(causal > 0, col - row, 0.0)) * causal
    last = col[CH - 1 : CH, :]
    start_fade = jnp.exp(col) * in_first
    start_last = jnp.exp(last) * last_first
    end_fade = jnp.exp(jnp.where(in_last > 0, last - col, 0.0)) * in_last
    return ratios, start_fade, start_last, end_fade


def forward_kernel(
    heads, pos_ref, reset_ref, proj, conv_w_ref, aux_ref, outs, state_out, inv_out, delta_out, ext, state
):
    chunk = pl.program_id(0)
    width = heads * (2 * DK + DV)

    @pl.when(chunk == 0)
    def _():
        ext[...] = jnp.zeros_like(ext)
        state[...] = jnp.zeros_like(state)

    state_out[0] = state[...]
    conv_w = conv_w_ref[...]
    aux = aux_ref[...]
    for row in range(proj.shape[0]):
        masks = position_masks(reset_ref[row], chunk)
        ext[row, 0:8, :] = ext[row, CH : CH + 8, :]
        ext[row, 8:, :] = proj[row, 0, :, :width].astype(bf16).astype(f32)
        conv = conv_taps(ext, row, conv_w, masks[5])
        active = conv * jax.nn.sigmoid(conv)
        beta_all, decay, _ = gates(proj[row, 0, :, width : width + LANES], aux)
        total = running(decay)
        total_rows = as_rows(total)
        for head in range(heads):
            at = row * heads + head
            q, k, v = head_parts(active, head, heads)
            q = q * (unit(q) * DK**-0.5)
            k = k * unit(k)
            beta = beta_all[:, head : head + 1]
            ratios, start_fade, start_last, end_fade = decay_terms(total, total_rows, head, heads, masks)
            both = jnp.concatenate([q, k], axis=0)
            pair = fine(both, k, (1, 1))
            inv = inverse_unit_lower(beta * (ratios * masks[1] * pair[CH:]))
            old = state[at]
            read = coarse(both, old)
            delta = coarse(inv, beta * (v - start_fade * read[CH:]))
            out = start_fade * read[:CH] + coarse(ratios * pair[:CH], delta)
            state[at] = start_last * old + coarse(end_fade * k, delta, (0, 0))
            outs[row, 0, :, head * DV : (head + 1) * DV] = out
            inv_out[0, at] = inv
            delta_out[0, at] = delta


def backward_kernel(
    heads,
    chunks,
    pos_ref,
    reset_ref,
    proj,
    tail,
    d_out,
    conv_w_ref,
    aux_ref,
    state_ref,
    inv_ref,
    delta_ref,
    d_proj,
    g_conv,
    g_decay,
    ext,
    dext,
    d_state,
):
    step = pl.program_id(0)
    chunk = chunks - 1 - step
    width = heads * (2 * DK + DV)

    @pl.when(step == 0)
    def _():
        dext[...] = jnp.zeros_like(dext)
        d_state[...] = jnp.zeros_like(d_state)
        g_conv[...] = jnp.zeros_like(g_conv)
        g_decay[...] = jnp.zeros_like(g_decay)

    conv_w = conv_w_ref[...]
    aux = aux_ref[...]
    lane_ids = lax.broadcasted_iota(jnp.int32, (CH, LANES), 1)
    ones = jnp.ones((CH, LANES), f32)
    for row in range(proj.shape[0]):
        masks = position_masks(reset_ref[row], chunk)
        taps = masks[5]
        ext[row, 0:8, :] = tail[row, 0].astype(bf16).astype(f32)
        ext[row, 8:, :] = proj[row, 0, :, :width].astype(bf16).astype(f32)
        conv = conv_taps(ext, row, conv_w, taps)
        sig = jax.nn.sigmoid(conv)
        active = conv * sig
        small = proj[row, 0, :, width : width + LANES]
        beta_all, decay, shifted = gates(small, aux)
        total = running(decay)
        total_rows = as_rows(total)
        d_beta_all = jnp.zeros((CH, LANES), f32)
        d_total = jnp.zeros((CH, LANES), f32)
        d_active = []
        for head in range(heads):
            at = row * heads + head
            a_q, a_k, v = head_parts(active, head, heads)
            q_scale = unit(a_q)
            k_scale = unit(a_k)
            q = a_q * (q_scale * DK**-0.5)
            k = a_k * k_scale
            beta = beta_all[:, head : head + 1]
            ratios, start_fade, start_last, end_fade = decay_terms(total, total_rows, head, heads, masks)
            both = jnp.concatenate([q, k], axis=0)
            pair = fine(both, k, (1, 1))
            key_key, query_key = pair[CH:], pair[:CH]
            old = state_ref[0, at]
            inv = inv_ref[0, at]
            delta = delta_ref[0, at]
            do = d_out[row, 0, :, head * DV : (head + 1) * DV]
            ds = d_state[at]
            read = coarse(both, old)
            readings = ratios * query_key
            faded = end_fade * k
            d_delta = coarse(readings, do, (0, 0)) + coarse(faded, ds)
            d_right = coarse(inv, d_delta, (0, 0))
            d_pair = coarse(jnp.concatenate([do, d_right], axis=0), delta, (1, 1))
            d_faded = coarse(delta, ds, (1, 1))
            d_read = jnp.concatenate([start_fade * do, -(beta * start_fade) * d_right], axis=0)
            d_both = coarse(d_read, old, (1, 1))
            d_state[at] = start_last * ds + coarse(both, d_read, (0, 0))
            d_v = beta * d_right
            d_read_pair = d_pair[:CH] * ratios
            d_sys = -d_pair[CH:] * (ratios * masks[1])
            d_key_key = beta * d_sys
            moved = d_key_key * key_key + d_read_pair * query_key
            recall = read[CH:]
            d_beta = jnp.sum(d_right * (v - start_fade * recall), axis=-1, keepdims=True) + jnp.sum(
                d_sys * key_key, axis=-1, keepdims=True
            )
            d_start = jnp.sum(do * read[:CH], axis=-1, keepdims=True) - beta * jnp.sum(
                d_right * recall, axis=-1, keepdims=True
            )
            d_end = jnp.sum(d_faded * k, axis=-1, keepdims=True) * end_fade
            d_last = jnp.sum(d_end, axis=0, keepdims=True) + start_last * jnp.sum(
                jnp.sum(ds * old, axis=-1, keepdims=True), axis=0, keepdims=True
            )
            last_row = lax.broadcasted_iota(jnp.int32, (CH, 1), 0) == CH - 1
            d_col = (
                jnp.sum(moved, axis=-1, keepdims=True)
                - fine(moved, ones, (0, 0))[:, 0:1]
                + d_start * start_fade
                - d_end
                + jnp.where(last_row, d_last, 0.0)
            )
            d_q = d_both[:CH] + coarse(d_read_pair, k)
            d_k = (
                d_both[CH:]
                + coarse(d_read_pair, q, (0, 0))
                + coarse(d_key_key, k)
                + coarse(d_key_key, k, (0, 0))
                + end_fade * d_faded
            )
            d_aq = (q_scale * DK**-0.5) * (d_q - a_q * (q_scale * q_scale * jnp.sum(a_q * d_q, axis=-1, keepdims=True)))
            d_ak = k_scale * (d_k - a_k * (k_scale * k_scale * jnp.sum(a_k * d_k, axis=-1, keepdims=True)))
            d_active.append((d_aq, d_ak, d_v))
            d_beta_all = jnp.where(lane_ids == head, d_beta, d_beta_all)
            d_total = jnp.where(lane_ids == heads + head, d_col, d_total)
        d_decay = running(d_total, reverse=True)
        d_shift = d_decay * (-aux[0:1]) * jax.nn.sigmoid(shifted)
        d_small = d_beta_all * beta_all * (1.0 - beta_all) + d_shift
        g_decay[0:1, :] += jnp.sum(d_decay * decay, axis=0, keepdims=True)
        g_decay[1:2, :] += jnp.sum(d_shift, axis=0, keepdims=True)
        d_act = jnp.concatenate([d_active[h][i] for i in range(3) for h in range(heads)], axis=1)
        d_conv = d_act * (sig * (1.0 + conv * (1.0 - sig)))
        d_in = None
        for j in range(TAPS):
            masked = d_conv * taps[j]
            g_conv[j : j + 1, :] += jnp.sum(
                masked * ext[row, 8 - (TAPS - 1) + j : 8 - (TAPS - 1) + j + CH, :], axis=0, keepdims=True
            )
            dext[row, j, 0:CH, :] = masked
            shift = TAPS - 1 - j
            part = conv_w[j : j + 1] * dext[row, j, shift : shift + CH, :]
            d_in = part if d_in is None else d_in + part
            dext[row, j, CH : CH + 8, :] = masked[0:8]
        d_proj[row, 0, :, :width] = d_in.astype(bf16)
        d_proj[row, 0, :, width : width + LANES] = d_small.astype(bf16)


def params():
    return pltpu.CompilerParams(dimension_semantics=("arbitrary",), vmem_limit_bytes=VMEM_BYTES)


def whole(array):
    return pl.BlockSpec(array.shape, lambda c, pos, rst: (0,) * array.ndim)


def mixer_forward(proj, pos, resets, conv_w, aux):
    rows_n, chunks, _, total = proj.shape
    width = total - LANES
    heads = width // (2 * DK + DV)
    units = rows_n * heads
    spec = lambda w: pl.BlockSpec((rows_n, 1, CH, w), lambda c, pos, rst: (0, pos[c], 0, 0))
    kept = lambda *s: pl.BlockSpec((1, units) + s, lambda c, pos, rst: (c, 0, 0, 0))
    return pl.pallas_call(
        partial(forward_kernel, heads),
        grid_spec=pltpu.PrefetchScalarGridSpec(
            num_scalar_prefetch=2,
            grid=(chunks,),
            in_specs=[spec(total), whole(conv_w), whole(aux)],
            out_specs=[spec(heads * DV), kept(DK, DV), kept(CH, CH), kept(CH, DV)],
            scratch_shapes=[pltpu.VMEM((rows_n, CH + 8, width), f32), pltpu.VMEM((units, DK, DV), f32)],
        ),
        out_shape=[
            jax.ShapeDtypeStruct((rows_n, chunks, CH, heads * DV), f32),
            jax.ShapeDtypeStruct((chunks, units, DK, DV), f32),
            jax.ShapeDtypeStruct((chunks, units, CH, CH), f32),
            jax.ShapeDtypeStruct((chunks, units, CH, DV), f32),
        ],
        cost_estimate=KERNEL_COST,
        compiler_params=params(),
        name="delta_forward",
    )(pos, resets, proj, conv_w, aux)


def mixer_backward(proj, d_out, pos, resets, conv_w, aux, states, invs, deltas):
    rows_n, chunks, _, total = proj.shape
    width = total - LANES
    heads = width // (2 * DK + DV)
    units = rows_n * heads
    back = lambda c: chunks - 1 - c
    spec = lambda w: pl.BlockSpec((rows_n, 1, CH, w), lambda c, pos, rst: (0, pos[back(c)], 0, 0))
    tail = pl.BlockSpec(
        (rows_n, 1, 8, width), lambda c, pos, rst: (0, pos[jnp.maximum(back(c) - 1, 0)], CH // 8 - 1, 0)
    )
    kept = lambda *s: pl.BlockSpec((1, units) + s, lambda c, pos, rst: (back(c), 0, 0, 0))
    return pl.pallas_call(
        partial(backward_kernel, heads, chunks),
        grid_spec=pltpu.PrefetchScalarGridSpec(
            num_scalar_prefetch=2,
            grid=(chunks,),
            in_specs=[spec(total), tail, spec(heads * DV), whole(conv_w), whole(aux)]
            + [kept(DK, DV), kept(CH, CH), kept(CH, DV)],
            out_specs=[
                spec(total),
                pl.BlockSpec((8, width), lambda c, pos, rst: (0, 0)),
                pl.BlockSpec((8, LANES), lambda c, pos, rst: (0, 0)),
            ],
            scratch_shapes=[
                pltpu.VMEM((rows_n, CH + 8, width), f32),
                pltpu.VMEM((rows_n, TAPS, CH + 8, width), f32),
                pltpu.VMEM((units, DK, DV), f32),
            ],
        ),
        out_shape=[
            jax.ShapeDtypeStruct((rows_n, chunks, CH, total), bf16),
            jax.ShapeDtypeStruct((8, width), f32),
            jax.ShapeDtypeStruct((8, LANES), f32),
        ],
        cost_estimate=KERNEL_COST,
        compiler_params=params(),
        name="delta_backward",
    )(pos, resets, proj, proj, d_out, conv_w, aux, states, invs, deltas)


def swap(value, axis, bit):
    return lax.ppermute(value, axis, [(i, i ^ bit) for i in range(lax.axis_size(axis))])


def routes(axis):
    bits = [1 << i for i in range(lax.axis_size(axis).bit_length() - 1)]
    return [bits[1:] + bits[:1], bits[:0:-1] + bits[:1]]


def slot_of(relative, chunks):
    return (relative >> 1) | ((relative & 1) * (chunks // 2))


def gather_rows(rows, axis):
    size = lax.axis_size(axis)
    orders = routes(axis)
    laid = []
    for row in range(rows.shape[0]):
        order = orders[row % 2]
        held = rows[row][None]
        names = [0]
        for bit in order[:-1]:
            held = jnp.concatenate([held, swap(held, axis, bit)], axis=0)
            names = names + [n ^ bit for n in names]
        other = swap(held, axis, order[-1])
        place = {name: i for i, name in enumerate(names)}
        for part in (held, other):
            if names == sorted(names):
                laid.append(part)
            else:
                laid.extend(part[place[n]][None] for n in sorted(names))
    whole_rows = jnp.concatenate(laid, axis=0)
    return whole_rows.reshape((rows.shape[0], size) + rows.shape[1:])


def scatter_rows(parts, axis):
    size = lax.axis_size(axis)
    orders = routes(axis)
    out = []
    for row in range(parts.shape[0]):
        order = orders[row % 2][::-1]
        half = size // 2
        held = parts[row, :half].astype(f32) + swap(parts[row, half:], axis, order[0]).astype(f32)
        names = list(range(0, size, 2))
        for bit in order[1:]:
            keep = [n for n in names if not n & bit]
            sent = jnp.stack([held[names.index(n ^ bit)] for n in keep]).astype(bf16)
            kept = jnp.stack([held[names.index(n)] for n in keep])
            held = kept + swap(sent, axis, bit).astype(f32)
            names = keep
        out.append(held[0])
    return jnp.stack(out)


def after(value, *earlier):
    return lax.optimization_barrier((value,) + earlier)[0]


def sum_all(value, axes):
    for axis in axes:
        for i in range(lax.axis_size(axis).bit_length() - 1):
            value = value + swap(value, axis, 1 << i)
    return value


def mm(left, right):
    return jnp.dot(left, right, preferred_element_type=f32)


def contract_rows(left, right):
    return lax.dot_general(left, right, (((0,), (0,)), ((), ())), preferred_element_type=f32)


def contract_cols(left, right):
    return lax.dot_general(left, right, (((1,), (1,)), ((), ())), preferred_element_type=f32)


def rms_scale(values, scale_gain):
    return values * lax.rsqrt(jnp.mean(values * values, axis=-1, keepdims=True) + EPS_NORM) * scale_gain


def head_norm(mixer_out, gate_head, norm_head):
    scaled = (
        mixer_out * lax.rsqrt(jnp.mean(mixer_out * mixer_out, axis=-1, keepdims=True) + EPS_HEAD) * norm_head
    )
    return scaled * jax.nn.silu(gate_head)


def head_norms(mixer_out, gate_head, norm_head):
    parts = [slice(i, i + DV) for i in range(0, gate_head.shape[-1], DV)]
    return jnp.concatenate([head_norm(mixer_out[:, p], gate_head[:, p], norm_head) for p in parts], axis=1)


def glu_hidden(gate_half, up_half):
    return jax.nn.silu(gate_half) * up_half


def exchanged(packed):
    return lax.all_to_all(packed, "seq", split_axis=0, concat_axis=0, tiled=True)


def stacked(blocks):
    full = lax.all_gather(blocks, "batch", axis=0, tiled=False)
    return full.reshape(-1, blocks.shape[-1])


def summed(partial_grad):
    own = lax.psum_scatter(partial_grad, "batch", scatter_dimension=0, tiled=True)
    return own.reshape(lax.axis_size("seq"), -1, own.shape[-1])


def shards(
    tokens,
    grad_out,
    resets,
    w_proj,
    w_small,
    w_out,
    w_gu,
    w_down,
    norm_in,
    norm_ff,
    norm_head,
    conv_w,
    a_log,
    dt_bias,
):
    size = lax.axis_size("seq")
    groups = lax.axis_size("batch")
    me = lax.axis_index("seq")
    batch_rows, span_len, _ = tokens.shape
    own_rows = w_proj.shape[0]
    heads = H // size
    ff = FF // size
    key_w, val_w = heads * DK, heads * DV
    conv_cols = 2 * key_w + val_w
    tok_rows = batch_rows * span_len
    shape_in = (batch_rows, span_len, D)
    everyone = (batch_rows, size, span_len)

    def shuffled(array):
        lead = array.shape[:-1]
        return array.reshape(lead + (size, groups, own_rows)).swapaxes(-3, -2).reshape(lead + (D,))

    def restored(array):
        lead = array.shape[:-1]
        return array.reshape(lead + (groups, size, own_rows)).swapaxes(-3, -2).reshape(lead + (D,))

    small = jnp.concatenate(
        [w_small[:, :H].reshape(own_rows, size, heads), w_small[:, H:].reshape(own_rows, size, heads)], axis=-1
    )
    small = jnp.pad(small, ((0, 0), (0, 0), (0, LANES - 2 * heads)))
    packed_mix = jnp.concatenate(
        [
            w_proj[:, :KW].reshape(own_rows, size, key_w),
            w_proj[:, KW : 2 * KW].reshape(own_rows, size, key_w),
            w_proj[:, 2 * KW : CW].reshape(own_rows, size, val_w),
            small,
        ],
        axis=-1,
    ).transpose(1, 0, 2)
    out_w = lax.all_gather(shuffled(w_out), "batch", axis=0, tiled=True)
    moved_mix = exchanged(packed_mix)
    mix_w = stacked(after(moved_mix, out_w))
    packed_gate, packed_gu = after(
        (
            w_proj[:, CW:].reshape(own_rows, size, val_w).transpose(1, 0, 2),
            w_gu.reshape(own_rows, 2, size, ff).transpose(2, 0, 1, 3).reshape(size, own_rows, 2 * ff),
        ),
        moved_mix,
    )
    gate_w = stacked(after(exchanged(packed_gate), mix_w))
    gu_w = stacked(after(exchanged(packed_gu), mix_w))
    down_w = lax.all_gather(after(shuffled(w_down), mix_w), "batch", axis=0, tiled=True)

    order = jnp.arange(size, dtype=jnp.int32) ^ me.astype(jnp.int32)
    slots = slot_of(order, size)
    conv_l = jnp.concatenate(
        [
            lax.dynamic_slice_in_dim(conv_w, me * key_w, key_w, 1),
            lax.dynamic_slice_in_dim(conv_w, KW + me * key_w, key_w, 1),
            lax.dynamic_slice_in_dim(conv_w, 2 * KW + me * val_w, val_w, 1),
        ],
        axis=1,
    )
    at_heads = (heads, LANES - 2 * heads)
    aux = jnp.pad(
        jnp.stack(
            [
                lax.dynamic_slice_in_dim(jnp.exp(a_log), me * heads, heads),
                lax.dynamic_slice_in_dim(dt_bias, me * heads, heads),
            ]
        ),
        ((0, 6), at_heads),
    )

    flat_in = shuffled(tokens).astype(f32)
    gain_in, gain_ff = shuffled(norm_in), shuffled(norm_ff)
    normed_in, pull_norm_in = jax.vjp(rms_scale, flat_in, gain_in)
    h_in = gather_rows(normed_in.astype(bf16), "seq").reshape(-1, D)
    proj = mm(h_in, mix_w).reshape(everyone + (conv_cols + LANES,))
    mixed, states, invs, deltas = mixer_forward(proj, slots, resets, conv_l, aux)
    gate = mm(h_in, gate_w)
    heads_out, pull_head = jax.vjp(head_norms, mixed.reshape(-1, val_w), gate, norm_head)
    z_rows = heads_out.astype(bf16)
    residual = flat_in + scatter_rows(mm(z_rows, out_w).astype(bf16).reshape(everyone + (D,)), "seq")

    normed_ff, pull_norm_ff = jax.vjp(rms_scale, residual, gain_ff)
    h_ff = gather_rows(normed_ff.astype(bf16), "seq").reshape(-1, D)
    d_own = shuffled(grad_out)
    d_out = gather_rows(d_own, "seq").reshape(-1, D)
    gate_up = mm(h_ff, gu_w)
    hidden_full, pull_glu = jax.vjp(glu_hidden, gate_up[:, :ff], gate_up[:, ff:])
    hidden = hidden_full.astype(bf16)
    block_out = residual + scatter_rows(mm(hidden, down_w).astype(bf16).reshape(everyone + (D,)), "seq")
    down_grad = contract_rows(d_out, hidden).astype(bf16)
    down_own = summed(down_grad)
    d_hidden = contract_cols(after(d_out, down_grad), down_w)
    d_gate_up = jnp.concatenate(pull_glu(d_hidden), axis=1).astype(bf16)
    d_h_ff = scatter_rows(contract_cols(d_gate_up, gu_w).astype(bf16).reshape(everyone + (D,)), "seq")
    gu_grad = contract_rows(h_ff, d_gate_up).astype(bf16)
    gu_own = summed(gu_grad)
    d_resid_norm, g_norm_ff = pull_norm_ff(d_h_ff)
    d_residual = d_own.astype(f32) + d_resid_norm

    d_branch = gather_rows(after(d_residual.astype(bf16), gu_grad, down_own), "seq").reshape(-1, D)
    d_heads = contract_cols(d_branch, out_w)
    d_mixed, d_gate, g_norm_head = pull_head(d_heads)
    d_gate = d_gate.astype(bf16)
    out_grad = jnp.concatenate(
        [contract_rows(h_in, d_gate).astype(bf16), contract_rows(d_branch, z_rows).astype(bf16)], axis=1
    )
    d_mixed = after(d_mixed, out_grad)
    d_proj, g_conv_l, g_decay = mixer_backward(
        proj, d_mixed.reshape(everyone + (val_w,)), slots, resets, conv_l, aux, states, invs, deltas
    )
    d_proj, gu_own = lax.optimization_barrier((d_proj.reshape(-1, conv_cols + LANES), gu_own))
    out_own = summed(out_grad)
    mix_grad = contract_rows(h_in, d_proj).astype(bf16)
    mix_own = summed(after(mix_grad, out_own))
    d_proj = after(d_proj, mix_grad)
    down_grads = exchanged(down_own)
    gu_grads = exchanged(gu_own)
    out_grads = exchanged(out_own)
    mix_grads = exchanged(mix_own)
    d_h_in = scatter_rows(
        (contract_cols(d_proj, mix_w) + contract_cols(d_gate, gate_w)).astype(bf16).reshape(everyone + (D,)), "seq"
    )
    d_flat, g_norm_in = pull_norm_in(d_h_in)
    d_tokens = restored((d_residual + d_flat).astype(bf16))

    local = jnp.concatenate([g_conv_l[:TAPS].reshape(-1), g_decay[:2, heads : 2 * heads].reshape(-1)])
    shared = gather_rows(sum_all(local, ("batch",))[None], "seq")[0][slots]
    g_conv_all = shared[:, : TAPS * conv_cols].reshape(size, TAPS, conv_cols).transpose(1, 0, 2)
    g_conv = jnp.concatenate(
        [
            g_conv_all[:, :, :key_w].reshape(TAPS, KW),
            g_conv_all[:, :, key_w : 2 * key_w].reshape(TAPS, KW),
            g_conv_all[:, :, 2 * key_w :].reshape(TAPS, VW),
        ],
        axis=1,
    )
    g_alog = shared[:, TAPS * conv_cols : TAPS * conv_cols + heads].reshape(H)
    g_dt = shared[:, TAPS * conv_cols + heads :].reshape(H)
    gains = sum_all(jnp.concatenate([g_norm_in, g_norm_ff, g_norm_head]), ("seq", "batch"))

    def columns_of(grads, first, width):
        return grads[:, :, first : first + width].astype(f32).transpose(1, 0, 2).reshape(own_rows, size * width)

    g_proj = jnp.concatenate(
        [
            columns_of(mix_grads, 0, key_w),
            columns_of(mix_grads, key_w, key_w),
            columns_of(mix_grads, 2 * key_w, val_w),
            columns_of(out_grads, 0, val_w),
        ],
        axis=1,
    )
    g_small = jnp.concatenate(
        [columns_of(mix_grads, conv_cols, heads), columns_of(mix_grads, conv_cols + heads, heads)], axis=1
    )
    g_out = out_grads[:, :, val_w:].astype(f32).transpose(0, 2, 1).reshape(VW, own_rows)
    g_gu = gu_grads.astype(f32).reshape(size, own_rows, 2, ff).transpose(1, 2, 0, 3)
    g_down = down_grads.astype(f32).transpose(0, 2, 1).reshape(FF, own_rows)
    return (
        restored(block_out.astype(bf16)),
        d_tokens,
        g_proj,
        g_small,
        g_out,
        g_gu.reshape(own_rows, 2 * FF),
        g_down,
        restored(gains[:D]),
        restored(gains[D : 2 * D]),
        gains[2 * D :],
        g_conv,
        g_alog,
        g_dt,
    )


def solution(mesh):
    rows = P(("seq", "batch"), None)
    cols = P(None, ("seq", "batch"))
    act = P("batch", "seq", None)
    in_specs = (act, act, P("batch"), rows, rows, rows, rows, rows) + (P(),) * 6
    out_specs = (act, act, rows, rows, cols, rows, cols) + (P(),) * 6
    return jax.shard_map(shards, mesh=mesh, in_specs=in_specs, out_specs=out_specs, check_vma=False)
```

```python
from functools import partial

import jax
import jax.numpy as jnp
from jax import lax
from jax.experimental import pallas as pl
from jax.experimental.pallas import tpu as pltpu
from jax.sharding import PartitionSpec as P

D = 2048
H = 16
DK = 128
DV = 256
FF = 5632
CH = 64
KW = 2048
VW = 4096
CW = 8192
TAPS = 4
LANES = 128

EPS_NORM = 1e-06
EPS_HEAD = 1e-05
EPS_UNIT = 1e-06
f32 = jnp.float32
bf16 = jnp.bfloat16
VMEM_BYTES = 56 * 1024 * 1024
KERNEL_COST = pl.CostEstimate(flops=60_000_000_000, bytes_accessed=40_000_000, transcendentals=0)


def dot_in(left, right, contract, precision):
    return lax.dot_general(
        left,
        right,
        (((contract[0],), (contract[1],)), ((), ())),
        precision=precision,
        preferred_element_type=f32,
    )


def fine(left, right, contract=(1, 0)):
    return dot_in(left, right, contract, lax.Precision.HIGHEST)


def coarse(left, right, contract=(1, 0)):
    return dot_in(left, right, contract, lax.Precision.HIGHEST)


def position_masks(reset, chunk):
    rows = lax.broadcasted_iota(jnp.int32, (CH, CH), 0)
    cols = lax.broadcasted_iota(jnp.int32, (CH, CH), 1)
    time = lax.broadcasted_iota(jnp.int32, (CH, 1), 0)
    offset = reset - chunk * CH
    cut = jnp.where(offset < 0, CH, offset)
    apart = (rows >= cut) & (cols < cut)
    causal = jnp.where((rows >= cols) & ~apart, 1.0, 0.0)
    strict = jnp.where((rows > cols) & ~apart, 1.0, 0.0)
    in_first = jnp.where(time < cut, 1.0, 0.0)
    last_first = jnp.where(CH - 1 < cut, 1.0, 0.0)
    in_last = jnp.where((time >= cut) | (cut > CH - 1), 1.0, 0.0)
    begin = jnp.where(time >= offset, offset, -chunk * CH)
    taps = [jnp.where(time - (TAPS - 1) + j >= begin, 1.0, 0.0) for j in range(TAPS)]
    return causal, strict, in_first, last_first, in_last, taps


def gates(small, aux):
    beta = jax.nn.sigmoid(small)
    shifted = small + aux[1:2]
    soft = jnp.maximum(shifted, 0.0) + jnp.log1p(jnp.exp(-jnp.abs(shifted)))
    return beta, -aux[0:1] * soft, shifted


def running(values, reverse=False):
    rows = lax.broadcasted_iota(jnp.int32, (CH, CH), 0)
    cols = lax.broadcasted_iota(jnp.int32, (CH, CH), 1)
    keep = (cols >= rows) if reverse else (cols <= rows)
    return fine(jnp.where(keep, 1.0, 0.0), values)


def as_rows(total):
    pick_row = lax.broadcasted_iota(jnp.int32, (LANES, LANES), 0)
    pick_col = lax.broadcasted_iota(jnp.int32, (LANES, LANES), 1)
    return fine(jnp.where(pick_row == pick_col, 1.0, 0.0), total, (1, 1))


def inverse_unit_lower(strict_part):
    rows = lax.broadcasted_iota(jnp.int32, (CH, CH), 0)
    cols = lax.broadcasted_iota(jnp.int32, (CH, CH), 1)
    eye = jnp.where(rows == cols, 1.0, 0.0)
    diag = jnp.where(rows // 16 == cols // 16, strict_part, 0.0)
    inv = eye - diag
    power = diag
    for _ in range(3):
        power = fine(power, power)
        inv = inv + fine(inv, power)
    for size in (16, 32):
        off = jnp.where((rows // size != cols // size) & (rows // (2 * size) == cols // (2 * size)), strict_part, 0.0)
        inv = inv - fine(fine(inv, off), inv)
    return inv


def conv_taps(ext_ref, row, conv_w, taps):
    out = None
    for j in range(TAPS):
        part = conv_w[j : j + 1] * (ext_ref[row, 8 - (TAPS - 1) + j : 8 - (TAPS - 1) + j + CH, :] * taps[j])
        out = part if out is None else out + part
    return out


def unit(values):
    return lax.rsqrt(jnp.sum(values * values, axis=-1, keepdims=True) + EPS_UNIT)


def head_parts(active, head, heads):
    q = active[:, head * DK : (head + 1) * DK]
    k = active[:, heads * DK + head * DK : heads * DK + (head + 1) * DK]
    v = active[:, 2 * heads * DK + head * DV : 2 * heads * DK + (head + 1) * DV]
    return q, k, v


def decay_terms(total, total_rows, head, heads, masks):
    causal, strict, in_first, last_first, in_last, _ = masks
    lane = heads + head
    col = total[:, lane : lane + 1]
    row = total_rows[lane : lane + 1, :]
    ratios = jnp.exp(jnp.where(causal > 0, col - row, 0.0)) * causal
    last = col[CH - 1 : CH, :]
    start_fade = jnp.exp(col) * in_first
    start_last = jnp.exp(last) * last_first
    end_fade = jnp.exp(jnp.where(in_last > 0, last - col, 0.0)) * in_last
    return ratios, start_fade, start_last, end_fade


def forward_kernel(
    heads, pos_ref, reset_ref, proj, small_ref, conv_w_ref, aux_ref, outs, state_out, inv_out, delta_out, ext, state
):
    chunk = pl.program_id(0)
    width = heads * (2 * DK + DV)

    @pl.when(chunk == 0)
    def _():
        ext[...] = jnp.zeros_like(ext)
        state[...] = jnp.zeros_like(state)

    state_out[0] = state[...]
    conv_w = conv_w_ref[...]
    aux = aux_ref[...]
    for row in range(proj.shape[1]):
        masks = position_masks(reset_ref[row], chunk)
        ext[row, 0:8, :] = ext[row, CH : CH + 8, :]
        ext[row, 8:, :] = proj[0, row, 0].astype(bf16).astype(f32)
        conv = conv_taps(ext, row, conv_w, masks[5])
        active = conv * jax.nn.sigmoid(conv)
        beta_all, decay, _ = gates(small_ref[0, row, 0], aux)
        total = running(decay)
        total_rows = as_rows(total)
        for head in range(heads):
            at = row * heads + head
            q, k, v = head_parts(active, head, heads)
            q = q * (unit(q) * DK**-0.5)
            k = k * unit(k)
            beta = beta_all[:, head : head + 1]
            ratios, start_fade, start_last, end_fade = decay_terms(total, total_rows, head, heads, masks)
            both = jnp.concatenate([q, k], axis=0)
            pair = fine(both, k, (1, 1))
            inv = inverse_unit_lower(beta * (ratios * masks[1] * pair[CH:]))
            old = state[at]
            read = coarse(both, old)
            delta = coarse(inv, beta * (v - start_fade * read[CH:]))
            out = start_fade * read[:CH] + coarse(ratios * pair[:CH], delta)
            state[at] = start_last * old + coarse(end_fade * k, delta, (0, 0))
            outs[0, row, 0, :, head * DV : (head + 1) * DV] = out
            inv_out[0, at] = inv
            delta_out[0, at] = delta


def backward_kernel(
    heads,
    chunks,
    pos_ref,
    reset_ref,
    proj,
    small_ref,
    tail,
    d_out,
    conv_w_ref,
    aux_ref,
    state_ref,
    inv_ref,
    delta_ref,
    d_proj,
    d_small_ref,
    g_conv,
    g_decay,
    ext,
    dext,
    d_state,
):
    step = pl.program_id(0)
    chunk = chunks - 1 - step
    width = heads * (2 * DK + DV)

    @pl.when(step == 0)
    def _():
        dext[...] = jnp.zeros_like(dext)
        d_state[...] = jnp.zeros_like(d_state)
        g_conv[...] = jnp.zeros_like(g_conv)
        g_decay[...] = jnp.zeros_like(g_decay)

    conv_w = conv_w_ref[...]
    aux = aux_ref[...]
    lane_ids = lax.broadcasted_iota(jnp.int32, (CH, LANES), 1)
    ones = jnp.ones((CH, LANES), f32)
    for row in range(proj.shape[1]):
        masks = position_masks(reset_ref[row], chunk)
        taps = masks[5]
        ext[row, 0:8, :] = tail[0, row, 0].astype(bf16).astype(f32)
        ext[row, 8:, :] = proj[0, row, 0].astype(bf16).astype(f32)
        conv = conv_taps(ext, row, conv_w, taps)
        sig = jax.nn.sigmoid(conv)
        active = conv * sig
        small = small_ref[0, row, 0]
        beta_all, decay, shifted = gates(small, aux)
        total = running(decay)
        total_rows = as_rows(total)
        d_beta_all = jnp.zeros((CH, LANES), f32)
        d_total = jnp.zeros((CH, LANES), f32)
        d_active = []
        for head in range(heads):
            at = row * heads + head
            a_q, a_k, v = head_parts(active, head, heads)
            q_scale = unit(a_q)
            k_scale = unit(a_k)
            q = a_q * (q_scale * DK**-0.5)
            k = a_k * k_scale
            beta = beta_all[:, head : head + 1]
            ratios, start_fade, start_last, end_fade = decay_terms(total, total_rows, head, heads, masks)
            both = jnp.concatenate([q, k], axis=0)
            pair = fine(both, k, (1, 1))
            key_key, query_key = pair[CH:], pair[:CH]
            old = state_ref[0, at]
            inv = inv_ref[0, at]
            delta = delta_ref[0, at]
            do = d_out[0, row, 0, :, head * DV : (head + 1) * DV]
            ds = d_state[at]
            read = coarse(both, old)
            readings = ratios * query_key
            faded = end_fade * k
            d_delta = coarse(readings, do, (0, 0)) + coarse(faded, ds)
            d_right = coarse(inv, d_delta, (0, 0))
            d_pair = coarse(jnp.concatenate([do, d_right], axis=0), delta, (1, 1))
            d_faded = coarse(delta, ds, (1, 1))
            d_read = jnp.concatenate([start_fade * do, -(beta * start_fade) * d_right], axis=0)
            d_both = coarse(d_read, old, (1, 1))
            d_state[at] = start_last * ds + coarse(both, d_read, (0, 0))
            d_v = beta * d_right
            d_read_pair = d_pair[:CH] * ratios
            d_sys = -d_pair[CH:] * (ratios * masks[1])
            d_key_key = beta * d_sys
            moved = d_key_key * key_key + d_read_pair * query_key
            recall = read[CH:]
            d_beta = jnp.sum(d_right * (v - start_fade * recall), axis=-1, keepdims=True) + jnp.sum(
                d_sys * key_key, axis=-1, keepdims=True
            )
            d_start = jnp.sum(do * read[:CH], axis=-1, keepdims=True) - beta * jnp.sum(
                d_right * recall, axis=-1, keepdims=True
            )
            d_end = jnp.sum(d_faded * k, axis=-1, keepdims=True) * end_fade
            d_last = jnp.sum(d_end, axis=0, keepdims=True) + start_last * jnp.sum(
                jnp.sum(ds * old, axis=-1, keepdims=True), axis=0, keepdims=True
            )
            last_row = lax.broadcasted_iota(jnp.int32, (CH, 1), 0) == CH - 1
            d_col = (
                jnp.sum(moved, axis=-1, keepdims=True)
                - fine(moved, ones, (0, 0))[:, 0:1]
                + d_start * start_fade
                - d_end
                + jnp.where(last_row, d_last, 0.0)
            )
            d_q = d_both[:CH] + coarse(d_read_pair, k)
            d_k = (
                d_both[CH:]
                + coarse(d_read_pair, q, (0, 0))
                + coarse(d_key_key, k)
                + coarse(d_key_key, k, (0, 0))
                + end_fade * d_faded
            )
            d_aq = (q_scale * DK**-0.5) * (d_q - a_q * (q_scale * q_scale * jnp.sum(a_q * d_q, axis=-1, keepdims=True)))
            d_ak = k_scale * (d_k - a_k * (k_scale * k_scale * jnp.sum(a_k * d_k, axis=-1, keepdims=True)))
            d_active.append((d_aq, d_ak, d_v))
            d_beta_all = jnp.where(lane_ids == head, d_beta, d_beta_all)
            d_total = jnp.where(lane_ids == heads + head, d_col, d_total)
        d_decay = running(d_total, reverse=True)
        d_shift = d_decay * (-aux[0:1]) * jax.nn.sigmoid(shifted)
        d_small = d_beta_all * beta_all * (1.0 - beta_all) + d_shift
        g_decay[0:1, :] += jnp.sum(d_decay * decay, axis=0, keepdims=True)
        g_decay[1:2, :] += jnp.sum(d_shift, axis=0, keepdims=True)
        d_act = jnp.concatenate([d_active[h][i] for i in range(3) for h in range(heads)], axis=1)
        d_conv = d_act * (sig * (1.0 + conv * (1.0 - sig)))
        d_in = None
        for j in range(TAPS):
            masked = d_conv * taps[j]
            g_conv[j : j + 1, :] += jnp.sum(
                masked * ext[row, 8 - (TAPS - 1) + j : 8 - (TAPS - 1) + j + CH, :], axis=0, keepdims=True
            )
            dext[row, j, 0:CH, :] = masked
            shift = TAPS - 1 - j
            part = conv_w[j : j + 1] * dext[row, j, shift : shift + CH, :]
            d_in = part if d_in is None else d_in + part
            dext[row, j, CH : CH + 8, :] = masked[0:8]
        d_proj[0, row, 0] = d_in.astype(bf16)
        d_small_ref[0, row, 0] = d_small.astype(bf16)


def params():
    return pltpu.CompilerParams(dimension_semantics=("arbitrary",), vmem_limit_bytes=VMEM_BYTES)


def whole(array):
    return pl.BlockSpec(array.shape, lambda c, pos, rst: (0,) * array.ndim)


def slot_spec(rows_n, width, chunk_of):
    return pl.BlockSpec(
        (1, rows_n, 1, CH, width), lambda c, pos, rst: (pos[chunk_of(c)] & 1, 0, pos[chunk_of(c)] >> 1, 0, 0)
    )


def mixer_forward(proj, small, pos, resets, conv_w, aux):
    _, rows_n, half, _, width = proj.shape
    chunks = 2 * half
    heads = width // (2 * DK + DV)
    units = rows_n * heads
    spec = lambda w: slot_spec(rows_n, w, lambda c: c)
    kept = lambda *s: pl.BlockSpec((1, units) + s, lambda c, pos, rst: (c, 0, 0, 0))
    return pl.pallas_call(
        partial(forward_kernel, heads),
        grid_spec=pltpu.PrefetchScalarGridSpec(
            num_scalar_prefetch=2,
            grid=(chunks,),
            in_specs=[spec(width), spec(LANES), whole(conv_w), whole(aux)],
            out_specs=[spec(heads * DV), kept(DK, DV), kept(CH, CH), kept(CH, DV)],
            scratch_shapes=[pltpu.VMEM((rows_n, CH + 8, width), f32), pltpu.VMEM((units, DK, DV), f32)],
        ),
        out_shape=[
            jax.ShapeDtypeStruct((2, rows_n, half, CH, heads * DV), f32),
            jax.ShapeDtypeStruct((chunks, units, DK, DV), f32),
            jax.ShapeDtypeStruct((chunks, units, CH, CH), f32),
            jax.ShapeDtypeStruct((chunks, units, CH, DV), f32),
        ],
        cost_estimate=KERNEL_COST,
        compiler_params=params(),
        name="delta_forward",
    )(pos, resets, proj, small, conv_w, aux)


def mixer_backward(proj, small, d_out, pos, resets, conv_w, aux, states, invs, deltas):
    _, rows_n, half, _, width = proj.shape
    chunks = 2 * half
    heads = width // (2 * DK + DV)
    units = rows_n * heads
    back = lambda c: chunks - 1 - c
    before = lambda c: jnp.maximum(back(c) - 1, 0)
    spec = lambda w: slot_spec(rows_n, w, back)
    tail = pl.BlockSpec(
        (1, rows_n, 1, 8, width),
        lambda c, pos, rst: (pos[before(c)] & 1, 0, pos[before(c)] >> 1, CH // 8 - 1, 0),
    )
    kept = lambda *s: pl.BlockSpec((1, units) + s, lambda c, pos, rst: (back(c), 0, 0, 0))
    return pl.pallas_call(
        partial(backward_kernel, heads, chunks),
        grid_spec=pltpu.PrefetchScalarGridSpec(
            num_scalar_prefetch=2,
            grid=(chunks,),
            in_specs=[spec(width), spec(LANES), tail, spec(heads * DV), whole(conv_w), whole(aux)]
            + [kept(DK, DV), kept(CH, CH), kept(CH, DV)],
            out_specs=[
                spec(width),
                spec(LANES),
                pl.BlockSpec((8, width), lambda c, pos, rst: (0, 0)),
                pl.BlockSpec((8, LANES), lambda c, pos, rst: (0, 0)),
            ],
            scratch_shapes=[
                pltpu.VMEM((rows_n, CH + 8, width), f32),
                pltpu.VMEM((rows_n, TAPS, CH + 8, width), f32),
                pltpu.VMEM((units, DK, DV), f32),
            ],
        ),
        out_shape=[
            jax.ShapeDtypeStruct((2, rows_n, half, CH, width), bf16),
            jax.ShapeDtypeStruct((2, rows_n, half, CH, LANES), bf16),
            jax.ShapeDtypeStruct((8, width), f32),
            jax.ShapeDtypeStruct((8, LANES), f32),
        ],
        cost_estimate=KERNEL_COST,
        compiler_params=params(),
        name="delta_backward",
    )(pos, resets, proj, small, proj, d_out, conv_w, aux, states, invs, deltas)


def local_call(body, name, inputs, specs, outs, bytes_accessed):
    return pl.pallas_call(
        body,
        grid=(1,),
        in_specs=specs,
        out_specs=whole_specs(outs),
        out_shape=outs,
        cost_estimate=pl.CostEstimate(flops=1_000_000, bytes_accessed=bytes_accessed, transcendentals=0),
        compiler_params=pltpu.CompilerParams(vmem_limit_bytes=VMEM_BYTES),
        name=name,
    )(*inputs)


def term_specs(terms):
    kept, got, steps = terms
    rows_n = kept.shape[0]
    first = pl.BlockSpec((rows_n, 1) + kept.shape[2:], lambda i: (0, 0, 0, 0))
    flat = [step for row in steps for step in row]
    return [kept, got] + flat, [first, first] + [pl.BlockSpec((1,) + s.shape[1:], lambda i: (0, 0, 0)) for s in flat]


def row_total(refs, row, rows_n):
    kept, got = refs[0], refs[1]
    each = (len(refs) - 2) // rows_n
    total = kept[row, 0].astype(f32) + got[row, 0].astype(f32)
    for step in refs[2 + row * each : 2 + (row + 1) * each]:
        total = total + step[0].astype(f32)
    return total


def in_order(values, groups):
    size, batches = groups
    own = values.shape[-1] // (size * batches)
    return jnp.concatenate(
        [
            values[:, (b * size + s) * own : (b * size + s + 1) * own]
            for s in range(size)
            for b in range(batches)
        ],
        axis=1,
    )


def whole_specs(arrays):
    zeros = lambda n: lambda i: (0,) * n
    return [pl.BlockSpec(a.shape, zeros(len(a.shape))) for a in arrays]


def add_and_norm(terms, base, gain):
    inputs, specs = term_specs(terms)
    rows_n, _, span, _ = terms[0].shape

    def body(*refs):
        base_ref, gain_ref, out_ref, norm_ref = refs[len(inputs) :]
        for row in range(rows_n):
            at = pl.ds(row * span, span)
            total = base_ref[at, :].astype(f32) + row_total(refs[: len(inputs)], row, rows_n)
            scale = lax.rsqrt(jnp.mean(total * total, axis=-1, keepdims=True) + EPS_NORM)
            out_ref[at, :] = total
            norm_ref[row] = (total * scale * gain_ref[...]).astype(bf16)

    extra = [base, gain.reshape(1, D)]
    return local_call(
        body,
        "add_and_norm",
        inputs + extra,
        specs + whole_specs(extra),
        [jax.ShapeDtypeStruct((rows_n * span, D), f32), jax.ShapeDtypeStruct((rows_n, span, D), bf16)],
        4_000_000,
    )


def norm_back(terms, base, through, gain, out_dtype, groups=None):
    inputs, specs = term_specs(terms)
    rows_n, _, span, _ = terms[0].shape
    with_rows = groups is None

    def body(*refs):
        base_ref, through_ref, gain_ref = refs[len(inputs) : len(inputs) + 3]
        outs = refs[len(inputs) + 3 :]
        g_gain = jnp.zeros((1, D), f32)
        for row in range(rows_n):
            at = pl.ds(row * span, span)
            d_norm = row_total(refs[: len(inputs)], row, rows_n)
            x = base_ref[at, :].astype(f32)
            scale = lax.rsqrt(jnp.mean(x * x, axis=-1, keepdims=True) + EPS_NORM)
            e = d_norm * gain_ref[...]
            lean = jnp.mean(e * x, axis=-1, keepdims=True)
            total = through_ref[at, :].astype(f32) + scale * e - x * (scale * scale * scale * lean)
            g_gain = g_gain + jnp.sum(d_norm * x * scale, axis=0, keepdims=True)
            if with_rows:
                outs[0][at, :] = total.astype(out_dtype)
                outs[1][row] = total.astype(bf16)
            else:
                outs[0][at, :] = in_order(total, groups).astype(out_dtype)
        outs[-1][...] = g_gain

    extra = [base, through, gain.reshape(1, D)]
    outs = [jax.ShapeDtypeStruct((rows_n * span, D), out_dtype)]
    if with_rows:
        outs.append(jax.ShapeDtypeStruct((rows_n, span, D), bf16))
    return local_call(
        body,
        "norm_back",
        inputs + extra,
        specs + whole_specs(extra),
        outs + [jax.ShapeDtypeStruct((1, D), f32)],
        4_000_000,
    )


def add_in_order(terms, base, groups):
    inputs, specs = term_specs(terms)
    rows_n, _, span, _ = terms[0].shape

    def body(*refs):
        base_ref, out_ref = refs[len(inputs) :]
        for row in range(rows_n):
            at = pl.ds(row * span, span)
            total = base_ref[at, :] + row_total(refs[: len(inputs)], row, rows_n)
            out_ref[at, :] = in_order(total, groups).astype(bf16)

    return local_call(
        body,
        "add_in_order",
        inputs + [base],
        specs + whole_specs([base]),
        [jax.ShapeDtypeStruct((rows_n * span, D), bf16)],
        3_000_000,
    )[0]


ROW_BLOCK = 256


def gated_norm(mixed, gate, gain):
    rows_n, width = mixed.shape

    def body(mixed_ref, gate_ref, gain_ref, out_ref):
        for at in range(0, width, DV):
            x = mixed_ref[:, at : at + DV]
            g = gate_ref[:, at : at + DV]
            scale = lax.rsqrt(jnp.mean(x * x, axis=-1, keepdims=True) + EPS_HEAD)
            out_ref[:, at : at + DV] = (x * scale * gain_ref[...] * (g * jax.nn.sigmoid(g))).astype(bf16)

    block = pl.BlockSpec((ROW_BLOCK, width), lambda i: (i, 0))
    return pl.pallas_call(
        body,
        grid=(rows_n // ROW_BLOCK,),
        in_specs=[block, block, pl.BlockSpec((1, DV), lambda i: (0, 0))],
        out_specs=block,
        out_shape=jax.ShapeDtypeStruct((rows_n, width), bf16),
        cost_estimate=pl.CostEstimate(flops=1_000_000, bytes_accessed=5_000_000, transcendentals=0),
        compiler_params=params(),
        name="gated_norm",
    )(mixed, gate, gain.reshape(1, DV))


def gated_norm_back(mixed, gate, gain, d_out):
    rows_n, width = mixed.shape

    def body(mixed_ref, gate_ref, gain_ref, d_ref, d_mixed_ref, d_gate_ref, g_gain_ref):
        @pl.when(pl.program_id(0) == 0)
        def _():
            g_gain_ref[...] = jnp.zeros_like(g_gain_ref)

        g_gain = jnp.zeros((1, DV), f32)
        for at in range(0, width, DV):
            x = mixed_ref[:, at : at + DV]
            g = gate_ref[:, at : at + DV]
            d = d_ref[:, at : at + DV]
            scale = lax.rsqrt(jnp.mean(x * x, axis=-1, keepdims=True) + EPS_HEAD)
            sig = jax.nn.sigmoid(g)
            through = d * (g * sig)
            unit_x = x * scale
            e = through * gain_ref[...]
            lean = jnp.mean(e * unit_x, axis=-1, keepdims=True)
            d_mixed_ref[:, at : at + DV] = scale * (e - unit_x * lean)
            d_gate_ref[:, at : at + DV] = (
                d * (unit_x * gain_ref[...]) * (sig * (1.0 + g * (1.0 - sig)))
            ).astype(bf16)
            g_gain = g_gain + jnp.sum(through * unit_x, axis=0, keepdims=True)
        g_gain_ref[0:1, :] += g_gain

    block = pl.BlockSpec((ROW_BLOCK, width), lambda i: (i, 0))
    return pl.pallas_call(
        body,
        grid=(rows_n // ROW_BLOCK,),
        in_specs=[block, block, pl.BlockSpec((1, DV), lambda i: (0, 0)), block],
        out_specs=[block, block, pl.BlockSpec((8, DV), lambda i: (0, 0))],
        out_shape=[
            jax.ShapeDtypeStruct((rows_n, width), f32),
            jax.ShapeDtypeStruct((rows_n, width), bf16),
            jax.ShapeDtypeStruct((8, DV), f32),
        ],
        cost_estimate=pl.CostEstimate(flops=1_000_000, bytes_accessed=9_000_000, transcendentals=0),
        compiler_params=params(),
        name="gated_norm_back",
    )(mixed, gate, gain.reshape(1, DV), d_out)


def laid_out(blocks, pieces, total):
    size, rows_n, _ = blocks[0].shape

    def body(*refs):
        out_ref = refs[-1]
        for which, first, width, start in pieces:
            for s in range(size):
                out_ref[:, start + s * width : start + (s + 1) * width] = refs[which][
                    s, :, first : first + width
                ].astype(f32)

    return local_call(
        body, "laid_out", blocks, whole_specs(blocks), [jax.ShapeDtypeStruct((rows_n, total), f32)], 5_000_000
    )[0]


def swap(value, axis, bit):
    return lax.ppermute(value, axis, [(i, i ^ bit) for i in range(lax.axis_size(axis))])


def routes(axis):
    bits = [1 << i for i in range(lax.axis_size(axis).bit_length() - 1)]
    return [bits[1:] + bits[:1], bits[:0:-1] + bits[:1]]


def gather_rows(rows, axis, ordered=True):
    laid = []
    for row, order in zip(rows, routes(axis) * rows.shape[0]):
        held = row[None]
        names = [0]
        parts = []
        for i, bit in enumerate(order[:-1]):
            got = swap(held, axis, bit)
            names = names + [n ^ (bit >> 1) for n in names]
            if i < len(order) - 2:
                held = jnp.concatenate([held, got], axis=0)
            else:
                parts = [held, got]
        if ordered and names != sorted(names):
            place = {name: i for i, name in enumerate(names)}
            size = len(names) // 2
            for n in sorted(names):
                which, at = divmod(place[n], size)
                laid.append(parts[which][at : at + 1])
        else:
            laid.extend(parts)
    even = jnp.concatenate(laid, axis=0).reshape((rows.shape[0], -1) + rows.shape[1:])
    return even, swap(even, axis, 1)


def scatter_rows(keep, send, axis, ordered=True, earlier=()):
    got = after(swap(send, axis, 1), *earlier)
    rows_n, half, span, width = keep.shape
    depth = half.bit_length() - 1
    steps = []
    for row, order in zip(range(rows_n), routes(axis) * rows_n):
        bits = order[:-1]
        axes = sorted(bits, reverse=True) if ordered else bits[::-1]
        shape = (2,) * depth + (span, width)
        terms = [keep[row].reshape(shape), got[row].reshape(shape)]
        mine = []
        for bit in bits[::-1]:
            at = axes.index(bit)
            sent = sum(lax.index_in_dim(t, 1, at, keepdims=False).astype(f32) for t in terms).astype(bf16)
            back = swap(sent, axis, bit)
            terms = [lax.index_in_dim(t, 0, at, keepdims=False) for t in terms] + [back]
            axes = [b for b in axes if b != bit]
            mine.append(back.reshape((-1, span, width)))
        steps.append(mine)
    return keep, got, steps


def joined(halves):
    return jnp.concatenate([h.reshape(-1, h.shape[-1]) for h in halves], axis=0)


def after(value, *earlier):
    return lax.optimization_barrier((value,) + earlier)[0]


def sum_all(value, axes):
    for axis in axes:
        for i in range(lax.axis_size(axis).bit_length() - 1):
            value = value + swap(value, axis, 1 << i)
    return value


def gather_small(value, axis):
    held = value[None]
    size = lax.axis_size(axis)
    for i in range(size.bit_length() - 1):
        held = jnp.concatenate([held, swap(held, axis, 1 << i)], axis=0)
    return held[jnp.arange(size, dtype=jnp.int32) ^ lax.axis_index(axis).astype(jnp.int32)]


def mm(left, right):
    return jnp.dot(left, right, preferred_element_type=f32)


def contract_rows(left, right):
    return lax.dot_general(left, right, (((0,), (0,)), ((), ())), preferred_element_type=f32)


def contract_cols(left, right):
    return lax.dot_general(left, right, (((1,), (1,)), ((), ())), preferred_element_type=f32)


def rms_scale(values, scale_gain):
    return values * lax.rsqrt(jnp.mean(values * values, axis=-1, keepdims=True) + EPS_NORM) * scale_gain


def glu_hidden(gate_half, up_half):
    return jax.nn.silu(gate_half) * up_half


def exchanged(packed):
    return lax.all_to_all(packed, "seq", split_axis=0, concat_axis=0, tiled=True)


def stacked(blocks):
    full = lax.all_gather(blocks, "batch", axis=0, tiled=False)
    return full.reshape(-1, blocks.shape[-1])


def summed(partial_grad):
    own = lax.psum_scatter(partial_grad, "batch", scatter_dimension=0, tiled=True)
    return own.reshape(lax.axis_size("seq"), -1, own.shape[-1])


def shards(
    tokens,
    grad_out,
    resets,
    w_proj,
    w_small,
    w_out,
    w_gu,
    w_down,
    norm_in,
    norm_ff,
    norm_head,
    conv_w,
    a_log,
    dt_bias,
):
    size = lax.axis_size("seq")
    groups = lax.axis_size("batch")
    me = lax.axis_index("seq")
    batch_rows, span_len, _ = tokens.shape
    own_rows = w_proj.shape[0]
    heads = H // size
    ff = FF // size
    key_w, val_w = heads * DK, heads * DV
    conv_cols = 2 * key_w + val_w
    half = batch_rows * size // 2 * span_len
    cut = 16 * ff // 11 // LANES * LANES
    halves = (batch_rows, size // 2, span_len)
    blocks = (2,) + halves

    def shuffled(array):
        lead = array.shape[:-1]
        return array.reshape(lead + (size, groups, own_rows)).swapaxes(-3, -2).reshape(lead + (D,))

    def restored(array):
        lead = array.shape[:-1]
        return array.reshape(lead + (groups, size, own_rows)).swapaxes(-3, -2).reshape(lead + (D,))

    out_w = lax.all_gather(w_out, "batch", axis=0, tiled=True)
    packed_mix = jnp.concatenate(
        [
            w_proj[:, :KW].reshape(own_rows, size, key_w),
            w_proj[:, KW : 2 * KW].reshape(own_rows, size, key_w),
            w_proj[:, 2 * KW : CW].reshape(own_rows, size, val_w),
        ],
        axis=-1,
    ).transpose(1, 0, 2)
    moved_mix = exchanged(packed_mix)
    own_in = shuffled(tokens).reshape(-1, D)
    gain_in, gain_ff = shuffled(norm_in), shuffled(norm_ff)
    h_in = joined(gather_rows(rms_scale(own_in.astype(f32), gain_in).astype(bf16).reshape(tokens.shape), "seq"))
    mix_w = stacked(after(moved_mix, out_w, h_in))
    packed_gate, packed_gu, w_small, d_own, own_down = after(
        (
            w_proj[:, CW:].reshape(own_rows, size, val_w).transpose(1, 0, 2),
            w_gu.reshape(own_rows, 2, size, ff).transpose(2, 0, 1, 3).reshape(size, own_rows, 2 * ff),
            w_small,
            shuffled(grad_out),
            shuffled(w_down),
        ),
        moved_mix,
    )
    d_out = joined(gather_rows(d_own, "seq", False))
    small_all = gather_small(gather_small(w_small, "seq"), "batch").reshape(D, 2 * H)
    small_w = jnp.pad(
        jnp.concatenate(
            [
                lax.dynamic_slice_in_dim(small_all, me * heads, heads, 1),
                lax.dynamic_slice_in_dim(small_all, H + me * heads, heads, 1),
            ],
            axis=1,
        ),
        ((0, 0), (0, LANES - 2 * heads)),
    )
    out_w = shuffled(out_w)
    moved_gate, moved_gu = exchanged(packed_gate), exchanged(packed_gu)
    moved_gate, moved_gu, small_w, mix_w = lax.optimization_barrier((moved_gate, moved_gu, small_w, mix_w))
    gate_w = stacked(moved_gate)
    moved_first, moved_rest = moved_gu[:, :, :cut], moved_gu[:, :, cut:]
    gu_first = stacked(moved_first)

    slots = jnp.arange(size, dtype=jnp.int32) ^ me.astype(jnp.int32)
    conv_l = jnp.concatenate(
        [
            lax.dynamic_slice_in_dim(conv_w, me * key_w, key_w, 1),
            lax.dynamic_slice_in_dim(conv_w, KW + me * key_w, key_w, 1),
            lax.dynamic_slice_in_dim(conv_w, 2 * KW + me * val_w, val_w, 1),
        ],
        axis=1,
    )
    at_heads = (heads, LANES - 2 * heads)
    aux = jnp.pad(
        jnp.stack(
            [
                lax.dynamic_slice_in_dim(jnp.exp(a_log), me * heads, heads),
                lax.dynamic_slice_in_dim(dt_bias, me * heads, heads),
            ]
        ),
        ((0, 6), at_heads),
    )

    proj = mm(h_in, mix_w).reshape(blocks + (conv_cols,))
    small = mm(h_in, small_w).reshape(blocks + (LANES,))
    proj, out_w, moved_rest, own_down = lax.optimization_barrier((proj, out_w, moved_rest, own_down))
    gu_rest = stacked(moved_rest)
    down_w = lax.all_gather(own_down, "batch", axis=0, tiled=True)
    mixed, states, invs, deltas = mixer_forward(proj, small, slots, resets, conv_l, aux)
    mixed = mixed.reshape(-1, val_w)
    gate = mm(h_in, gate_w)
    z_rows = gated_norm(mixed, gate, norm_head)

    def parts(product, left):
        send = product(left[half:]).astype(bf16).reshape(halves + (D,))
        return product(left[:half]).astype(bf16).reshape(halves + (D,)), send

    keep, send = parts(lambda rows: mm(rows, out_w), z_rows)
    keep, send, d_out = after((keep, send, d_out), gu_first)
    residual, normed_ff = add_and_norm(
        scatter_rows(keep, send, "seq"), after(own_in, gu_rest), gain_ff
    )

    h_halves = gather_rows(normed_ff, "seq", False)
    gu_w = jnp.concatenate([gu_first, gu_rest], axis=1)
    h_ff = joined(h_halves)
    gate_up = mm(h_ff, gu_w)
    hidden_full, pull_glu = jax.vjp(glu_hidden, gate_up[:, :ff], gate_up[:, ff:])
    hidden = after(hidden_full.astype(bf16), down_w)
    down_grad = contract_rows(d_out, hidden).astype(bf16)
    down_own = summed(down_grad)
    d_hidden = contract_cols(after(d_out, down_grad), down_w)
    d_gate_up = jnp.concatenate(pull_glu(d_hidden), axis=1).astype(bf16)
    keep, send = parts(lambda rows: contract_cols(rows, gu_w), d_gate_up)
    terms = scatter_rows(keep, send, "seq", False)
    gu_grad = contract_rows(after(h_ff, keep, send), d_gate_up).astype(bf16)
    gu_own = summed(gu_grad)
    out_parts = parts(lambda rows: mm(rows, down_w), after(hidden, keep, send))
    d_residual, d_branch, g_norm_ff = norm_back(terms, residual, d_own.reshape(-1, D), gain_ff, f32)

    d_branch = joined(gather_rows(after(d_branch, gu_grad, down_own, out_parts), "seq"))
    d_heads = contract_cols(d_branch, out_w)
    d_mixed, d_gate, g_norm_head = gated_norm_back(mixed, gate, norm_head, d_heads)
    out_grad = jnp.concatenate(
        [contract_rows(h_in, d_gate).astype(bf16), contract_rows(d_branch, z_rows).astype(bf16)], axis=1
    )
    d_mixed = after(d_mixed, out_grad)
    d_proj, d_small, g_conv_l, g_decay = mixer_backward(
        proj, small, d_mixed.reshape(blocks + (val_w,)), slots, resets, conv_l, aux, states, invs, deltas
    )
    d_proj, gu_own = lax.optimization_barrier((d_proj.reshape(-1, conv_cols), gu_own))
    d_small = d_small.reshape(-1, LANES)
    out_own = summed(out_grad)
    mix_grad = contract_rows(h_in, d_proj).astype(bf16)
    mix_own = summed(mix_grad)
    d_proj, d_small, g_conv_l, gu_own, out_parts = after((d_proj, d_small, g_conv_l, gu_own, out_parts), mix_grad)
    ff_grads = exchanged(jnp.concatenate([gu_own, down_own], axis=-1))
    keep, send = parts(
        lambda rows: contract_cols(rows[:, :conv_cols], mix_w)
        + contract_cols(rows[:, conv_cols : conv_cols + val_w], gate_w)
        + contract_cols(rows[:, conv_cols + val_w :], small_w),
        jnp.concatenate([d_proj, d_gate, d_small], axis=1),
    )
    d_tokens, g_norm_in = norm_back(
        scatter_rows(keep, send, "seq", earlier=(ff_grads, out_own)), own_in, d_residual, gain_in, bf16, (size, groups)
    )
    block_out = add_in_order(scatter_rows(*after(out_parts, keep, send), "seq", False), residual, (size, groups))

    small_grad = contract_rows(d_small, h_in)[: 2 * heads]
    local = jnp.concatenate(
        [g_conv_l[:TAPS].reshape(-1), g_decay[:2, heads : 2 * heads].reshape(-1), small_grad.reshape(-1)]
    )
    shared = gather_small(sum_all(local, ("batch",)), "seq")
    g_conv_all = shared[:, : TAPS * conv_cols].reshape(size, TAPS, conv_cols).transpose(1, 0, 2)
    g_conv = jnp.concatenate(
        [
            g_conv_all[:, :, :key_w].reshape(TAPS, KW),
            g_conv_all[:, :, key_w : 2 * key_w].reshape(TAPS, KW),
            g_conv_all[:, :, 2 * key_w :].reshape(TAPS, VW),
        ],
        axis=1,
    )
    g_alog = shared[:, TAPS * conv_cols : TAPS * conv_cols + heads].reshape(H)
    g_dt = shared[:, TAPS * conv_cols + heads : TAPS * conv_cols + 2 * heads].reshape(H)
    g_small = lax.dynamic_slice_in_dim(
        shared[:, TAPS * conv_cols + 2 * heads :].reshape(size, 2, heads, D),
        (lax.axis_index("batch") * size + me) * own_rows,
        own_rows,
        3,
    )
    g_small = g_small.transpose(3, 1, 0, 2).reshape(own_rows, 2 * H)
    gains = sum_all(jnp.concatenate([g_norm_in[0], g_norm_ff[0], g_norm_head[0]]), ("seq", "batch"))

    out_grads = exchanged(out_own)
    mix_own, d_tokens, block_out, out_grads = lax.optimization_barrier((mix_own, d_tokens, block_out, out_grads))
    g_gu = laid_out([ff_grads], [(0, 0, ff, 0), (0, ff, ff, FF)], 2 * FF)
    g_down = ff_grads[:, :, 2 * ff :].astype(f32).transpose(0, 2, 1).reshape(FF, own_rows)
    g_out = out_grads[:, :, val_w:].astype(f32).transpose(0, 2, 1).reshape(VW, own_rows)
    mix_grads = exchanged(mix_own)
    g_proj = laid_out(
        [mix_grads, out_grads],
        [(0, 0, key_w, 0), (0, key_w, key_w, KW), (0, 2 * key_w, val_w, 2 * KW), (1, 0, val_w, CW)],
        CW + VW,
    )
    return (
        block_out.reshape(tokens.shape),
        d_tokens.reshape(tokens.shape),
        g_proj,
        g_small,
        g_out,
        g_gu,
        g_down,
        restored(gains[:D]),
        restored(gains[D : 2 * D]),
        gains[2 * D :],
        g_conv,
        g_alog,
        g_dt,
    )


def solution(mesh):
    rows = P(("seq", "batch"), None)
    cols = P(None, ("seq", "batch"))
    act = P("batch", "seq", None)
    in_specs = (act, act, P("batch"), rows, rows, rows, rows, rows) + (P(),) * 6
    out_specs = (act, act, rows, rows, cols, rows, cols) + (P(),) * 6
    return jax.shard_map(shards, mesh=mesh, in_specs=in_specs, out_specs=out_specs, check_vma=False)
```

```python
from functools import partial

import jax
import jax.numpy as jnp
from jax import lax
from jax.experimental import pallas as pl
from jax.experimental.pallas import tpu as pltpu
from jax.sharding import PartitionSpec as P

D = 2048
H = 16
DK = 128
DV = 256
FF = 5632
CH = 64
KW = 2048
VW = 4096
CW = 8192
TAPS = 4
LANES = 128

EPS_NORM = 1e-06
EPS_HEAD = 1e-05
EPS_UNIT = 1e-06
f32 = jnp.float32
bf16 = jnp.bfloat16
VMEM_BYTES = 56 * 1024 * 1024
KERNEL_COST = pl.CostEstimate(flops=30_000_000_000, bytes_accessed=40_000_000, transcendentals=0)


def dot_in(left, right, contract, precision):
    return lax.dot_general(
        left,
        right,
        (((contract[0],), (contract[1],)), ((), ())),
        precision=precision,
        preferred_element_type=f32,
    )


def fine(left, right, contract=(1, 0)):
    return dot_in(left, right, contract, lax.Precision.HIGH)


def coarse(left, right, contract=(1, 0)):
    return dot_in(left, right, contract, lax.Precision.HIGH)


def position_masks(reset, chunk):
    rows = lax.broadcasted_iota(jnp.int32, (CH, CH), 0)
    cols = lax.broadcasted_iota(jnp.int32, (CH, CH), 1)
    time = lax.broadcasted_iota(jnp.int32, (CH, 1), 0)
    offset = reset - chunk * CH
    cut = jnp.where(offset < 0, CH, offset)
    apart = (rows >= cut) & (cols < cut)
    causal = jnp.where((rows >= cols) & ~apart, 1.0, 0.0)
    strict = jnp.where((rows > cols) & ~apart, 1.0, 0.0)
    in_first = jnp.where(time < cut, 1.0, 0.0)
    last_first = jnp.where(CH - 1 < cut, 1.0, 0.0)
    in_last = jnp.where((time >= cut) | (cut > CH - 1), 1.0, 0.0)
    begin = jnp.where(time >= offset, offset, -chunk * CH)
    taps = [jnp.where(time - (TAPS - 1) + j >= begin, 1.0, 0.0) for j in range(TAPS)]
    return causal, strict, in_first, last_first, in_last, taps


def gates(small, aux):
    beta = jax.nn.sigmoid(small)
    shifted = small + aux[1:2]
    soft = jnp.maximum(shifted, 0.0) + jnp.log1p(jnp.exp(-jnp.abs(shifted)))
    return beta, -aux[0:1] * soft, shifted


def running(values, reverse=False):
    rows = lax.broadcasted_iota(jnp.int32, (CH, CH), 0)
    cols = lax.broadcasted_iota(jnp.int32, (CH, CH), 1)
    keep = (cols >= rows) if reverse else (cols <= rows)
    return fine(jnp.where(keep, 1.0, 0.0), values)


def as_rows(total):
    pick_row = lax.broadcasted_iota(jnp.int32, (LANES, LANES), 0)
    pick_col = lax.broadcasted_iota(jnp.int32, (LANES, LANES), 1)
    return fine(jnp.where(pick_row == pick_col, 1.0, 0.0), total, (1, 1))


def inverses_unit_lower(parts):
    size = parts[0].shape[0]
    rows = lax.broadcasted_iota(jnp.int32, (size, size), 0)
    cols = lax.broadcasted_iota(jnp.int32, (size, size), 1)
    eye = jnp.where(rows == cols, 1.0, 0.0)
    block = lambda n: jnp.where((rows & -n) == (cols & -n), 1.0, 0.0)
    inside = {n: block(n) for n in (16, 32, 64)}
    power = [part * inside[16] for part in parts]
    inv = [eye - diag for diag in power]
    for _ in range(3):
        power = [fine(p, p) for p in power]
        more = [fine(i, p) for i, p in zip(inv, power)]
        inv = [i + m for i, m in zip(inv, more)]
    for n in (16, 32):
        ring = inside[2 * n] - inside[n]
        left = [fine(i, part * ring) for i, part in zip(inv, parts)]
        more = [fine(l, i) for l, i in zip(left, inv)]
        inv = [i - m for i, m in zip(inv, more)]
    return inv


def conv_taps(ext_ref, row, conv_w, taps):
    out = None
    for j in range(TAPS):
        part = conv_w[j : j + 1] * (ext_ref[row, 8 - (TAPS - 1) + j : 8 - (TAPS - 1) + j + CH, :] * taps[j])
        out = part if out is None else out + part
    return out


def unit(values):
    return lax.rsqrt(jnp.sum(values * values, axis=-1, keepdims=True) + EPS_UNIT)


def head_parts(active, head, heads):
    q = active[:, head * DK : (head + 1) * DK]
    k = active[:, heads * DK + head * DK : heads * DK + (head + 1) * DK]
    v = active[:, 2 * heads * DK + head * DV : 2 * heads * DK + (head + 1) * DV]
    return q, k, v


def decay_terms(total, total_rows, head, heads, masks):
    causal, strict, in_first, last_first, in_last, _ = masks
    lane = heads + head
    col = total[:, lane : lane + 1]
    row = total_rows[lane : lane + 1, :]
    ratios = jnp.exp(jnp.where(causal > 0, col - row, 0.0)) * causal
    last = col[CH - 1 : CH, :]
    start_fade = jnp.exp(col) * in_first
    start_last = jnp.exp(last) * last_first
    end_fade = jnp.exp(jnp.where(in_last > 0, last - col, 0.0)) * in_last
    return ratios, start_fade, start_last, end_fade


def backward_kernel(
    heads,
    chunks,
    pos_ref,
    reset_ref,
    proj,
    small_ref,
    tail,
    d_out,
    conv_w_ref,
    aux_ref,
    state_ref,
    inv_ref,
    delta_ref,
    d_proj,
    d_small_ref,
    g_conv,
    g_decay,
    ext,
    dext,
    d_state,
):
    step = pl.program_id(0)
    chunk = chunks - 1 - step
    width = heads * (2 * DK + DV)

    @pl.when(step == 0)
    def _():
        dext[...] = jnp.zeros_like(dext)
        d_state[...] = jnp.zeros_like(d_state)
        g_conv[...] = jnp.zeros_like(g_conv)
        g_decay[...] = jnp.zeros_like(g_decay)

    conv_w = conv_w_ref[...]
    aux = aux_ref[...]
    lane_ids = lax.broadcasted_iota(jnp.int32, (CH, LANES), 1)
    last_row = lax.broadcasted_iota(jnp.int32, (CH, 1), 0) == CH - 1
    ones = jnp.ones((CH, LANES), f32)
    rows = range(proj.shape[1])
    units = range(len(rows) * heads)
    row_of = [u // heads for u in units]
    head_of = [u % heads for u in units]
    masks = [position_masks(reset_ref[r], chunk) for r in rows]
    conv = []
    for r in rows:
        ext[r, 0:8, :] = tail[0, r, 0].astype(bf16).astype(f32)
        ext[r, 8:, :] = proj[0, r, 0].astype(bf16).astype(f32)
        conv.append(conv_taps(ext, r, conv_w, masks[r][5]))
    sig = [jax.nn.sigmoid(c) for c in conv]
    active = [c * g for c, g in zip(conv, sig)]
    gated = [gates(small_ref[0, r, 0], aux) for r in rows]
    beta_all = [g[0] for g in gated]
    decay = [g[1] for g in gated]
    shifted = [g[2] for g in gated]
    total = [running(d) for d in decay]
    total_rows = [as_rows(t) for t in total]
    parts = [head_parts(active[row_of[u]], head_of[u], heads) for u in units]
    a_q, a_k, v = ([p[i] for p in parts] for i in range(3))
    q_scale = [unit(a) for a in a_q]
    k_scale = [unit(a) for a in a_k]
    q = [a_q[u] * (q_scale[u] * DK**-0.5) for u in units]
    k = [a_k[u] * k_scale[u] for u in units]
    beta = [beta_all[row_of[u]][:, head_of[u] : head_of[u] + 1] for u in units]
    terms = [
        decay_terms(total[row_of[u]], total_rows[row_of[u]], head_of[u], heads, masks[row_of[u]]) for u in units
    ]
    ratios, start_fade, start_last, end_fade = ([t[i] for t in terms] for i in range(4))
    both = [jnp.concatenate([q[u], k[u]], axis=0) for u in units]
    pair = [fine(both[u], k[u], (1, 1)) for u in units]
    key_key = [p[CH:] for p in pair]
    query_key = [p[:CH] for p in pair]
    old = [state_ref[0, u] for u in units]
    inv = [inv_ref[0, u] for u in units]
    delta = [delta_ref[0, u] for u in units]
    do = [d_out[0, row_of[u], 0, :, head_of[u] * DV : (head_of[u] + 1) * DV] for u in units]
    ds = [d_state[u] for u in units]
    read = [coarse(both[u], old[u]) for u in units]
    readings = [ratios[u] * query_key[u] for u in units]
    faded = [end_fade[u] * k[u] for u in units]
    back_read = [coarse(readings[u], do[u], (0, 0)) for u in units]
    back_state = [coarse(faded[u], ds[u]) for u in units]
    d_right = [coarse(inv[u], back_read[u] + back_state[u], (0, 0)) for u in units]
    d_pair = [coarse(jnp.concatenate([do[u], d_right[u]], axis=0), delta[u], (1, 1)) for u in units]
    d_faded = [coarse(delta[u], ds[u], (1, 1)) for u in units]
    d_read = [
        jnp.concatenate([start_fade[u] * do[u], -(beta[u] * start_fade[u]) * d_right[u]], axis=0) for u in units
    ]
    grown = [coarse(both[u], d_read[u], (0, 0)) for u in units]
    d_both = [coarse(d_read[u], old[u], (1, 1)) for u in units]
    for u in units:
        d_state[u] = start_last[u] * ds[u] + grown[u]
    d_v = [beta[u] * d_right[u] for u in units]
    d_read_pair = [d_pair[u][:CH] * ratios[u] for u in units]
    d_sys = [-d_pair[u][CH:] * (ratios[u] * masks[row_of[u]][1]) for u in units]
    d_key_key = [beta[u] * d_sys[u] for u in units]
    moved = [d_key_key[u] * key_key[u] + d_read_pair[u] * query_key[u] for u in units]
    moved_cols = [fine(m, ones, (0, 0))[:, 0:1] for m in moved]
    q_more = [coarse(d_read_pair[u], k[u]) for u in units]
    k_more = [coarse(jnp.concatenate([d_read_pair[u], d_key_key[u]], axis=0), both[u], (0, 0)) for u in units]
    k_most = [coarse(d_key_key[u], k[u]) for u in units]
    d_beta_all = [jnp.zeros((CH, LANES), f32) for _ in rows]
    d_total = [jnp.zeros((CH, LANES), f32) for _ in rows]
    d_active = []
    for u in units:
        r, head = row_of[u], head_of[u]
        recall = read[u][CH:]
        d_beta = jnp.sum(d_right[u] * (v[u] - start_fade[u] * recall), axis=-1, keepdims=True) + jnp.sum(
            d_sys[u] * key_key[u], axis=-1, keepdims=True
        )
        d_start = jnp.sum(do[u] * read[u][:CH], axis=-1, keepdims=True) - beta[u] * jnp.sum(
            d_right[u] * recall, axis=-1, keepdims=True
        )
        d_end = jnp.sum(d_faded[u] * k[u], axis=-1, keepdims=True) * end_fade[u]
        d_last = jnp.sum(d_end, axis=0, keepdims=True) + start_last[u] * jnp.sum(
            jnp.sum(ds[u] * old[u], axis=-1, keepdims=True), axis=0, keepdims=True
        )
        d_col = (
            jnp.sum(moved[u], axis=-1, keepdims=True)
            - moved_cols[u]
            + d_start * start_fade[u]
            - d_end
            + jnp.where(last_row, d_last, 0.0)
        )
        d_q = d_both[u][:CH] + q_more[u]
        d_k = d_both[u][CH:] + k_more[u] + k_most[u] + end_fade[u] * d_faded[u]
        d_aq = (q_scale[u] * DK**-0.5) * (
            d_q - a_q[u] * (q_scale[u] * q_scale[u] * jnp.sum(a_q[u] * d_q, axis=-1, keepdims=True))
        )
        d_ak = k_scale[u] * (
            d_k - a_k[u] * (k_scale[u] * k_scale[u] * jnp.sum(a_k[u] * d_k, axis=-1, keepdims=True))
        )
        d_active.append((d_aq, d_ak, d_v[u]))
        d_beta_all[r] = jnp.where(lane_ids == head, d_beta, d_beta_all[r])
        d_total[r] = jnp.where(lane_ids == heads + head, d_col, d_total[r])
    d_decay = [running(d, reverse=True) for d in d_total]
    for r in rows:
        taps = masks[r][5]
        d_shift = d_decay[r] * (-aux[0:1]) * jax.nn.sigmoid(shifted[r])
        d_small_ref[0, r, 0] = (d_beta_all[r] * beta_all[r] * (1.0 - beta_all[r]) + d_shift).astype(bf16)
        g_decay[0:1, :] += jnp.sum(d_decay[r] * decay[r], axis=0, keepdims=True)
        g_decay[1:2, :] += jnp.sum(d_shift, axis=0, keepdims=True)
        own = d_active[r * heads : (r + 1) * heads]
        d_act = jnp.concatenate([own[h][i] for i in range(3) for h in range(heads)], axis=1)
        d_conv = d_act * (sig[r] * (1.0 + conv[r] * (1.0 - sig[r])))
        d_in = None
        for j in range(TAPS):
            masked = d_conv * taps[j]
            g_conv[j : j + 1, :] += jnp.sum(
                masked * ext[r, 8 - (TAPS - 1) + j : 8 - (TAPS - 1) + j + CH, :], axis=0, keepdims=True
            )
            dext[r, j, 0:CH, :] = masked
            shift = TAPS - 1 - j
            part = conv_w[j : j + 1] * dext[r, j, shift : shift + CH, :]
            d_in = part if d_in is None else d_in + part
            dext[r, j, CH : CH + 8, :] = masked[0:8]
        d_proj[0, r, 0] = d_in.astype(bf16)


def params():
    return pltpu.CompilerParams(dimension_semantics=("arbitrary",), vmem_limit_bytes=VMEM_BYTES)


def whole(array):
    return pl.BlockSpec(array.shape, lambda c, pos, rst: (0,) * array.ndim)


SMALL_COST = pl.CostEstimate(flops=1_000_000, bytes_accessed=1_000, transcendentals=0)


def slot_spec(rows_n, width, chunk_of):
    return pl.BlockSpec(
        (1, rows_n, 1, CH, width), lambda c, pos, rst: (pos[chunk_of(c)] & 1, 0, pos[chunk_of(c)] >> 1, 0, 0)
    )


def prepare_kernel(
    heads, pos_ref, reset_ref, first, second, tail, small_a, small_b, conv_w_ref, aux_ref, *outs_and_scratch
):
    both_out, value_out, inv_out, read_out, cols_out, ext = outs_and_scratch
    step = pl.program_id(0)
    conv_w = conv_w_ref[...]
    aux = aux_ref[...]
    lane_ids = lax.broadcasted_iota(jnp.int32, (CH, LANES), 1)
    systems = []
    for row in range(first.shape[1]):
        ext[row, 0:8, :] = jnp.where(step > 0, tail[0, row, 0].astype(bf16).astype(f32), 0.0)
        ext[row, 8 : 8 + CH, :] = first[0, row, 0].astype(bf16).astype(f32)
        ext[row, 8 + CH :, :] = second[0, row, 0].astype(bf16).astype(f32)
        for which, small_ref in enumerate((small_a, small_b)):
            masks = position_masks(reset_ref[row], 2 * step + which)
            conv = None
            for j in range(TAPS):
                at = which * CH + 8 - (TAPS - 1) + j
                part = conv_w[j : j + 1] * (ext[row, at : at + CH, :] * masks[5][j])
                conv = part if conv is None else conv + part
            active = conv * jax.nn.sigmoid(conv)
            beta_all, decay, _ = gates(small_ref[0, row, 0], aux)
            total = running(decay)
            total_rows = as_rows(total)
            for head in range(heads):
                at = row * heads + head
                q, k, v = head_parts(active, head, heads)
                q = q * (unit(q) * DK**-0.5)
                k = k * unit(k)
                beta = beta_all[:, head : head + 1]
                ratios, start_fade, start_last, end_fade = decay_terms(total, total_rows, head, heads, masks)
                both = jnp.concatenate([q, k], axis=0)
                pair = fine(both, k, (1, 1))
                both_out[which, at] = both
                value_out[which, at] = v
                systems.append((which, at, beta * (ratios * masks[1] * pair[CH:])))
                read_out[which, at] = ratios * pair[:CH]
                cols_out[which, at] = jnp.where(
                    lane_ids == 0,
                    beta,
                    jnp.where(lane_ids == 1, start_fade, jnp.where(lane_ids == 2, end_fade, start_last)),
                )
    for (which, at, _), inv in zip(systems, inverses_unit_lower([part for _, _, part in systems])):
        inv_out[which, at] = inv


def scan_kernel(heads, pos_ref, both_ref, value_ref, inv_ref, read_ref, cols_ref, outs, state_out, delta_out, state):
    @pl.when(pl.program_id(0) == 0)
    def _():
        state[...] = jnp.zeros_like(state)

    state_out[0] = state[...]
    units = range(state.shape[0])
    old = [state[u] for u in units]
    beta = [cols_ref[0, u, :, 0:1] for u in units]
    start_fade = [cols_ref[0, u, :, 1:2] for u in units]
    end_fade = [cols_ref[0, u, :, 2:3] for u in units]
    start_last = [cols_ref[0, u, 0:1, 3:4] for u in units]
    read = [coarse(both_ref[0, u], old[u]) for u in units]
    right = [beta[u] * (value_ref[0, u] - start_fade[u] * read[u][CH:]) for u in units]
    delta = [coarse(inv_ref[0, u], right[u]) for u in units]
    grown = [coarse(end_fade[u] * both_ref[0, u, CH:, :], delta[u], (0, 0)) for u in units]
    local = [coarse(read_ref[0, u], delta[u]) for u in units]
    for u in units:
        row, head = divmod(u, heads)
        state[u] = start_last[u] * old[u] + grown[u]
        outs[0, row, 0, :, head * DV : (head + 1) * DV] = start_fade[u] * read[u][:CH] + local[u]
        delta_out[0, u] = delta[u]


def mixer_prepare(proj, small, pos, resets, conv_w, aux):
    _, rows_n, half, _, _ = proj.shape
    width = conv_w.shape[1]
    chunks = 2 * half
    heads = width // (2 * DK + DV)
    units = rows_n * heads
    tail = pl.BlockSpec(
        (1, rows_n, 1, 8, width),
        lambda i, pos, rst: (
            pos[jnp.maximum(2 * i - 1, 0)] & 1,
            0,
            pos[jnp.maximum(2 * i - 1, 0)] >> 1,
            CH // 8 - 1,
            0,
        ),
    )
    even = lambda w: slot_spec(rows_n, w, lambda i: 2 * i)
    odd = lambda w: slot_spec(rows_n, w, lambda i: 2 * i + 1)
    shapes = ((2 * CH, DK), (CH, DV), (CH, CH), (CH, CH), (CH, LANES))
    return pl.pallas_call(
        partial(prepare_kernel, heads),
        grid_spec=pltpu.PrefetchScalarGridSpec(
            num_scalar_prefetch=2,
            grid=(half,),
            in_specs=[even(width), odd(width), tail, even(LANES), odd(LANES), whole(conv_w), whole(aux)],
            out_specs=[pl.BlockSpec((2, units) + s, lambda i, pos, rst: (i, 0, 0, 0)) for s in shapes],
            scratch_shapes=[pltpu.VMEM((rows_n, 2 * CH + 8, width), f32)],
        ),
        out_shape=[jax.ShapeDtypeStruct((chunks, units) + s, f32) for s in shapes],
        cost_estimate=KERNEL_COST,
        compiler_params=params(),
        name="delta_prepare",
    )(pos, resets, proj, proj, proj, small, small, conv_w, aux)


def mixer_scan(prepared, pos, rows_n):
    chunks, units = prepared[0].shape[:2]
    heads = units // rows_n
    kept = lambda *s: pl.BlockSpec((1, units) + s, lambda c, pos: (c, 0, 0, 0))
    mixed, states, deltas = pl.pallas_call(
        partial(scan_kernel, heads),
        grid_spec=pltpu.PrefetchScalarGridSpec(
            num_scalar_prefetch=1,
            grid=(chunks,),
            in_specs=[kept(*p.shape[2:]) for p in prepared],
            out_specs=[
                pl.BlockSpec(
                    (1, rows_n, 1, CH, heads * DV), lambda c, pos: (pos[c] & 1, 0, pos[c] >> 1, 0, 0)
                ),
                kept(DK, DV),
                kept(CH, DV),
            ],
            scratch_shapes=[pltpu.VMEM((units, DK, DV), f32)],
        ),
        out_shape=[
            jax.ShapeDtypeStruct((2, rows_n, chunks // 2, CH, heads * DV), f32),
            jax.ShapeDtypeStruct((chunks, units, DK, DV), f32),
            jax.ShapeDtypeStruct((chunks, units, CH, DV), f32),
        ],
        cost_estimate=SMALL_COST,
        compiler_params=params(),
        name="delta_scan",
    )(pos, *prepared)
    return mixed, states, prepared[2], deltas


def mixer_backward(proj, small, d_out, pos, resets, conv_w, aux, states, invs, deltas):
    _, rows_n, half, _, _ = proj.shape
    width = conv_w.shape[1]
    chunks = 2 * half
    heads = width // (2 * DK + DV)
    units = rows_n * heads
    back = lambda c: chunks - 1 - c
    before = lambda c: jnp.maximum(back(c) - 1, 0)
    spec = lambda w: slot_spec(rows_n, w, back)
    tail = pl.BlockSpec(
        (1, rows_n, 1, 8, width),
        lambda c, pos, rst: (pos[before(c)] & 1, 0, pos[before(c)] >> 1, CH // 8 - 1, 0),
    )
    kept = lambda *s: pl.BlockSpec((1, units) + s, lambda c, pos, rst: (back(c), 0, 0, 0))
    return pl.pallas_call(
        partial(backward_kernel, heads, chunks),
        grid_spec=pltpu.PrefetchScalarGridSpec(
            num_scalar_prefetch=2,
            grid=(chunks,),
            in_specs=[spec(width), spec(LANES), tail, spec(heads * DV), whole(conv_w), whole(aux)]
            + [kept(DK, DV), kept(CH, CH), kept(CH, DV)],
            out_specs=[
                spec(width),
                spec(LANES),
                pl.BlockSpec((8, width), lambda c, pos, rst: (0, 0)),
                pl.BlockSpec((8, LANES), lambda c, pos, rst: (0, 0)),
            ],
            scratch_shapes=[
                pltpu.VMEM((rows_n, CH + 8, width), f32),
                pltpu.VMEM((rows_n, TAPS, CH + 8, width), f32),
                pltpu.VMEM((units, DK, DV), f32),
            ],
        ),
        out_shape=[
            jax.ShapeDtypeStruct((2, rows_n, half, CH, width), bf16),
            jax.ShapeDtypeStruct((2, rows_n, half, CH, LANES), bf16),
            jax.ShapeDtypeStruct((8, width), f32),
            jax.ShapeDtypeStruct((8, LANES), f32),
        ],
        cost_estimate=KERNEL_COST,
        compiler_params=params(),
        name="delta_backward",
    )(pos, resets, proj, small, proj, d_out, conv_w, aux, states, invs, deltas)


def local_call(body, name, inputs, specs, outs, bytes_accessed=0):
    return pl.pallas_call(
        body,
        grid=(1,),
        in_specs=specs,
        out_specs=whole_specs(outs),
        out_shape=outs,
        cost_estimate=SMALL_COST,
        compiler_params=pltpu.CompilerParams(vmem_limit_bytes=VMEM_BYTES),
        name=name,
    )(*inputs)


def term_specs(terms):
    kept, got, steps = terms
    rows_n = kept.shape[0]
    first = pl.BlockSpec((rows_n, 1) + kept.shape[2:], lambda i: (0, 0, 0, 0))
    flat = [step for row in steps for step in row]
    return [kept, got] + flat, [first, first] + [pl.BlockSpec((1,) + s.shape[1:], lambda i: (0, 0, 0)) for s in flat]


def row_total(refs, row, rows_n):
    kept, got = refs[0], refs[1]
    each = (len(refs) - 2) // rows_n
    total = kept[row, 0].astype(f32) + got[row, 0].astype(f32)
    for step in refs[2 + row * each : 2 + (row + 1) * each]:
        total = total + step[0].astype(f32)
    return total


def in_order(values, groups):
    size, batches = groups
    own = values.shape[-1] // (size * batches)
    return jnp.concatenate(
        [
            values[:, (b * size + s) * own : (b * size + s + 1) * own]
            for s in range(size)
            for b in range(batches)
        ],
        axis=1,
    )


def whole_specs(arrays):
    zeros = lambda n: lambda i: (0,) * n
    return [pl.BlockSpec(a.shape, zeros(len(a.shape))) for a in arrays]


def add_and_norm(terms, base, gain):
    inputs, specs = term_specs(terms)
    rows_n, _, span, _ = terms[0].shape

    def body(*refs):
        base_ref, gain_ref, out_ref, norm_ref = refs[len(inputs) :]
        for row in range(rows_n):
            at = pl.ds(row * span, span)
            total = base_ref[at, :].astype(f32) + row_total(refs[: len(inputs)], row, rows_n)
            scale = lax.rsqrt(jnp.mean(total * total, axis=-1, keepdims=True) + EPS_NORM)
            out_ref[at, :] = total
            norm_ref[row] = (total * scale * gain_ref[...]).astype(bf16)

    extra = [base, gain.reshape(1, D)]
    return local_call(
        body,
        "add_and_norm",
        inputs + extra,
        specs + whole_specs(extra),
        [jax.ShapeDtypeStruct((rows_n * span, D), f32), jax.ShapeDtypeStruct((rows_n, span, D), bf16)],
        4_000_000,
    )


def norm_back(terms, base, through, gain, out_dtype, groups=None):
    inputs, specs = term_specs(terms)
    rows_n, _, span, _ = terms[0].shape
    with_rows = groups is None

    def body(*refs):
        base_ref, through_ref, gain_ref = refs[len(inputs) : len(inputs) + 3]
        outs = refs[len(inputs) + 3 :]
        g_gain = jnp.zeros((1, D), f32)
        for row in range(rows_n):
            at = pl.ds(row * span, span)
            d_norm = row_total(refs[: len(inputs)], row, rows_n)
            x = base_ref[at, :].astype(f32)
            scale = lax.rsqrt(jnp.mean(x * x, axis=-1, keepdims=True) + EPS_NORM)
            e = d_norm * gain_ref[...]
            lean = jnp.mean(e * x, axis=-1, keepdims=True)
            total = through_ref[at, :].astype(f32) + scale * e - x * (scale * scale * scale * lean)
            g_gain = g_gain + jnp.sum(d_norm * x * scale, axis=0, keepdims=True)
            if with_rows:
                outs[0][at, :] = total.astype(out_dtype)
                outs[1][row] = total.astype(bf16)
            else:
                outs[0][at, :] = in_order(total, groups).astype(out_dtype)
        outs[-1][...] = g_gain

    extra = [base, through, gain.reshape(1, D)]
    outs = [jax.ShapeDtypeStruct((rows_n * span, D), out_dtype)]
    if with_rows:
        outs.append(jax.ShapeDtypeStruct((rows_n, span, D), bf16))
    return local_call(
        body,
        "norm_back",
        inputs + extra,
        specs + whole_specs(extra),
        outs + [jax.ShapeDtypeStruct((1, D), f32)],
        4_000_000,
    )


def add_in_order(terms, base, groups):
    inputs, specs = term_specs(terms)
    rows_n, _, span, _ = terms[0].shape

    def body(*refs):
        base_ref, out_ref = refs[len(inputs) :]
        for row in range(rows_n):
            at = pl.ds(row * span, span)
            total = base_ref[at, :] + row_total(refs[: len(inputs)], row, rows_n)
            out_ref[at, :] = in_order(total, groups).astype(bf16)

    return local_call(
        body,
        "add_in_order",
        inputs + [base],
        specs + whole_specs([base]),
        [jax.ShapeDtypeStruct((rows_n * span, D), bf16)],
        3_000_000,
    )[0]


ROW_BLOCK = 256


def gated_norm(mixed, proj, gain):
    rows_n, width = mixed.shape
    gate_block = pl.BlockSpec((ROW_BLOCK, width), lambda i: (i, proj.shape[1] // width - 1))

    def body(mixed_ref, gate_ref, gain_ref, out_ref):
        for at in range(0, width, DV):
            x = mixed_ref[:, at : at + DV]
            g = gate_ref[:, at : at + DV]
            scale = lax.rsqrt(jnp.mean(x * x, axis=-1, keepdims=True) + EPS_HEAD)
            out_ref[:, at : at + DV] = (x * scale * gain_ref[...] * (g * jax.nn.sigmoid(g))).astype(bf16)

    block = pl.BlockSpec((ROW_BLOCK, width), lambda i: (i, 0))
    return pl.pallas_call(
        body,
        grid=(rows_n // ROW_BLOCK,),
        in_specs=[block, gate_block, pl.BlockSpec((1, DV), lambda i: (0, 0))],
        out_specs=block,
        out_shape=jax.ShapeDtypeStruct((rows_n, width), bf16),
        cost_estimate=SMALL_COST,
        compiler_params=params(),
        name="gated_norm",
    )(mixed, proj, gain.reshape(1, DV))


def gated_norm_back(mixed, proj, gain, d_out):
    rows_n, width = mixed.shape
    gate_block = pl.BlockSpec((ROW_BLOCK, width), lambda i: (i, proj.shape[1] // width - 1))

    def body(mixed_ref, gate_ref, gain_ref, d_ref, d_mixed_ref, d_gate_ref, g_gain_ref):
        @pl.when(pl.program_id(0) == 0)
        def _():
            g_gain_ref[...] = jnp.zeros_like(g_gain_ref)

        g_gain = jnp.zeros((1, DV), f32)
        for at in range(0, width, DV):
            x = mixed_ref[:, at : at + DV]
            g = gate_ref[:, at : at + DV]
            d = d_ref[:, at : at + DV]
            scale = lax.rsqrt(jnp.mean(x * x, axis=-1, keepdims=True) + EPS_HEAD)
            sig = jax.nn.sigmoid(g)
            through = d * (g * sig)
            unit_x = x * scale
            e = through * gain_ref[...]
            lean = jnp.mean(e * unit_x, axis=-1, keepdims=True)
            d_mixed_ref[:, at : at + DV] = scale * (e - unit_x * lean)
            d_gate_ref[:, at : at + DV] = (
                d * (unit_x * gain_ref[...]) * (sig * (1.0 + g * (1.0 - sig)))
            ).astype(bf16)
            g_gain = g_gain + jnp.sum(through * unit_x, axis=0, keepdims=True)
        g_gain_ref[0:1, :] += g_gain

    block = pl.BlockSpec((ROW_BLOCK, width), lambda i: (i, 0))
    return pl.pallas_call(
        body,
        grid=(rows_n // ROW_BLOCK,),
        in_specs=[block, gate_block, pl.BlockSpec((1, DV), lambda i: (0, 0)), block],
        out_specs=[block, block, pl.BlockSpec((8, DV), lambda i: (0, 0))],
        out_shape=[
            jax.ShapeDtypeStruct((rows_n, width), f32),
            jax.ShapeDtypeStruct((rows_n, width), bf16),
            jax.ShapeDtypeStruct((8, DV), f32),
        ],
        cost_estimate=SMALL_COST,
        compiler_params=params(),
        name="gated_norm_back",
    )(mixed, proj, gain.reshape(1, DV), d_out)


def laid_out(blocks, pieces, total):
    size, rows_n, _ = blocks[0].shape

    def body(*refs):
        out_ref = refs[-1]
        for which, first, width, start in pieces:
            for s in range(size):
                out_ref[:, start + s * width : start + (s + 1) * width] = refs[which][
                    s, :, first : first + width
                ].astype(f32)

    return local_call(
        body, "laid_out", blocks, whole_specs(blocks), [jax.ShapeDtypeStruct((rows_n, total), f32)], 5_000_000
    )[0]


def swap(value, axis, bit):
    return lax.ppermute(value, axis, [(i, i ^ bit) for i in range(lax.axis_size(axis))])


def routes(axis):
    bits = [1 << i for i in range(lax.axis_size(axis).bit_length() - 1)]
    return [bits[1:] + bits[:1], bits[:0:-1] + bits[:1]]


def gather_rows(rows, axis, ordered=True, earlier=None):
    laid = []
    for row, order in zip(rows, routes(axis) * rows.shape[0]):
        held = row[None]
        names = [0]
        parts = []
        for i, bit in enumerate(order[:-1]):
            got = swap(held, axis, bit)
            names = names + [n ^ (bit >> 1) for n in names]
            if i < len(order) - 2:
                held = jnp.concatenate([held, got], axis=0)
            else:
                parts = [held, got]
        if ordered and names != sorted(names):
            place = {name: i for i, name in enumerate(names)}
            size = len(names) // 2
            for n in sorted(names):
                which, at = divmod(place[n], size)
                laid.append(parts[which][at : at + 1])
        else:
            laid.extend(parts)
    even = jnp.concatenate(laid, axis=0).reshape((rows.shape[0], -1) + rows.shape[1:])
    if earlier is not None:
        even, earlier = lax.optimization_barrier((even, earlier))
        return even, swap(even, axis, 1), earlier
    return even, swap(even, axis, 1)


def scatter_rows(keep, send, axis, ordered=True, earlier=()):
    got = after(swap(send, axis, 1), *earlier)
    rows_n, half, span, width = keep.shape
    depth = half.bit_length() - 1
    steps = []
    for row, order in zip(range(rows_n), routes(axis) * rows_n):
        bits = order[:-1]
        axes = sorted(bits, reverse=True) if ordered else bits[::-1]
        shape = (2,) * depth + (span, width)
        terms = [keep[row].reshape(shape), got[row].reshape(shape)]
        mine = []
        for bit in bits[::-1]:
            at = axes.index(bit)
            sent = sum(lax.index_in_dim(t, 1, at, keepdims=False).astype(f32) for t in terms).astype(bf16)
            back = swap(sent, axis, bit)
            terms = [lax.index_in_dim(t, 0, at, keepdims=False) for t in terms] + [back]
            axes = [b for b in axes if b != bit]
            mine.append(back.reshape((-1, span, width)))
        steps.append(mine)
    return keep, got, steps


def joined(halves):
    return jnp.concatenate([h.reshape(-1, h.shape[-1]) for h in halves], axis=0)


def after(value, *earlier):
    return lax.optimization_barrier((value,) + earlier)[0]


def sum_all(value, axes):
    for axis in axes:
        for i in range(lax.axis_size(axis).bit_length() - 1):
            value = value + swap(value, axis, 1 << i)
    return value


def gather_small(value, axis):
    held = value[None]
    size = lax.axis_size(axis)
    for i in range(size.bit_length() - 1):
        held = jnp.concatenate([held, swap(held, axis, 1 << i)], axis=0)
    return held[jnp.arange(size, dtype=jnp.int32) ^ lax.axis_index(axis).astype(jnp.int32)]


def mm(left, right):
    return jnp.dot(left, right, preferred_element_type=f32)


def contract_rows(left, right):
    return lax.dot_general(left, right, (((0,), (0,)), ((), ())), preferred_element_type=f32)


def contract_cols(left, right):
    return lax.dot_general(left, right, (((1,), (1,)), ((), ())), preferred_element_type=f32)


def rms_scale(values, scale_gain):
    return values * lax.rsqrt(jnp.mean(values * values, axis=-1, keepdims=True) + EPS_NORM) * scale_gain


def glu_hidden(gate_half, up_half):
    return jax.nn.silu(gate_half) * up_half


def exchanged(packed):
    return lax.all_to_all(packed, "seq", split_axis=0, concat_axis=0, tiled=True)


def stacked(blocks):
    full = lax.all_gather(blocks, "batch", axis=0, tiled=False)
    return full.reshape(-1, blocks.shape[-1])


def summed(partial_grad):
    own = lax.psum_scatter(partial_grad, "batch", scatter_dimension=0, tiled=True)
    return own.reshape(lax.axis_size("seq"), -1, own.shape[-1])


def shards(
    tokens,
    grad_out,
    resets,
    w_proj,
    w_small,
    w_out,
    w_gu,
    w_down,
    norm_in,
    norm_ff,
    norm_head,
    conv_w,
    a_log,
    dt_bias,
):
    size = lax.axis_size("seq")
    groups = lax.axis_size("batch")
    me = lax.axis_index("seq")
    batch_rows, span_len, _ = tokens.shape
    own_rows = w_proj.shape[0]
    heads = H // size
    ff = FF // size
    key_w, val_w = heads * DK, heads * DV
    conv_cols = 2 * key_w + val_w
    half = batch_rows * size // 2 * span_len
    halves = (batch_rows, size // 2, span_len)
    blocks = (2,) + halves

    def shuffled(array):
        lead = array.shape[:-1]
        return array.reshape(lead + (size, groups, own_rows)).swapaxes(-3, -2).reshape(lead + (D,))

    def restored(array):
        lead = array.shape[:-1]
        return array.reshape(lead + (groups, size, own_rows)).swapaxes(-3, -2).reshape(lead + (D,))

    out_w = lax.all_gather(w_out, "batch", axis=0, tiled=True)
    packed_mix = jnp.concatenate(
        [
            w_proj[:, :KW].reshape(own_rows, size, key_w),
            w_proj[:, KW : 2 * KW].reshape(own_rows, size, key_w),
            w_proj[:, 2 * KW : CW].reshape(own_rows, size, val_w),
            w_proj[:, CW:].reshape(own_rows, size, val_w),
        ],
        axis=-1,
    ).transpose(1, 0, 2)
    moved_mix = exchanged(packed_mix)
    own_in = shuffled(tokens).reshape(-1, D)
    gain_in, gain_ff = shuffled(norm_in), shuffled(norm_ff)
    h_in = joined(gather_rows(rms_scale(own_in.astype(f32), gain_in).astype(bf16).reshape(tokens.shape), "seq"))
    mix_w = stacked(after(moved_mix, out_w, h_in))
    packed_gu, w_small, d_own, own_down = after(
        (
            w_gu.reshape(own_rows, 2, size, ff).transpose(2, 0, 1, 3).reshape(size, own_rows, 2 * ff),
            w_small,
            shuffled(grad_out),
            shuffled(w_down),
        ),
        moved_mix,
    )
    d_halves = gather_rows(d_own, "seq", False)
    small_all = gather_small(gather_small(w_small, "seq"), "batch").reshape(D, 2 * H)
    small_w = jnp.pad(
        jnp.concatenate(
            [
                lax.dynamic_slice_in_dim(small_all, me * heads, heads, 1),
                lax.dynamic_slice_in_dim(small_all, H + me * heads, heads, 1),
            ],
            axis=1,
        ),
        ((0, 0), (0, LANES - 2 * heads)),
    )
    out_w = shuffled(out_w)
    moved_gu = exchanged(packed_gu)

    slots = jnp.arange(size, dtype=jnp.int32) ^ me.astype(jnp.int32)
    conv_l = jnp.concatenate(
        [
            lax.dynamic_slice_in_dim(conv_w, me * key_w, key_w, 1),
            lax.dynamic_slice_in_dim(conv_w, KW + me * key_w, key_w, 1),
            lax.dynamic_slice_in_dim(conv_w, 2 * KW + me * val_w, val_w, 1),
        ],
        axis=1,
    )
    at_heads = (heads, LANES - 2 * heads)
    aux = jnp.pad(
        jnp.stack(
            [
                lax.dynamic_slice_in_dim(jnp.exp(a_log), me * heads, heads),
                lax.dynamic_slice_in_dim(dt_bias, me * heads, heads),
            ]
        ),
        ((0, 6), at_heads),
    )

    small = mm(h_in, small_w).reshape(blocks + (LANES,))
    proj = mm(h_in, mix_w)
    down_first = lax.all_gather(own_down[:, : D // 2], "batch", axis=0, tiled=True)
    prepared = mixer_prepare(proj.reshape(blocks + (-1,)), small, slots, resets, conv_l, aux)
    prepared, moved_gu, down_first = lax.optimization_barrier((prepared, moved_gu, down_first))
    down_rest = lax.all_gather(own_down[:, D // 2 :], "batch", axis=0, tiled=True)
    gu_w = stacked(moved_gu)
    mixed, states, invs, deltas = mixer_scan(prepared, slots, batch_rows)
    mixed = mixed.reshape(-1, val_w)
    z_rows = gated_norm(mixed, proj, norm_head)

    def parts(product, left):
        send = product(left[half:]).astype(bf16).reshape(halves + (D,))
        return product(left[:half]).astype(bf16).reshape(halves + (D,)), send

    keep, send = parts(lambda rows: mm(rows, out_w), z_rows)
    d_out = joined(after(d_halves, keep, send))
    residual, normed_ff = add_and_norm(scatter_rows(keep, send, "seq"), own_in, gain_ff)

    even, odd, gu_w = gather_rows(normed_ff, "seq", False, gu_w)
    h_ff = joined((even, odd))
    gate_up = mm(h_ff, gu_w)
    hidden_full, pull_glu = jax.vjp(glu_hidden, gate_up[:, :ff], gate_up[:, ff:])
    hidden, down_rest = lax.optimization_barrier((hidden_full.astype(bf16), down_rest))
    down_grad = contract_rows(d_out, hidden).astype(bf16)
    down_own = summed(down_grad)
    d_hidden = contract_cols(d_out[:, : D // 2], down_first) + contract_cols(d_out[:, D // 2 :], down_rest)
    down_w = jnp.concatenate([down_first, down_rest], axis=1)
    d_gate_up = jnp.concatenate(pull_glu(d_hidden), axis=1).astype(bf16)
    keep, send = parts(lambda rows: contract_cols(rows, gu_w), d_gate_up)
    terms = scatter_rows(keep, send, "seq", False)
    gu_grad = contract_rows(after(h_ff, keep, send), d_gate_up).astype(bf16)
    gu_own = summed(gu_grad)
    out_parts = parts(lambda rows: mm(rows, down_w), after(hidden, keep, send))
    d_residual, d_branch, g_norm_ff = norm_back(terms, residual, d_own.reshape(-1, D), gain_ff, f32)

    d_branch = joined(gather_rows(after(d_branch, gu_grad, down_own, out_parts), "seq"))
    d_heads = contract_cols(d_branch, out_w)
    d_mixed, d_gate, g_norm_head = gated_norm_back(mixed, proj, norm_head, d_heads)
    out_grad = jnp.concatenate(
        [contract_rows(h_in, d_gate).astype(bf16), contract_rows(d_branch, z_rows).astype(bf16)], axis=1
    )
    d_mixed, out_grad = lax.optimization_barrier((d_mixed, out_grad))
    d_proj, d_small, g_conv_l, g_decay = mixer_backward(
        proj.reshape(blocks + (-1,)), small, d_mixed.reshape(blocks + (val_w,)), slots, resets, conv_l, aux, states, invs, deltas
    )
    d_proj, gu_own = lax.optimization_barrier((d_proj.reshape(-1, conv_cols), gu_own))
    d_small = d_small.reshape(-1, LANES)
    out_own = summed(out_grad)
    mix_grad = contract_rows(h_in, d_proj).astype(bf16)
    mix_moved = lax.all_to_all(
        mix_grad.reshape(groups, size, own_rows, conv_cols), "seq", split_axis=1, concat_axis=1, tiled=True
    )
    mix_grads = lax.psum_scatter(mix_moved, "batch", scatter_dimension=0, tiled=True)[0]
    d_proj, d_small, g_conv_l, gu_own = after((d_proj, d_small, g_conv_l, gu_own), mix_grad)
    gu_grads, down_grads = exchanged(gu_own), exchanged(down_own)
    block_out = add_in_order(scatter_rows(*out_parts, "seq", False), residual, (size, groups))
    keep, send = parts(
        lambda rows: contract_cols(rows[:, : conv_cols + val_w], mix_w)
        + contract_cols(rows[:, conv_cols + val_w :], small_w),
        jnp.concatenate([d_proj, d_gate, d_small], axis=1),
    )
    d_tokens, g_norm_in = norm_back(
        scatter_rows(keep, send, "seq"), own_in, after(d_residual, out_own), gain_in, bf16, (size, groups)
    )

    small_grad = contract_rows(d_small, h_in)[: 2 * heads]
    local = jnp.concatenate(
        [g_conv_l[:TAPS].reshape(-1), g_decay[:2, heads : 2 * heads].reshape(-1), small_grad.reshape(-1)]
    )
    shared = gather_small(sum_all(local, ("batch",)), "seq")
    g_conv_all = shared[:, : TAPS * conv_cols].reshape(size, TAPS, conv_cols).transpose(1, 0, 2)
    g_conv = jnp.concatenate(
        [
            g_conv_all[:, :, :key_w].reshape(TAPS, KW),
            g_conv_all[:, :, key_w : 2 * key_w].reshape(TAPS, KW),
            g_conv_all[:, :, 2 * key_w :].reshape(TAPS, VW),
        ],
        axis=1,
    )
    g_alog = shared[:, TAPS * conv_cols : TAPS * conv_cols + heads].reshape(H)
    g_dt = shared[:, TAPS * conv_cols + heads : TAPS * conv_cols + 2 * heads].reshape(H)
    g_small = lax.dynamic_slice_in_dim(
        shared[:, TAPS * conv_cols + 2 * heads :].reshape(size, 2, heads, D),
        (lax.axis_index("batch") * size + me) * own_rows,
        own_rows,
        3,
    )
    g_small = g_small.transpose(3, 1, 0, 2).reshape(own_rows, 2 * H)
    gains = sum_all(jnp.concatenate([g_norm_in[0], g_norm_ff[0], g_norm_head[0]]), ("seq", "batch"))
    gains = jnp.concatenate([restored(gains[: 2 * D].reshape(2, D)).reshape(-1), gains[2 * D :]])

    out_grads = exchanged(out_own)
    g_gu = laid_out([gu_grads], [(0, 0, ff, 0), (0, ff, ff, FF)], 2 * FF)
    g_down = down_grads.astype(f32).transpose(0, 2, 1).reshape(FF, own_rows)
    g_out = out_grads[:, :, val_w:].astype(f32).transpose(0, 2, 1).reshape(VW, own_rows)
    ready = (d_tokens, block_out, out_grads, g_gu, g_down, g_out, gains, g_conv, g_small)
    mix_grads, ready = lax.optimization_barrier((mix_grads, ready))
    d_tokens, block_out, out_grads, g_gu, g_down, g_out, gains, g_conv, g_small = ready
    g_proj = laid_out(
        [mix_grads, out_grads],
        [(0, 0, key_w, 0), (0, key_w, key_w, KW), (0, 2 * key_w, val_w, 2 * KW), (1, 0, val_w, CW)],
        CW + VW,
    )
    return (
        block_out.reshape(tokens.shape),
        d_tokens.reshape(tokens.shape),
        g_proj,
        g_small,
        g_out,
        g_gu,
        g_down,
        gains[:D],
        gains[D : 2 * D],
        gains[2 * D :],
        g_conv,
        g_alog,
        g_dt,
    )


def solution(mesh):
    rows = P(("seq", "batch"), None)
    cols = P(None, ("seq", "batch"))
    act = P("batch", "seq", None)
    in_specs = (act, act, P("batch"), rows, rows, rows, rows, rows) + (P(),) * 6
    out_specs = (act, act, rows, rows, cols, rows, cols) + (P(),) * 6
    return jax.shard_map(shards, mesh=mesh, in_specs=in_specs, out_specs=out_specs, check_vma=False)
```

```python
from functools import partial

import jax
import jax.numpy as jnp
from jax import lax
from jax.experimental import pallas as pl
from jax.experimental.pallas import tpu as pltpu
from jax.sharding import PartitionSpec as P

D = 2048
H = 16
DK = 128
DV = 256
FF = 5632
CH = 64
KW = 2048
VW = 4096
CW = 8192
TAPS = 4
LANES = 128

EPS_NORM = 1e-06
EPS_HEAD = 1e-05
EPS_UNIT = 1e-06
f32 = jnp.float32
bf16 = jnp.bfloat16
VMEM_BYTES = 56 * 1024 * 1024
KERNEL_COST = pl.CostEstimate(flops=30_000_000_000, bytes_accessed=40_000_000, transcendentals=0)


def dot_in(left, right, contract, precision):
    return lax.dot_general(
        left,
        right,
        (((contract[0],), (contract[1],)), ((), ())),
        precision=precision,
        preferred_element_type=f32,
    )


def fine(left, right, contract=(1, 0)):
    return dot_in(left, right, contract, lax.Precision.HIGH)


def coarse(left, right, contract=(1, 0)):
    return dot_in(left, right, contract, lax.Precision.HIGH)


def position_masks(reset, chunk):
    rows = lax.broadcasted_iota(jnp.int32, (CH, CH), 0)
    cols = lax.broadcasted_iota(jnp.int32, (CH, CH), 1)
    time = lax.broadcasted_iota(jnp.int32, (CH, 1), 0)
    offset = reset - chunk * CH
    cut = jnp.where(offset < 0, CH, offset)
    apart = (rows >= cut) & (cols < cut)
    causal = jnp.where((rows >= cols) & ~apart, 1.0, 0.0)
    strict = jnp.where((rows > cols) & ~apart, 1.0, 0.0)
    in_first = jnp.where(time < cut, 1.0, 0.0)
    last_first = jnp.where(CH - 1 < cut, 1.0, 0.0)
    in_last = jnp.where((time >= cut) | (cut > CH - 1), 1.0, 0.0)
    begin = jnp.where(time >= offset, offset, -chunk * CH)
    taps = [jnp.where(time - (TAPS - 1) + j >= begin, 1.0, 0.0) for j in range(TAPS)]
    return causal, strict, in_first, last_first, in_last, taps


def gates(small, aux):
    beta = jax.nn.sigmoid(small)
    shifted = small + aux[1:2]
    soft = jnp.maximum(shifted, 0.0) + jnp.log1p(jnp.exp(-jnp.abs(shifted)))
    return beta, -aux[0:1] * soft, shifted


def running(values, reverse=False):
    rows = lax.broadcasted_iota(jnp.int32, (CH, CH), 0)
    cols = lax.broadcasted_iota(jnp.int32, (CH, CH), 1)
    keep = (cols >= rows) if reverse else (cols <= rows)
    return fine(jnp.where(keep, 1.0, 0.0), values)


def as_rows(total):
    pick_row = lax.broadcasted_iota(jnp.int32, (LANES, LANES), 0)
    pick_col = lax.broadcasted_iota(jnp.int32, (LANES, LANES), 1)
    return fine(jnp.where(pick_row == pick_col, 1.0, 0.0), total, (1, 1))


def inverses_unit_lower(parts):
    size = parts[0].shape[0]
    rows = lax.broadcasted_iota(jnp.int32, (size, size), 0)
    cols = lax.broadcasted_iota(jnp.int32, (size, size), 1)
    eye = jnp.where(rows == cols, 1.0, 0.0)
    block = lambda n: jnp.where((rows & -n) == (cols & -n), 1.0, 0.0)
    inside = {n: block(n) for n in (16, 32, 64)}
    power = [part * inside[16] for part in parts]
    inv = [eye - diag for diag in power]
    for _ in range(3):
        power = [fine(p, p) for p in power]
        more = [fine(i, p) for i, p in zip(inv, power)]
        inv = [i + m for i, m in zip(inv, more)]
    for n in (16, 32):
        ring = inside[2 * n] - inside[n]
        left = [fine(i, part * ring) for i, part in zip(inv, parts)]
        more = [fine(l, i) for l, i in zip(left, inv)]
        inv = [i - m for i, m in zip(inv, more)]
    return inv


def conv_taps(ext_ref, row, conv_w, taps):
    out = None
    for j in range(TAPS):
        part = conv_w[j : j + 1] * (ext_ref[row, 8 - (TAPS - 1) + j : 8 - (TAPS - 1) + j + CH, :] * taps[j])
        out = part if out is None else out + part
    return out


def unit(values):
    return lax.rsqrt(jnp.sum(values * values, axis=-1, keepdims=True) + EPS_UNIT)


def head_parts(active, head, heads):
    q = active[:, head * DK : (head + 1) * DK]
    k = active[:, heads * DK + head * DK : heads * DK + (head + 1) * DK]
    v = active[:, 2 * heads * DK + head * DV : 2 * heads * DK + (head + 1) * DV]
    return q, k, v


def decay_terms(total, total_rows, head, heads, masks):
    causal, strict, in_first, last_first, in_last, _ = masks
    lane = heads + head
    col = total[:, lane : lane + 1]
    row = total_rows[lane : lane + 1, :]
    ratios = jnp.exp(jnp.where(causal > 0, col - row, 0.0)) * causal
    last = col[CH - 1 : CH, :]
    start_fade = jnp.exp(col) * in_first
    start_last = jnp.exp(last) * last_first
    end_fade = jnp.exp(jnp.where(in_last > 0, last - col, 0.0)) * in_last
    return ratios, start_fade, start_last, end_fade


def backward_kernel(
    heads,
    chunks,
    pos_ref,
    reset_ref,
    proj,
    small_ref,
    tail,
    d_out,
    conv_w_ref,
    aux_ref,
    state_ref,
    inv_ref,
    delta_ref,
    d_proj,
    d_small_ref,
    g_conv,
    g_decay,
    ext,
    dext,
    d_state,
):
    step = pl.program_id(0)
    chunk = chunks - 1 - step
    width = heads * (2 * DK + DV)

    @pl.when(step == 0)
    def _():
        dext[...] = jnp.zeros_like(dext)
        d_state[...] = jnp.zeros_like(d_state)
        g_conv[...] = jnp.zeros_like(g_conv)
        g_decay[...] = jnp.zeros_like(g_decay)

    conv_w = conv_w_ref[...]
    aux = aux_ref[...]
    lane_ids = lax.broadcasted_iota(jnp.int32, (CH, LANES), 1)
    last_row = lax.broadcasted_iota(jnp.int32, (CH, 1), 0) == CH - 1
    ones = jnp.ones((CH, LANES), f32)
    rows = range(proj.shape[1])
    units = range(len(rows) * heads)
    row_of = [u // heads for u in units]
    head_of = [u % heads for u in units]
    masks = [position_masks(reset_ref[r], chunk) for r in rows]
    conv = []
    for r in rows:
        ext[r, 0:8, :] = tail[0, r, 0].astype(bf16).astype(f32)
        ext[r, 8:, :] = proj[0, r, 0].astype(bf16).astype(f32)
        conv.append(conv_taps(ext, r, conv_w, masks[r][5]))
    sig = [jax.nn.sigmoid(c) for c in conv]
    active = [c * g for c, g in zip(conv, sig)]
    gated = [gates(small_ref[0, r, 0], aux) for r in rows]
    beta_all = [g[0] for g in gated]
    decay = [g[1] for g in gated]
    shifted = [g[2] for g in gated]
    total = [running(d) for d in decay]
    total_rows = [as_rows(t) for t in total]
    parts = [head_parts(active[row_of[u]], head_of[u], heads) for u in units]
    a_q, a_k, v = ([p[i] for p in parts] for i in range(3))
    q_scale = [unit(a) for a in a_q]
    k_scale = [unit(a) for a in a_k]
    q = [a_q[u] * (q_scale[u] * DK**-0.5) for u in units]
    k = [a_k[u] * k_scale[u] for u in units]
    beta = [beta_all[row_of[u]][:, head_of[u] : head_of[u] + 1] for u in units]
    terms = [
        decay_terms(total[row_of[u]], total_rows[row_of[u]], head_of[u], heads, masks[row_of[u]]) for u in units
    ]
    ratios, start_fade, start_last, end_fade = ([t[i] for t in terms] for i in range(4))
    both = [jnp.concatenate([q[u], k[u]], axis=0) for u in units]
    pair = [fine(both[u], k[u], (1, 1)) for u in units]
    key_key = [p[CH:] for p in pair]
    query_key = [p[:CH] for p in pair]
    old = [state_ref[0, u] for u in units]
    inv = [inv_ref[0, u] for u in units]
    delta = [delta_ref[0, u] for u in units]
    do = [d_out[0, row_of[u], 0, :, head_of[u] * DV : (head_of[u] + 1) * DV] for u in units]
    ds = [d_state[u] for u in units]
    read = [coarse(both[u], old[u]) for u in units]
    readings = [ratios[u] * query_key[u] for u in units]
    faded = [end_fade[u] * k[u] for u in units]
    back_read = [coarse(readings[u], do[u], (0, 0)) for u in units]
    back_state = [coarse(faded[u], ds[u]) for u in units]
    d_right = [coarse(inv[u], back_read[u] + back_state[u], (0, 0)) for u in units]
    d_pair = [coarse(jnp.concatenate([do[u], d_right[u]], axis=0), delta[u], (1, 1)) for u in units]
    d_faded = [coarse(delta[u], ds[u], (1, 1)) for u in units]
    d_read = [
        jnp.concatenate([start_fade[u] * do[u], -(beta[u] * start_fade[u]) * d_right[u]], axis=0) for u in units
    ]
    grown = [coarse(both[u], d_read[u], (0, 0)) for u in units]
    d_both = [coarse(d_read[u], old[u], (1, 1)) for u in units]
    for u in units:
        d_state[u] = start_last[u] * ds[u] + grown[u]
    d_v = [beta[u] * d_right[u] for u in units]
    d_read_pair = [d_pair[u][:CH] * ratios[u] for u in units]
    d_sys = [-d_pair[u][CH:] * (ratios[u] * masks[row_of[u]][1]) for u in units]
    d_key_key = [beta[u] * d_sys[u] for u in units]
    moved = [d_key_key[u] * key_key[u] + d_read_pair[u] * query_key[u] for u in units]
    moved_cols = [fine(m, ones, (0, 0))[:, 0:1] for m in moved]
    q_more = [coarse(d_read_pair[u], k[u]) for u in units]
    k_more = [coarse(jnp.concatenate([d_read_pair[u], d_key_key[u]], axis=0), both[u], (0, 0)) for u in units]
    k_most = [coarse(d_key_key[u], k[u]) for u in units]
    d_beta_all = [jnp.zeros((CH, LANES), f32) for _ in rows]
    d_total = [jnp.zeros((CH, LANES), f32) for _ in rows]
    d_active = []
    for u in units:
        r, head = row_of[u], head_of[u]
        recall = read[u][CH:]
        d_beta = jnp.sum(d_right[u] * (v[u] - start_fade[u] * recall), axis=-1, keepdims=True) + jnp.sum(
            d_sys[u] * key_key[u], axis=-1, keepdims=True
        )
        d_start = jnp.sum(do[u] * read[u][:CH], axis=-1, keepdims=True) - beta[u] * jnp.sum(
            d_right[u] * recall, axis=-1, keepdims=True
        )
        d_end = jnp.sum(d_faded[u] * k[u], axis=-1, keepdims=True) * end_fade[u]
        d_last = jnp.sum(d_end, axis=0, keepdims=True) + start_last[u] * jnp.sum(
            jnp.sum(ds[u] * old[u], axis=-1, keepdims=True), axis=0, keepdims=True
        )
        d_col = (
            jnp.sum(moved[u], axis=-1, keepdims=True)
            - moved_cols[u]
            + d_start * start_fade[u]
            - d_end
            + jnp.where(last_row, d_last, 0.0)
        )
        d_q = d_both[u][:CH] + q_more[u]
        d_k = d_both[u][CH:] + k_more[u] + k_most[u] + end_fade[u] * d_faded[u]
        d_aq = (q_scale[u] * DK**-0.5) * (
            d_q - a_q[u] * (q_scale[u] * q_scale[u] * jnp.sum(a_q[u] * d_q, axis=-1, keepdims=True))
        )
        d_ak = k_scale[u] * (
            d_k - a_k[u] * (k_scale[u] * k_scale[u] * jnp.sum(a_k[u] * d_k, axis=-1, keepdims=True))
        )
        d_active.append((d_aq, d_ak, d_v[u]))
        d_beta_all[r] = jnp.where(lane_ids == head, d_beta, d_beta_all[r])
        d_total[r] = jnp.where(lane_ids == heads + head, d_col, d_total[r])
    d_decay = [running(d, reverse=True) for d in d_total]
    for r in rows:
        taps = masks[r][5]
        d_shift = d_decay[r] * (-aux[0:1]) * jax.nn.sigmoid(shifted[r])
        d_small_ref[0, r, 0] = (d_beta_all[r] * beta_all[r] * (1.0 - beta_all[r]) + d_shift).astype(bf16)
        g_decay[0:1, :] += jnp.sum(d_decay[r] * decay[r], axis=0, keepdims=True)
        g_decay[1:2, :] += jnp.sum(d_shift, axis=0, keepdims=True)
        own = d_active[r * heads : (r + 1) * heads]
        d_act = jnp.concatenate([own[h][i] for i in range(3) for h in range(heads)], axis=1)
        d_conv = d_act * (sig[r] * (1.0 + conv[r] * (1.0 - sig[r])))
        d_in = None
        for j in range(TAPS):
            masked = d_conv * taps[j]
            g_conv[j : j + 1, :] += jnp.sum(
                masked * ext[r, 8 - (TAPS - 1) + j : 8 - (TAPS - 1) + j + CH, :], axis=0, keepdims=True
            )
            dext[r, j, 0:CH, :] = masked
            shift = TAPS - 1 - j
            part = conv_w[j : j + 1] * dext[r, j, shift : shift + CH, :]
            d_in = part if d_in is None else d_in + part
            dext[r, j, CH : CH + 8, :] = masked[0:8]
        d_proj[0, r, 0] = d_in.astype(bf16)


def params():
    return pltpu.CompilerParams(dimension_semantics=("arbitrary",), vmem_limit_bytes=VMEM_BYTES)


def whole(array):
    return pl.BlockSpec(array.shape, lambda c, pos, rst: (0,) * array.ndim)


SMALL_COST = pl.CostEstimate(flops=1_000_000, bytes_accessed=1_000, transcendentals=0)


def slot_spec(rows_n, width, chunk_of):
    return pl.BlockSpec(
        (1, rows_n, 1, CH, width), lambda c, pos, rst: (pos[chunk_of(c)] & 1, 0, pos[chunk_of(c)] >> 1, 0, 0)
    )


def prepare_kernel(
    heads, pos_ref, reset_ref, first, second, tail, small_a, small_b, conv_w_ref, aux_ref, *outs_and_scratch
):
    both_out, value_out, inv_out, read_out, cols_out, ext = outs_and_scratch
    step = pl.program_id(0)
    conv_w = conv_w_ref[...]
    aux = aux_ref[...]
    lane_ids = lax.broadcasted_iota(jnp.int32, (CH, LANES), 1)
    systems = []
    for row in range(first.shape[1]):
        ext[row, 0:8, :] = jnp.where(step > 0, tail[0, row, 0].astype(bf16).astype(f32), 0.0)
        ext[row, 8 : 8 + CH, :] = first[0, row, 0].astype(bf16).astype(f32)
        ext[row, 8 + CH :, :] = second[0, row, 0].astype(bf16).astype(f32)
        for which, small_ref in enumerate((small_a, small_b)):
            masks = position_masks(reset_ref[row], 2 * step + which)
            conv = None
            for j in range(TAPS):
                at = which * CH + 8 - (TAPS - 1) + j
                part = conv_w[j : j + 1] * (ext[row, at : at + CH, :] * masks[5][j])
                conv = part if conv is None else conv + part
            active = conv * jax.nn.sigmoid(conv)
            beta_all, decay, _ = gates(small_ref[0, row, 0], aux)
            total = running(decay)
            total_rows = as_rows(total)
            for head in range(heads):
                at = row * heads + head
                q, k, v = head_parts(active, head, heads)
                q = q * (unit(q) * DK**-0.5)
                k = k * unit(k)
                beta = beta_all[:, head : head + 1]
                ratios, start_fade, start_last, end_fade = decay_terms(total, total_rows, head, heads, masks)
                both = jnp.concatenate([q, k], axis=0)
                pair = fine(both, k, (1, 1))
                both_out[which, at] = both
                value_out[which, at] = v
                systems.append((which, at, beta * (ratios * masks[1] * pair[CH:])))
                read_out[which, at] = ratios * pair[:CH]
                cols_out[which, at] = jnp.where(
                    lane_ids == 0,
                    beta,
                    jnp.where(lane_ids == 1, start_fade, jnp.where(lane_ids == 2, end_fade, start_last)),
                )
    for (which, at, _), inv in zip(systems, inverses_unit_lower([part for _, _, part in systems])):
        inv_out[which, at] = inv


def scan_kernel(heads, pos_ref, both_ref, value_ref, inv_ref, read_ref, cols_ref, outs, state_out, delta_out, state):
    @pl.when(pl.program_id(0) == 0)
    def _():
        state[...] = jnp.zeros_like(state)

    state_out[0] = state[...]
    units = range(state.shape[0])
    old = [state[u] for u in units]
    beta = [cols_ref[0, u, :, 0:1] for u in units]
    start_fade = [cols_ref[0, u, :, 1:2] for u in units]
    end_fade = [cols_ref[0, u, :, 2:3] for u in units]
    start_last = [cols_ref[0, u, 0:1, 3:4] for u in units]
    read = [coarse(both_ref[0, u], old[u]) for u in units]
    right = [beta[u] * (value_ref[0, u] - start_fade[u] * read[u][CH:]) for u in units]
    delta = [coarse(inv_ref[0, u], right[u]) for u in units]
    grown = [coarse(end_fade[u] * both_ref[0, u, CH:, :], delta[u], (0, 0)) for u in units]
    local = [coarse(read_ref[0, u], delta[u]) for u in units]
    for u in units:
        row, head = divmod(u, heads)
        state[u] = start_last[u] * old[u] + grown[u]
        outs[0, row, 0, :, head * DV : (head + 1) * DV] = start_fade[u] * read[u][:CH] + local[u]
        delta_out[0, u] = delta[u]


def mixer_prepare(proj, small, pos, resets, conv_w, aux):
    _, rows_n, half, _, _ = proj.shape
    width = conv_w.shape[1]
    chunks = 2 * half
    heads = width // (2 * DK + DV)
    units = rows_n * heads
    tail = pl.BlockSpec(
        (1, rows_n, 1, 8, width),
        lambda i, pos, rst: (
            pos[jnp.maximum(2 * i - 1, 0)] & 1,
            0,
            pos[jnp.maximum(2 * i - 1, 0)] >> 1,
            CH // 8 - 1,
            0,
        ),
    )
    even = lambda w: slot_spec(rows_n, w, lambda i: 2 * i)
    odd = lambda w: slot_spec(rows_n, w, lambda i: 2 * i + 1)
    shapes = ((2 * CH, DK), (CH, DV), (CH, CH), (CH, CH), (CH, LANES))
    return pl.pallas_call(
        partial(prepare_kernel, heads),
        grid_spec=pltpu.PrefetchScalarGridSpec(
            num_scalar_prefetch=2,
            grid=(half,),
            in_specs=[even(width), odd(width), tail, even(LANES), odd(LANES), whole(conv_w), whole(aux)],
            out_specs=[pl.BlockSpec((2, units) + s, lambda i, pos, rst: (i, 0, 0, 0)) for s in shapes],
            scratch_shapes=[pltpu.VMEM((rows_n, 2 * CH + 8, width), f32)],
        ),
        out_shape=[jax.ShapeDtypeStruct((chunks, units) + s, f32) for s in shapes],
        cost_estimate=KERNEL_COST,
        compiler_params=params(),
        name="delta_prepare",
    )(pos, resets, proj, proj, proj, small, small, conv_w, aux)


def mixer_scan(prepared, pos, rows_n):
    chunks, units = prepared[0].shape[:2]
    heads = units // rows_n
    kept = lambda *s: pl.BlockSpec((1, units) + s, lambda c, pos: (c, 0, 0, 0))
    mixed, states, deltas = pl.pallas_call(
        partial(scan_kernel, heads),
        grid_spec=pltpu.PrefetchScalarGridSpec(
            num_scalar_prefetch=1,
            grid=(chunks,),
            in_specs=[kept(*p.shape[2:]) for p in prepared],
            out_specs=[
                pl.BlockSpec(
                    (1, rows_n, 1, CH, heads * DV), lambda c, pos: (pos[c] & 1, 0, pos[c] >> 1, 0, 0)
                ),
                kept(DK, DV),
                kept(CH, DV),
            ],
            scratch_shapes=[pltpu.VMEM((units, DK, DV), f32)],
        ),
        out_shape=[
            jax.ShapeDtypeStruct((2, rows_n, chunks // 2, CH, heads * DV), f32),
            jax.ShapeDtypeStruct((chunks, units, DK, DV), f32),
            jax.ShapeDtypeStruct((chunks, units, CH, DV), f32),
        ],
        cost_estimate=SMALL_COST,
        compiler_params=params(),
        name="delta_scan",
    )(pos, *prepared)
    return mixed, states, prepared[2], deltas


def mixer_backward(proj, small, d_out, pos, resets, conv_w, aux, states, invs, deltas):
    _, rows_n, half, _, _ = proj.shape
    width = conv_w.shape[1]
    chunks = 2 * half
    heads = width // (2 * DK + DV)
    units = rows_n * heads
    back = lambda c: chunks - 1 - c
    before = lambda c: jnp.maximum(back(c) - 1, 0)
    spec = lambda w: slot_spec(rows_n, w, back)
    tail = pl.BlockSpec(
        (1, rows_n, 1, 8, width),
        lambda c, pos, rst: (pos[before(c)] & 1, 0, pos[before(c)] >> 1, CH // 8 - 1, 0),
    )
    kept = lambda *s: pl.BlockSpec((1, units) + s, lambda c, pos, rst: (back(c), 0, 0, 0))
    return pl.pallas_call(
        partial(backward_kernel, heads, chunks),
        grid_spec=pltpu.PrefetchScalarGridSpec(
            num_scalar_prefetch=2,
            grid=(chunks,),
            in_specs=[spec(width), spec(LANES), tail, spec(heads * DV), whole(conv_w), whole(aux)]
            + [kept(DK, DV), kept(CH, CH), kept(CH, DV)],
            out_specs=[
                spec(width),
                spec(LANES),
                pl.BlockSpec((8, width), lambda c, pos, rst: (0, 0)),
                pl.BlockSpec((8, LANES), lambda c, pos, rst: (0, 0)),
            ],
            scratch_shapes=[
                pltpu.VMEM((rows_n, CH + 8, width), f32),
                pltpu.VMEM((rows_n, TAPS, CH + 8, width), f32),
                pltpu.VMEM((units, DK, DV), f32),
            ],
        ),
        out_shape=[
            jax.ShapeDtypeStruct((2, rows_n, half, CH, width), bf16),
            jax.ShapeDtypeStruct((2, rows_n, half, CH, LANES), bf16),
            jax.ShapeDtypeStruct((8, width), f32),
            jax.ShapeDtypeStruct((8, LANES), f32),
        ],
        cost_estimate=KERNEL_COST,
        compiler_params=params(),
        name="delta_backward",
    )(pos, resets, proj, small, proj, d_out, conv_w, aux, states, invs, deltas)


def local_call(body, name, inputs, specs, outs, bytes_accessed=0):
    return pl.pallas_call(
        body,
        grid=(1,),
        in_specs=specs,
        out_specs=whole_specs(outs),
        out_shape=outs,
        cost_estimate=SMALL_COST,
        compiler_params=pltpu.CompilerParams(vmem_limit_bytes=VMEM_BYTES),
        name=name,
    )(*inputs)


def term_specs(terms):
    kept, got, steps = terms
    rows_n = kept.shape[0]
    first = pl.BlockSpec((rows_n, 1) + kept.shape[2:], lambda i: (0, 0, 0, 0))
    flat = [step for row in steps for step in row]
    return [kept, got] + flat, [first, first] + [pl.BlockSpec((1,) + s.shape[1:], lambda i: (0, 0, 0)) for s in flat]


def row_total(refs, row, rows_n):
    kept, got = refs[0], refs[1]
    each = (len(refs) - 2) // rows_n
    total = kept[row, 0].astype(f32) + got[row, 0].astype(f32)
    for step in refs[2 + row * each : 2 + (row + 1) * each]:
        total = total + step[0].astype(f32)
    return total


def in_order(values, groups):
    size, batches = groups
    own = values.shape[-1] // (size * batches)
    return jnp.concatenate(
        [
            values[:, (b * size + s) * own : (b * size + s + 1) * own]
            for s in range(size)
            for b in range(batches)
        ],
        axis=1,
    )


def whole_specs(arrays):
    zeros = lambda n: lambda i: (0,) * n
    return [pl.BlockSpec(a.shape, zeros(len(a.shape))) for a in arrays]


def add_and_norm(terms, base, gain):
    inputs, specs = term_specs(terms)
    rows_n, _, span, _ = terms[0].shape

    def body(*refs):
        base_ref, gain_ref, out_ref, norm_ref = refs[len(inputs) :]
        for row in range(rows_n):
            at = pl.ds(row * span, span)
            total = base_ref[at, :].astype(f32) + row_total(refs[: len(inputs)], row, rows_n)
            scale = lax.rsqrt(jnp.mean(total * total, axis=-1, keepdims=True) + EPS_NORM)
            out_ref[at, :] = total
            norm_ref[row] = (total * scale * gain_ref[...]).astype(bf16)

    extra = [base, gain.reshape(1, D)]
    return local_call(
        body,
        "add_and_norm",
        inputs + extra,
        specs + whole_specs(extra),
        [jax.ShapeDtypeStruct((rows_n * span, D), f32), jax.ShapeDtypeStruct((rows_n, span, D), bf16)],
        4_000_000,
    )


def norm_back(terms, base, through, gain, out_dtype, groups=None):
    inputs, specs = term_specs(terms)
    rows_n, _, span, _ = terms[0].shape
    with_rows = groups is None

    def body(*refs):
        base_ref, through_ref, gain_ref = refs[len(inputs) : len(inputs) + 3]
        outs = refs[len(inputs) + 3 :]
        g_gain = jnp.zeros((1, D), f32)
        for row in range(rows_n):
            at = pl.ds(row * span, span)
            d_norm = row_total(refs[: len(inputs)], row, rows_n)
            x = base_ref[at, :].astype(f32)
            scale = lax.rsqrt(jnp.mean(x * x, axis=-1, keepdims=True) + EPS_NORM)
            e = d_norm * gain_ref[...]
            lean = jnp.mean(e * x, axis=-1, keepdims=True)
            total = through_ref[at, :].astype(f32) + scale * e - x * (scale * scale * scale * lean)
            g_gain = g_gain + jnp.sum(d_norm * x * scale, axis=0, keepdims=True)
            if with_rows:
                outs[0][at, :] = total.astype(out_dtype)
                outs[1][row] = total.astype(bf16)
            else:
                outs[0][at, :] = in_order(total, groups).astype(out_dtype)
        outs[-1][...] = g_gain

    extra = [base, through, gain.reshape(1, D)]
    outs = [jax.ShapeDtypeStruct((rows_n * span, D), out_dtype)]
    if with_rows:
        outs.append(jax.ShapeDtypeStruct((rows_n, span, D), bf16))
    return local_call(
        body,
        "norm_back",
        inputs + extra,
        specs + whole_specs(extra),
        outs + [jax.ShapeDtypeStruct((1, D), f32)],
        4_000_000,
    )


def add_in_order(terms, base, groups):
    inputs, specs = term_specs(terms)
    rows_n, _, span, _ = terms[0].shape

    def body(*refs):
        base_ref, out_ref = refs[len(inputs) :]
        for row in range(rows_n):
            at = pl.ds(row * span, span)
            total = base_ref[at, :] + row_total(refs[: len(inputs)], row, rows_n)
            out_ref[at, :] = in_order(total, groups).astype(bf16)

    return local_call(
        body,
        "add_in_order",
        inputs + [base],
        specs + whole_specs([base]),
        [jax.ShapeDtypeStruct((rows_n * span, D), bf16)],
        3_000_000,
    )[0]


ROW_BLOCK = 256


def gated_norm(mixed, proj, gain):
    rows_n, width = mixed.shape
    gate_block = pl.BlockSpec((ROW_BLOCK, width), lambda i: (i, proj.shape[1] // width - 1))

    def body(mixed_ref, gate_ref, gain_ref, out_ref):
        for at in range(0, width, DV):
            x = mixed_ref[:, at : at + DV]
            g = gate_ref[:, at : at + DV]
            scale = lax.rsqrt(jnp.mean(x * x, axis=-1, keepdims=True) + EPS_HEAD)
            out_ref[:, at : at + DV] = (x * scale * gain_ref[...] * (g * jax.nn.sigmoid(g))).astype(bf16)

    block = pl.BlockSpec((ROW_BLOCK, width), lambda i: (i, 0))
    return pl.pallas_call(
        body,
        grid=(rows_n // ROW_BLOCK,),
        in_specs=[block, gate_block, pl.BlockSpec((1, DV), lambda i: (0, 0))],
        out_specs=block,
        out_shape=jax.ShapeDtypeStruct((rows_n, width), bf16),
        cost_estimate=SMALL_COST,
        compiler_params=params(),
        name="gated_norm",
    )(mixed, proj, gain.reshape(1, DV))


def gated_norm_back(mixed, proj, gain, d_out):
    rows_n, width = mixed.shape
    gate_block = pl.BlockSpec((ROW_BLOCK, width), lambda i: (i, proj.shape[1] // width - 1))

    def body(mixed_ref, gate_ref, gain_ref, d_ref, d_mixed_ref, d_gate_ref, g_gain_ref):
        @pl.when(pl.program_id(0) == 0)
        def _():
            g_gain_ref[...] = jnp.zeros_like(g_gain_ref)

        g_gain = jnp.zeros((1, DV), f32)
        for at in range(0, width, DV):
            x = mixed_ref[:, at : at + DV]
            g = gate_ref[:, at : at + DV]
            d = d_ref[:, at : at + DV]
            scale = lax.rsqrt(jnp.mean(x * x, axis=-1, keepdims=True) + EPS_HEAD)
            sig = jax.nn.sigmoid(g)
            through = d * (g * sig)
            unit_x = x * scale
            e = through * gain_ref[...]
            lean = jnp.mean(e * unit_x, axis=-1, keepdims=True)
            d_mixed_ref[:, at : at + DV] = scale * (e - unit_x * lean)
            d_gate_ref[:, at : at + DV] = (
                d * (unit_x * gain_ref[...]) * (sig * (1.0 + g * (1.0 - sig)))
            ).astype(bf16)
            g_gain = g_gain + jnp.sum(through * unit_x, axis=0, keepdims=True)
        g_gain_ref[0:1, :] += g_gain

    block = pl.BlockSpec((ROW_BLOCK, width), lambda i: (i, 0))
    return pl.pallas_call(
        body,
        grid=(rows_n // ROW_BLOCK,),
        in_specs=[block, gate_block, pl.BlockSpec((1, DV), lambda i: (0, 0)), block],
        out_specs=[block, block, pl.BlockSpec((8, DV), lambda i: (0, 0))],
        out_shape=[
            jax.ShapeDtypeStruct((rows_n, width), f32),
            jax.ShapeDtypeStruct((rows_n, width), bf16),
            jax.ShapeDtypeStruct((8, DV), f32),
        ],
        cost_estimate=SMALL_COST,
        compiler_params=params(),
        name="gated_norm_back",
    )(mixed, proj, gain.reshape(1, DV), d_out)


def laid_out(blocks, pieces, total):
    size, rows_n, _ = blocks[0].shape

    def body(*refs):
        out_ref = refs[-1]
        for which, first, width, start in pieces:
            for s in range(size):
                out_ref[:, start + s * width : start + (s + 1) * width] = refs[which][
                    s, :, first : first + width
                ].astype(f32)

    return local_call(
        body, "laid_out", blocks, whole_specs(blocks), [jax.ShapeDtypeStruct((rows_n, total), f32)], 5_000_000
    )[0]


def swap(value, axis, bit):
    return lax.ppermute(value, axis, [(i, i ^ bit) for i in range(lax.axis_size(axis))])


def routes(axis):
    bits = [1 << i for i in range(lax.axis_size(axis).bit_length() - 1)]
    return [bits[1:] + bits[:1], bits[:0:-1] + bits[:1]]


def gather_rows(rows, axis, ordered=True, earlier=None):
    laid = []
    for row, order in zip(rows, routes(axis) * rows.shape[0]):
        held = row[None]
        names = [0]
        parts = []
        for i, bit in enumerate(order[:-1]):
            got = swap(held, axis, bit)
            names = names + [n ^ (bit >> 1) for n in names]
            if i < len(order) - 2:
                held = jnp.concatenate([held, got], axis=0)
            else:
                parts = [held, got]
        if ordered and names != sorted(names):
            place = {name: i for i, name in enumerate(names)}
            size = len(names) // 2
            for n in sorted(names):
                which, at = divmod(place[n], size)
                laid.append(parts[which][at : at + 1])
        else:
            laid.extend(parts)
    even = jnp.concatenate(laid, axis=0).reshape((rows.shape[0], -1) + rows.shape[1:])
    if earlier is not None:
        even, earlier = lax.optimization_barrier((even, earlier))
        return even, swap(even, axis, 1), earlier
    return even, swap(even, axis, 1)


def scatter_rows(keep, send, axis, ordered=True, earlier=()):
    got = after(swap(send, axis, 1), *earlier)
    rows_n, half, span, width = keep.shape
    depth = half.bit_length() - 1
    steps = []
    for row, order in zip(range(rows_n), routes(axis) * rows_n):
        bits = order[:-1]
        axes = sorted(bits, reverse=True) if ordered else bits[::-1]
        shape = (2,) * depth + (span, width)
        terms = [keep[row].reshape(shape), got[row].reshape(shape)]
        mine = []
        for bit in bits[::-1]:
            at = axes.index(bit)
            sent = sum(lax.index_in_dim(t, 1, at, keepdims=False).astype(f32) for t in terms).astype(bf16)
            back = swap(sent, axis, bit)
            terms = [lax.index_in_dim(t, 0, at, keepdims=False) for t in terms] + [back]
            axes = [b for b in axes if b != bit]
            mine.append(back.reshape((-1, span, width)))
        steps.append(mine)
    return keep, got, steps


def joined(halves):
    return jnp.concatenate([h.reshape(-1, h.shape[-1]) for h in halves], axis=0)


def after(value, *earlier):
    return lax.optimization_barrier((value,) + earlier)[0]


def sum_all(value, axes):
    for axis in axes:
        for i in range(lax.axis_size(axis).bit_length() - 1):
            value = value + swap(value, axis, 1 << i)
    return value


def gather_small(value, axis):
    held = value[None]
    size = lax.axis_size(axis)
    for i in range(size.bit_length() - 1):
        held = jnp.concatenate([held, swap(held, axis, 1 << i)], axis=0)
    return held[jnp.arange(size, dtype=jnp.int32) ^ lax.axis_index(axis).astype(jnp.int32)]


def mm(left, right):
    return jnp.dot(left, right, preferred_element_type=f32)


def contract_rows(left, right):
    return lax.dot_general(left, right, (((0,), (0,)), ((), ())), preferred_element_type=f32)


def contract_cols(left, right):
    return lax.dot_general(left, right, (((1,), (1,)), ((), ())), preferred_element_type=f32)


def rms_scale(values, scale_gain):
    return values * lax.rsqrt(jnp.mean(values * values, axis=-1, keepdims=True) + EPS_NORM) * scale_gain


def glu_hidden(gate_half, up_half):
    return jax.nn.silu(gate_half) * up_half


def exchanged(packed):
    return lax.all_to_all(packed, "seq", split_axis=0, concat_axis=0, tiled=True)


def stacked(blocks):
    full = lax.all_gather(blocks, "batch", axis=0, tiled=False)
    return full.reshape(-1, blocks.shape[-1])


def summed(partial_grad):
    own = lax.psum_scatter(partial_grad, "batch", scatter_dimension=0, tiled=True)
    return own.reshape(lax.axis_size("seq"), -1, own.shape[-1])


def shards(
    tokens,
    grad_out,
    resets,
    w_proj,
    w_small,
    w_out,
    w_gu,
    w_down,
    norm_in,
    norm_ff,
    norm_head,
    conv_w,
    a_log,
    dt_bias,
):
    size = lax.axis_size("seq")
    groups = lax.axis_size("batch")
    me = lax.axis_index("seq")
    batch_rows, span_len, _ = tokens.shape
    own_rows = w_proj.shape[0]
    heads = H // size
    ff = FF // size
    key_w, val_w = heads * DK, heads * DV
    conv_cols = 2 * key_w + val_w
    half = batch_rows * size // 2 * span_len
    halves = (batch_rows, size // 2, span_len)
    blocks = (2,) + halves

    def shuffled(array):
        lead = array.shape[:-1]
        return array.reshape(lead + (size, groups, own_rows)).swapaxes(-3, -2).reshape(lead + (D,))

    def restored(array):
        lead = array.shape[:-1]
        return array.reshape(lead + (groups, size, own_rows)).swapaxes(-3, -2).reshape(lead + (D,))

    out_w = lax.all_gather(w_out, "batch", axis=0, tiled=True)
    packed_mix = jnp.concatenate(
        [
            w_proj[:, :KW].reshape(own_rows, size, key_w),
            w_proj[:, KW : 2 * KW].reshape(own_rows, size, key_w),
            w_proj[:, 2 * KW : CW].reshape(own_rows, size, val_w),
            w_proj[:, CW:].reshape(own_rows, size, val_w),
        ],
        axis=-1,
    ).transpose(1, 0, 2)
    moved_mix = exchanged(packed_mix)
    own_in = shuffled(tokens).reshape(-1, D)
    gain_in, gain_ff = shuffled(norm_in), shuffled(norm_ff)
    h_in = joined(gather_rows(rms_scale(own_in.astype(f32), gain_in).astype(bf16).reshape(tokens.shape), "seq"))
    mix_w = stacked(after(moved_mix, out_w, h_in))
    packed_gu, w_small, d_own, own_down = after(
        (
            w_gu.reshape(own_rows, 2, size, ff).transpose(2, 0, 1, 3).reshape(size, own_rows, 2 * ff),
            w_small,
            shuffled(grad_out),
            shuffled(w_down),
        ),
        moved_mix,
    )
    d_halves = gather_rows(d_own, "seq", False)
    small_all = gather_small(gather_small(w_small, "seq"), "batch").reshape(D, 2 * H)
    small_w = jnp.pad(
        jnp.concatenate(
            [
                lax.dynamic_slice_in_dim(small_all, me * heads, heads, 1),
                lax.dynamic_slice_in_dim(small_all, H + me * heads, heads, 1),
            ],
            axis=1,
        ),
        ((0, 0), (0, LANES - 2 * heads)),
    )
    out_w = shuffled(out_w)
    moved_gu = exchanged(packed_gu)

    slots = jnp.arange(size, dtype=jnp.int32) ^ me.astype(jnp.int32)
    conv_l = jnp.concatenate(
        [
            lax.dynamic_slice_in_dim(conv_w, me * key_w, key_w, 1),
            lax.dynamic_slice_in_dim(conv_w, KW + me * key_w, key_w, 1),
            lax.dynamic_slice_in_dim(conv_w, 2 * KW + me * val_w, val_w, 1),
        ],
        axis=1,
    )
    at_heads = (heads, LANES - 2 * heads)
    aux = jnp.pad(
        jnp.stack(
            [
                lax.dynamic_slice_in_dim(jnp.exp(a_log), me * heads, heads),
                lax.dynamic_slice_in_dim(dt_bias, me * heads, heads),
            ]
        ),
        ((0, 6), at_heads),
    )

    small = mm(h_in, small_w).reshape(blocks + (LANES,))
    proj = mm(h_in, mix_w)
    down_first = lax.all_gather(own_down[:, : D // 2], "batch", axis=0, tiled=True)
    prepared = mixer_prepare(proj.reshape(blocks + (-1,)), small, slots, resets, conv_l, aux)
    prepared, moved_gu, down_first = lax.optimization_barrier((prepared, moved_gu, down_first))
    down_rest = lax.all_gather(own_down[:, D // 2 :], "batch", axis=0, tiled=True)
    gu_w = stacked(moved_gu)
    mixed, states, invs, deltas = mixer_scan(prepared, slots, batch_rows)
    mixed = mixed.reshape(-1, val_w)
    z_rows = gated_norm(mixed, proj, norm_head)

    def parts(product, left):
        send = product(left[half:]).astype(bf16).reshape(halves + (D,))
        return product(left[:half]).astype(bf16).reshape(halves + (D,)), send

    keep, send = parts(lambda rows: mm(rows, out_w), z_rows)
    d_out = joined(after(d_halves, keep, send))
    residual, normed_ff = add_and_norm(scatter_rows(keep, send, "seq"), own_in, gain_ff)

    even, odd, gu_w = gather_rows(normed_ff, "seq", False, gu_w)
    h_ff = joined((even, odd))
    gate_up = mm(h_ff, gu_w)
    hidden_full, pull_glu = jax.vjp(glu_hidden, gate_up[:, :ff], gate_up[:, ff:])
    hidden = hidden_full.astype(bf16)
    down_grad = contract_rows(d_out, hidden).astype(bf16)
    hidden, down_rest = lax.optimization_barrier((hidden, down_rest))
    down_own = summed(down_grad)
    d_hidden = contract_cols(d_out[:, : D // 2], down_first) + contract_cols(d_out[:, D // 2 :], down_rest)
    down_w = jnp.concatenate([down_first, down_rest], axis=1)
    d_gate_up = jnp.concatenate(pull_glu(d_hidden), axis=1).astype(bf16)
    keep, send = parts(lambda rows: contract_cols(rows, gu_w), d_gate_up)
    terms = scatter_rows(keep, send, "seq", False)
    gu_grad = contract_rows(after(h_ff, keep, send), d_gate_up).astype(bf16)
    gu_own = summed(gu_grad)
    out_parts = parts(lambda rows: mm(rows, down_w), after(hidden, keep, send))
    d_residual, d_branch, g_norm_ff = norm_back(terms, residual, d_own.reshape(-1, D), gain_ff, f32)

    d_branch = joined(gather_rows(after(d_branch, gu_grad, down_own, out_parts), "seq"))
    d_heads = contract_cols(d_branch, out_w)
    d_mixed, d_gate, g_norm_head = gated_norm_back(mixed, proj, norm_head, d_heads)
    out_grad = jnp.concatenate(
        [contract_rows(h_in, d_gate).astype(bf16), contract_rows(d_branch, z_rows).astype(bf16)], axis=1
    )
    d_mixed, out_grad = lax.optimization_barrier((d_mixed, out_grad))
    d_proj, d_small, g_conv_l, g_decay = mixer_backward(
        proj.reshape(blocks + (-1,)), small, d_mixed.reshape(blocks + (val_w,)), slots, resets, conv_l, aux, states, invs, deltas
    )
    d_proj, gu_own = lax.optimization_barrier((d_proj.reshape(-1, conv_cols), gu_own))
    d_small = d_small.reshape(-1, LANES)
    out_own = summed(out_grad)
    mix_grad = contract_rows(h_in, d_proj).astype(bf16)
    mix_moved = lax.all_to_all(
        mix_grad.reshape(groups, size, own_rows, conv_cols), "seq", split_axis=1, concat_axis=1, tiled=True
    )
    d_proj, d_small, g_conv_l, gu_own = after((d_proj, d_small, g_conv_l, gu_own), mix_grad)
    mix_moved, gu_own = lax.optimization_barrier((mix_moved, gu_own))
    mix_grads = lax.psum_scatter(mix_moved, "batch", scatter_dimension=0, tiled=True)[0]
    gu_grads, down_grads = exchanged(gu_own), exchanged(down_own)
    block_out = add_in_order(scatter_rows(*out_parts, "seq", False), residual, (size, groups))
    keep, send = parts(
        lambda rows: contract_cols(rows[:, : conv_cols + val_w], mix_w)
        + contract_cols(rows[:, conv_cols + val_w :], small_w),
        jnp.concatenate([d_proj, d_gate, d_small], axis=1),
    )
    d_tokens, g_norm_in = norm_back(
        scatter_rows(keep, send, "seq"), own_in, after(d_residual, out_own), gain_in, bf16, (size, groups)
    )

    small_grad = contract_rows(d_small, h_in)[: 2 * heads]
    local = jnp.concatenate(
        [g_conv_l[:TAPS].reshape(-1), g_decay[:2, heads : 2 * heads].reshape(-1), small_grad.reshape(-1)]
    )
    shared = gather_small(sum_all(local, ("batch",)), "seq")
    g_conv_all = shared[:, : TAPS * conv_cols].reshape(size, TAPS, conv_cols).transpose(1, 0, 2)
    g_conv = jnp.concatenate(
        [
            g_conv_all[:, :, :key_w].reshape(TAPS, KW),
            g_conv_all[:, :, key_w : 2 * key_w].reshape(TAPS, KW),
            g_conv_all[:, :, 2 * key_w :].reshape(TAPS, VW),
        ],
        axis=1,
    )
    g_alog = shared[:, TAPS * conv_cols : TAPS * conv_cols + heads].reshape(H)
    g_dt = shared[:, TAPS * conv_cols + heads : TAPS * conv_cols + 2 * heads].reshape(H)
    g_small = lax.dynamic_slice_in_dim(
        shared[:, TAPS * conv_cols + 2 * heads :].reshape(size, 2, heads, D),
        (lax.axis_index("batch") * size + me) * own_rows,
        own_rows,
        3,
    )
    g_small = g_small.transpose(3, 1, 0, 2).reshape(own_rows, 2 * H)
    gains = sum_all(jnp.concatenate([g_norm_in[0], g_norm_ff[0], g_norm_head[0]]), ("seq", "batch"))
    gains = jnp.concatenate([restored(gains[: 2 * D].reshape(2, D)).reshape(-1), gains[2 * D :]])

    out_grads = exchanged(out_own)
    g_gu = laid_out([gu_grads], [(0, 0, ff, 0), (0, ff, ff, FF)], 2 * FF)
    g_down = down_grads.astype(f32).transpose(0, 2, 1).reshape(FF, own_rows)
    g_out = out_grads[:, :, val_w:].astype(f32).transpose(0, 2, 1).reshape(VW, own_rows)
    ready = (d_tokens, block_out, out_grads, g_gu, g_down, g_out, gains, g_conv, g_small)
    mix_grads, ready = lax.optimization_barrier((mix_grads, ready))
    d_tokens, block_out, out_grads, g_gu, g_down, g_out, gains, g_conv, g_small = ready
    g_proj = laid_out(
        [mix_grads, out_grads],
        [(0, 0, key_w, 0), (0, key_w, key_w, KW), (0, 2 * key_w, val_w, 2 * KW), (1, 0, val_w, CW)],
        CW + VW,
    )
    return (
        block_out.reshape(tokens.shape),
        d_tokens.reshape(tokens.shape),
        g_proj,
        g_small,
        g_out,
        g_gu,
        g_down,
        gains[:D],
        gains[D : 2 * D],
        gains[2 * D :],
        g_conv,
        g_alog,
        g_dt,
    )


def solution(mesh):
    rows = P(("seq", "batch"), None)
    cols = P(None, ("seq", "batch"))
    act = P("batch", "seq", None)
    in_specs = (act, act, P("batch"), rows, rows, rows, rows, rows) + (P(),) * 6
    out_specs = (act, act, rows, rows, cols, rows, cols) + (P(),) * 6
    return jax.shard_map(shards, mesh=mesh, in_specs=in_specs, out_specs=out_specs, check_vma=False)
```

```python
from functools import partial

import jax
import jax.numpy as jnp
from jax import lax
from jax.experimental import pallas as pl
from jax.experimental.pallas import tpu as pltpu
from jax.sharding import PartitionSpec as P

D = 2048
H = 16
DK = 128
DV = 256
FF = 5632
CH = 64
KW = 2048
VW = 4096
CW = 8192
TAPS = 4
LANES = 128

EPS_NORM = 1e-06
EPS_HEAD = 1e-05
EPS_UNIT = 1e-06
f32 = jnp.float32
bf16 = jnp.bfloat16
VMEM_BYTES = 56 * 1024 * 1024
KERNEL_COST = pl.CostEstimate(flops=30_000_000_000, bytes_accessed=40_000_000, transcendentals=0)


def dot_in(left, right, contract, precision):
    return lax.dot_general(
        left,
        right,
        (((contract[0],), (contract[1],)), ((), ())),
        precision=precision,
        preferred_element_type=f32,
    )


def fine(left, right, contract=(1, 0)):
    return dot_in(left, right, contract, lax.Precision.HIGH)


def coarse(left, right, contract=(1, 0)):
    return dot_in(left, right, contract, lax.Precision.HIGH)


def position_masks(reset, chunk):
    rows = lax.broadcasted_iota(jnp.int32, (CH, CH), 0)
    cols = lax.broadcasted_iota(jnp.int32, (CH, CH), 1)
    time = lax.broadcasted_iota(jnp.int32, (CH, 1), 0)
    offset = reset - chunk * CH
    cut = jnp.where(offset < 0, CH, offset)
    apart = (rows >= cut) & (cols < cut)
    causal = jnp.where((rows >= cols) & ~apart, 1.0, 0.0)
    strict = jnp.where((rows > cols) & ~apart, 1.0, 0.0)
    in_first = jnp.where(time < cut, 1.0, 0.0)
    last_first = jnp.where(CH - 1 < cut, 1.0, 0.0)
    in_last = jnp.where((time >= cut) | (cut > CH - 1), 1.0, 0.0)
    begin = jnp.where(time >= offset, offset, -chunk * CH)
    taps = [jnp.where(time - (TAPS - 1) + j >= begin, 1.0, 0.0) for j in range(TAPS)]
    return causal, strict, in_first, last_first, in_last, taps


def gates(small, aux):
    beta = jax.nn.sigmoid(small)
    shifted = small + aux[1:2]
    soft = jnp.maximum(shifted, 0.0) + jnp.log1p(jnp.exp(-jnp.abs(shifted)))
    return beta, -aux[0:1] * soft, shifted


def running(values, reverse=False):
    rows = lax.broadcasted_iota(jnp.int32, (CH, CH), 0)
    cols = lax.broadcasted_iota(jnp.int32, (CH, CH), 1)
    keep = (cols >= rows) if reverse else (cols <= rows)
    return fine(jnp.where(keep, 1.0, 0.0), values)


def as_rows(total):
    pick_row = lax.broadcasted_iota(jnp.int32, (LANES, LANES), 0)
    pick_col = lax.broadcasted_iota(jnp.int32, (LANES, LANES), 1)
    return fine(jnp.where(pick_row == pick_col, 1.0, 0.0), total, (1, 1))


def inverses_unit_lower(parts):
    size = parts[0].shape[0]
    rows = lax.broadcasted_iota(jnp.int32, (size, size), 0)
    cols = lax.broadcasted_iota(jnp.int32, (size, size), 1)
    eye = jnp.where(rows == cols, 1.0, 0.0)
    block = lambda n: jnp.where((rows & -n) == (cols & -n), 1.0, 0.0)
    inside = {n: block(n) for n in (16, 32, 64)}
    power = [part * inside[16] for part in parts]
    inv = [eye - diag for diag in power]
    for _ in range(3):
        power = [fine(p, p) for p in power]
        more = [fine(i, p) for i, p in zip(inv, power)]
        inv = [i + m for i, m in zip(inv, more)]
    for n in (16, 32):
        ring = inside[2 * n] - inside[n]
        left = [fine(i, part * ring) for i, part in zip(inv, parts)]
        more = [fine(l, i) for l, i in zip(left, inv)]
        inv = [i - m for i, m in zip(inv, more)]
    return inv


def conv_taps(ext_ref, row, conv_w, taps):
    out = None
    for j in range(TAPS):
        part = conv_w[j : j + 1] * (ext_ref[row, 8 - (TAPS - 1) + j : 8 - (TAPS - 1) + j + CH, :] * taps[j])
        out = part if out is None else out + part
    return out


def unit(values):
    return lax.rsqrt(jnp.sum(values * values, axis=-1, keepdims=True) + EPS_UNIT)


def head_parts(active, head, heads):
    q = active[:, head * DK : (head + 1) * DK]
    k = active[:, heads * DK + head * DK : heads * DK + (head + 1) * DK]
    v = active[:, 2 * heads * DK + head * DV : 2 * heads * DK + (head + 1) * DV]
    return q, k, v


def decay_terms(total, total_rows, head, heads, masks):
    causal, strict, in_first, last_first, in_last, _ = masks
    lane = heads + head
    col = total[:, lane : lane + 1]
    row = total_rows[lane : lane + 1, :]
    ratios = jnp.exp(jnp.where(causal > 0, col - row, 0.0)) * causal
    last = col[CH - 1 : CH, :]
    start_fade = jnp.exp(col) * in_first
    start_last = jnp.exp(last) * last_first
    end_fade = jnp.exp(jnp.where(in_last > 0, last - col, 0.0)) * in_last
    return ratios, start_fade, start_last, end_fade


def backward_kernel(
    heads,
    chunks,
    pos_ref,
    reset_ref,
    proj,
    small_ref,
    tail,
    d_out,
    conv_w_ref,
    aux_ref,
    state_ref,
    inv_ref,
    delta_ref,
    d_proj,
    d_small_ref,
    g_conv,
    g_decay,
    ext,
    dext,
    d_state,
):
    step = pl.program_id(0)
    chunk = chunks - 1 - step
    width = heads * (2 * DK + DV)

    @pl.when(step == 0)
    def _():
        dext[...] = jnp.zeros_like(dext)
        d_state[...] = jnp.zeros_like(d_state)
        g_conv[...] = jnp.zeros_like(g_conv)
        g_decay[...] = jnp.zeros_like(g_decay)

    conv_w = conv_w_ref[...]
    aux = aux_ref[...]
    lane_ids = lax.broadcasted_iota(jnp.int32, (CH, LANES), 1)
    last_row = lax.broadcasted_iota(jnp.int32, (CH, 1), 0) == CH - 1
    ones = jnp.ones((CH, LANES), f32)
    rows = range(proj.shape[1])
    units = range(len(rows) * heads)
    row_of = [u // heads for u in units]
    head_of = [u % heads for u in units]
    masks = [position_masks(reset_ref[r], chunk) for r in rows]
    conv = []
    for r in rows:
        ext[r, 0:8, :] = tail[0, r, 0].astype(bf16).astype(f32)
        ext[r, 8:, :] = proj[0, r, 0].astype(bf16).astype(f32)
        conv.append(conv_taps(ext, r, conv_w, masks[r][5]))
    sig = [jax.nn.sigmoid(c) for c in conv]
    active = [c * g for c, g in zip(conv, sig)]
    gated = [gates(small_ref[0, r, 0], aux) for r in rows]
    beta_all = [g[0] for g in gated]
    decay = [g[1] for g in gated]
    shifted = [g[2] for g in gated]
    total = [running(d) for d in decay]
    total_rows = [as_rows(t) for t in total]
    parts = [head_parts(active[row_of[u]], head_of[u], heads) for u in units]
    a_q, a_k, v = ([p[i] for p in parts] for i in range(3))
    q_scale = [unit(a) for a in a_q]
    k_scale = [unit(a) for a in a_k]
    q = [a_q[u] * (q_scale[u] * DK**-0.5) for u in units]
    k = [a_k[u] * k_scale[u] for u in units]
    beta = [beta_all[row_of[u]][:, head_of[u] : head_of[u] + 1] for u in units]
    terms = [
        decay_terms(total[row_of[u]], total_rows[row_of[u]], head_of[u], heads, masks[row_of[u]]) for u in units
    ]
    ratios, start_fade, start_last, end_fade = ([t[i] for t in terms] for i in range(4))
    both = [jnp.concatenate([q[u], k[u]], axis=0) for u in units]
    pair = [fine(both[u], k[u], (1, 1)) for u in units]
    key_key = [p[CH:] for p in pair]
    query_key = [p[:CH] for p in pair]
    old = [state_ref[0, u] for u in units]
    inv = [inv_ref[0, u] for u in units]
    delta = [delta_ref[0, u] for u in units]
    do = [d_out[0, row_of[u], 0, :, head_of[u] * DV : (head_of[u] + 1) * DV] for u in units]
    ds = [d_state[u] for u in units]
    read = [coarse(both[u], old[u]) for u in units]
    readings = [ratios[u] * query_key[u] for u in units]
    faded = [end_fade[u] * k[u] for u in units]
    back_read = [coarse(readings[u], do[u], (0, 0)) for u in units]
    back_state = [coarse(faded[u], ds[u]) for u in units]
    d_right = [coarse(inv[u], back_read[u] + back_state[u], (0, 0)) for u in units]
    d_pair = [coarse(jnp.concatenate([do[u], d_right[u]], axis=0), delta[u], (1, 1)) for u in units]
    d_faded = [coarse(delta[u], ds[u], (1, 1)) for u in units]
    d_read = [
        jnp.concatenate([start_fade[u] * do[u], -(beta[u] * start_fade[u]) * d_right[u]], axis=0) for u in units
    ]
    grown = [coarse(both[u], d_read[u], (0, 0)) for u in units]
    d_both = [coarse(d_read[u], old[u], (1, 1)) for u in units]
    for u in units:
        d_state[u] = start_last[u] * ds[u] + grown[u]
    d_v = [beta[u] * d_right[u] for u in units]
    d_read_pair = [d_pair[u][:CH] * ratios[u] for u in units]
    d_sys = [-d_pair[u][CH:] * (ratios[u] * masks[row_of[u]][1]) for u in units]
    d_key_key = [beta[u] * d_sys[u] for u in units]
    moved = [d_key_key[u] * key_key[u] + d_read_pair[u] * query_key[u] for u in units]
    moved_cols = [fine(m, ones, (0, 0))[:, 0:1] for m in moved]
    q_more = [coarse(d_read_pair[u], k[u]) for u in units]
    k_more = [coarse(jnp.concatenate([d_read_pair[u], d_key_key[u]], axis=0), both[u], (0, 0)) for u in units]
    k_most = [coarse(d_key_key[u], k[u]) for u in units]
    d_beta_all = [jnp.zeros((CH, LANES), f32) for _ in rows]
    d_total = [jnp.zeros((CH, LANES), f32) for _ in rows]
    d_active = []
    for u in units:
        r, head = row_of[u], head_of[u]
        recall = read[u][CH:]
        d_beta = jnp.sum(d_right[u] * (v[u] - start_fade[u] * recall), axis=-1, keepdims=True) + jnp.sum(
            d_sys[u] * key_key[u], axis=-1, keepdims=True
        )
        d_start = jnp.sum(do[u] * read[u][:CH], axis=-1, keepdims=True) - beta[u] * jnp.sum(
            d_right[u] * recall, axis=-1, keepdims=True
        )
        d_end = jnp.sum(d_faded[u] * k[u], axis=-1, keepdims=True) * end_fade[u]
        d_last = jnp.sum(d_end, axis=0, keepdims=True) + start_last[u] * jnp.sum(
            jnp.sum(ds[u] * old[u], axis=-1, keepdims=True), axis=0, keepdims=True
        )
        d_col = (
            jnp.sum(moved[u], axis=-1, keepdims=True)
            - moved_cols[u]
            + d_start * start_fade[u]
            - d_end
            + jnp.where(last_row, d_last, 0.0)
        )
        d_q = d_both[u][:CH] + q_more[u]
        d_k = d_both[u][CH:] + k_more[u] + k_most[u] + end_fade[u] * d_faded[u]
        d_aq = (q_scale[u] * DK**-0.5) * (
            d_q - a_q[u] * (q_scale[u] * q_scale[u] * jnp.sum(a_q[u] * d_q, axis=-1, keepdims=True))
        )
        d_ak = k_scale[u] * (
            d_k - a_k[u] * (k_scale[u] * k_scale[u] * jnp.sum(a_k[u] * d_k, axis=-1, keepdims=True))
        )
        d_active.append((d_aq, d_ak, d_v[u]))
        d_beta_all[r] = jnp.where(lane_ids == head, d_beta, d_beta_all[r])
        d_total[r] = jnp.where(lane_ids == heads + head, d_col, d_total[r])
    d_decay = [running(d, reverse=True) for d in d_total]
    for r in rows:
        taps = masks[r][5]
        d_shift = d_decay[r] * (-aux[0:1]) * jax.nn.sigmoid(shifted[r])
        d_small_ref[0, r, 0] = (d_beta_all[r] * beta_all[r] * (1.0 - beta_all[r]) + d_shift).astype(bf16)
        g_decay[0:1, :] += jnp.sum(d_decay[r] * decay[r], axis=0, keepdims=True)
        g_decay[1:2, :] += jnp.sum(d_shift, axis=0, keepdims=True)
        own = d_active[r * heads : (r + 1) * heads]
        d_act = jnp.concatenate([own[h][i] for i in range(3) for h in range(heads)], axis=1)
        d_conv = d_act * (sig[r] * (1.0 + conv[r] * (1.0 - sig[r])))
        d_in = None
        for j in range(TAPS):
            masked = d_conv * taps[j]
            g_conv[j : j + 1, :] += jnp.sum(
                masked * ext[r, 8 - (TAPS - 1) + j : 8 - (TAPS - 1) + j + CH, :], axis=0, keepdims=True
            )
            dext[r, j, 0:CH, :] = masked
            shift = TAPS - 1 - j
            part = conv_w[j : j + 1] * dext[r, j, shift : shift + CH, :]
            d_in = part if d_in is None else d_in + part
            dext[r, j, CH : CH + 8, :] = masked[0:8]
        d_proj[0, r, 0] = d_in.astype(bf16)


def params():
    return pltpu.CompilerParams(dimension_semantics=("arbitrary",), vmem_limit_bytes=VMEM_BYTES)


def whole(array):
    return pl.BlockSpec(array.shape, lambda c, pos, rst: (0,) * array.ndim)


SMALL_COST = pl.CostEstimate(flops=1_000_000, bytes_accessed=1_000, transcendentals=0)


def slot_spec(rows_n, width, chunk_of):
    return pl.BlockSpec(
        (1, rows_n, 1, CH, width), lambda c, pos, rst: (pos[chunk_of(c)] & 1, 0, pos[chunk_of(c)] >> 1, 0, 0)
    )


def prepare_kernel(
    heads, pos_ref, reset_ref, first, second, tail, small_a, small_b, conv_w_ref, aux_ref, *outs_and_scratch
):
    both_out, value_out, inv_out, read_out, cols_out, ext = outs_and_scratch
    step = pl.program_id(0)
    conv_w = conv_w_ref[...]
    aux = aux_ref[...]
    lane_ids = lax.broadcasted_iota(jnp.int32, (CH, LANES), 1)
    systems = []
    for row in range(first.shape[1]):
        ext[row, 0:8, :] = jnp.where(step > 0, tail[0, row, 0].astype(bf16).astype(f32), 0.0)
        ext[row, 8 : 8 + CH, :] = first[0, row, 0].astype(bf16).astype(f32)
        ext[row, 8 + CH :, :] = second[0, row, 0].astype(bf16).astype(f32)
        for which, small_ref in enumerate((small_a, small_b)):
            masks = position_masks(reset_ref[row], 2 * step + which)
            conv = None
            for j in range(TAPS):
                at = which * CH + 8 - (TAPS - 1) + j
                part = conv_w[j : j + 1] * (ext[row, at : at + CH, :] * masks[5][j])
                conv = part if conv is None else conv + part
            active = conv * jax.nn.sigmoid(conv)
            beta_all, decay, _ = gates(small_ref[0, row, 0], aux)
            total = running(decay)
            total_rows = as_rows(total)
            for head in range(heads):
                at = row * heads + head
                q, k, v = head_parts(active, head, heads)
                q = q * (unit(q) * DK**-0.5)
                k = k * unit(k)
                beta = beta_all[:, head : head + 1]
                ratios, start_fade, start_last, end_fade = decay_terms(total, total_rows, head, heads, masks)
                both = jnp.concatenate([q, k], axis=0)
                pair = fine(both, k, (1, 1))
                both_out[which, at] = both
                value_out[which, at] = v
                systems.append((which, at, beta * (ratios * masks[1] * pair[CH:])))
                read_out[which, at] = ratios * pair[:CH]
                cols_out[which, at] = jnp.where(
                    lane_ids == 0,
                    beta,
                    jnp.where(lane_ids == 1, start_fade, jnp.where(lane_ids == 2, end_fade, start_last)),
                )
    for (which, at, _), inv in zip(systems, inverses_unit_lower([part for _, _, part in systems])):
        inv_out[which, at] = inv


def scan_kernel(heads, pos_ref, both_ref, value_ref, inv_ref, read_ref, cols_ref, outs, state_out, delta_out, state):
    @pl.when(pl.program_id(0) == 0)
    def _():
        state[...] = jnp.zeros_like(state)

    state_out[0] = state[...]
    units = range(state.shape[0])
    old = [state[u] for u in units]
    beta = [cols_ref[0, u, :, 0:1] for u in units]
    start_fade = [cols_ref[0, u, :, 1:2] for u in units]
    end_fade = [cols_ref[0, u, :, 2:3] for u in units]
    start_last = [cols_ref[0, u, 0:1, 3:4] for u in units]
    read = [coarse(both_ref[0, u], old[u]) for u in units]
    right = [beta[u] * (value_ref[0, u] - start_fade[u] * read[u][CH:]) for u in units]
    delta = [coarse(inv_ref[0, u], right[u]) for u in units]
    grown = [coarse(end_fade[u] * both_ref[0, u, CH:, :], delta[u], (0, 0)) for u in units]
    local = [coarse(read_ref[0, u], delta[u]) for u in units]
    for u in units:
        row, head = divmod(u, heads)
        state[u] = start_last[u] * old[u] + grown[u]
        outs[0, row, 0, :, head * DV : (head + 1) * DV] = start_fade[u] * read[u][:CH] + local[u]
        delta_out[0, u] = delta[u]


def mixer_prepare(proj, small, pos, resets, conv_w, aux):
    _, rows_n, half, _, _ = proj.shape
    width = conv_w.shape[1]
    chunks = 2 * half
    heads = width // (2 * DK + DV)
    units = rows_n * heads
    tail = pl.BlockSpec(
        (1, rows_n, 1, 8, width),
        lambda i, pos, rst: (
            pos[jnp.maximum(2 * i - 1, 0)] & 1,
            0,
            pos[jnp.maximum(2 * i - 1, 0)] >> 1,
            CH // 8 - 1,
            0,
        ),
    )
    even = lambda w: slot_spec(rows_n, w, lambda i: 2 * i)
    odd = lambda w: slot_spec(rows_n, w, lambda i: 2 * i + 1)
    shapes = ((2 * CH, DK), (CH, DV), (CH, CH), (CH, CH), (CH, LANES))
    return pl.pallas_call(
        partial(prepare_kernel, heads),
        grid_spec=pltpu.PrefetchScalarGridSpec(
            num_scalar_prefetch=2,
            grid=(half,),
            in_specs=[even(width), odd(width), tail, even(LANES), odd(LANES), whole(conv_w), whole(aux)],
            out_specs=[pl.BlockSpec((2, units) + s, lambda i, pos, rst: (i, 0, 0, 0)) for s in shapes],
            scratch_shapes=[pltpu.VMEM((rows_n, 2 * CH + 8, width), f32)],
        ),
        out_shape=[jax.ShapeDtypeStruct((chunks, units) + s, f32) for s in shapes],
        cost_estimate=KERNEL_COST,
        compiler_params=params(),
        name="delta_prepare",
    )(pos, resets, proj, proj, proj, small, small, conv_w, aux)


def mixer_scan(prepared, pos, rows_n):
    chunks, units = prepared[0].shape[:2]
    heads = units // rows_n
    kept = lambda *s: pl.BlockSpec((1, units) + s, lambda c, pos: (c, 0, 0, 0))
    mixed, states, deltas = pl.pallas_call(
        partial(scan_kernel, heads),
        grid_spec=pltpu.PrefetchScalarGridSpec(
            num_scalar_prefetch=1,
            grid=(chunks,),
            in_specs=[kept(*p.shape[2:]) for p in prepared],
            out_specs=[
                pl.BlockSpec(
                    (1, rows_n, 1, CH, heads * DV), lambda c, pos: (pos[c] & 1, 0, pos[c] >> 1, 0, 0)
                ),
                kept(DK, DV),
                kept(CH, DV),
            ],
            scratch_shapes=[pltpu.VMEM((units, DK, DV), f32)],
        ),
        out_shape=[
            jax.ShapeDtypeStruct((2, rows_n, chunks // 2, CH, heads * DV), f32),
            jax.ShapeDtypeStruct((chunks, units, DK, DV), f32),
            jax.ShapeDtypeStruct((chunks, units, CH, DV), f32),
        ],
        cost_estimate=SMALL_COST,
        compiler_params=params(),
        name="delta_scan",
    )(pos, *prepared)
    return mixed, states, prepared[2], deltas


def mixer_backward(proj, small, d_out, pos, resets, conv_w, aux, states, invs, deltas):
    _, rows_n, half, _, _ = proj.shape
    width = conv_w.shape[1]
    chunks = 2 * half
    heads = width // (2 * DK + DV)
    units = rows_n * heads
    back = lambda c: chunks - 1 - c
    before = lambda c: jnp.maximum(back(c) - 1, 0)
    spec = lambda w: slot_spec(rows_n, w, back)
    tail = pl.BlockSpec(
        (1, rows_n, 1, 8, width),
        lambda c, pos, rst: (pos[before(c)] & 1, 0, pos[before(c)] >> 1, CH // 8 - 1, 0),
    )
    kept = lambda *s: pl.BlockSpec((1, units) + s, lambda c, pos, rst: (back(c), 0, 0, 0))
    return pl.pallas_call(
        partial(backward_kernel, heads, chunks),
        grid_spec=pltpu.PrefetchScalarGridSpec(
            num_scalar_prefetch=2,
            grid=(chunks,),
            in_specs=[spec(width), spec(LANES), tail, spec(heads * DV), whole(conv_w), whole(aux)]
            + [kept(DK, DV), kept(CH, CH), kept(CH, DV)],
            out_specs=[
                spec(width),
                spec(LANES),
                pl.BlockSpec((8, width), lambda c, pos, rst: (0, 0)),
                pl.BlockSpec((8, LANES), lambda c, pos, rst: (0, 0)),
            ],
            scratch_shapes=[
                pltpu.VMEM((rows_n, CH + 8, width), f32),
                pltpu.VMEM((rows_n, TAPS, CH + 8, width), f32),
                pltpu.VMEM((units, DK, DV), f32),
            ],
        ),
        out_shape=[
            jax.ShapeDtypeStruct((2, rows_n, half, CH, width), bf16),
            jax.ShapeDtypeStruct((2, rows_n, half, CH, LANES), bf16),
            jax.ShapeDtypeStruct((8, width), f32),
            jax.ShapeDtypeStruct((8, LANES), f32),
        ],
        cost_estimate=KERNEL_COST,
        compiler_params=params(),
        name="delta_backward",
    )(pos, resets, proj, small, proj, d_out, conv_w, aux, states, invs, deltas)


def local_call(body, name, inputs, specs, outs, bytes_accessed=0):
    return pl.pallas_call(
        body,
        grid=(1,),
        in_specs=specs,
        out_specs=whole_specs(outs),
        out_shape=outs,
        cost_estimate=SMALL_COST,
        compiler_params=pltpu.CompilerParams(vmem_limit_bytes=VMEM_BYTES),
        name=name,
    )(*inputs)


def term_specs(terms):
    kept, got, steps = terms
    rows_n = kept.shape[0]
    first = pl.BlockSpec((rows_n, 1) + kept.shape[2:], lambda i: (0, 0, 0, 0))
    flat = [step for row in steps for step in row]
    return [kept, got] + flat, [first, first] + [pl.BlockSpec((1,) + s.shape[1:], lambda i: (0, 0, 0)) for s in flat]


def row_total(refs, row, rows_n):
    kept, got = refs[0], refs[1]
    each = (len(refs) - 2) // rows_n
    total = kept[row, 0].astype(f32) + got[row, 0].astype(f32)
    for step in refs[2 + row * each : 2 + (row + 1) * each]:
        total = total + step[0].astype(f32)
    return total


def in_order(values, groups):
    size, batches = groups
    own = values.shape[-1] // (size * batches)
    return jnp.concatenate(
        [
            values[:, (b * size + s) * own : (b * size + s + 1) * own]
            for s in range(size)
            for b in range(batches)
        ],
        axis=1,
    )


def whole_specs(arrays):
    zeros = lambda n: lambda i: (0,) * n
    return [pl.BlockSpec(a.shape, zeros(len(a.shape))) for a in arrays]


def add_and_norm(terms, base, gain):
    inputs, specs = term_specs(terms)
    rows_n, _, span, _ = terms[0].shape

    def body(*refs):
        base_ref, gain_ref, out_ref, norm_ref = refs[len(inputs) :]
        for row in range(rows_n):
            at = pl.ds(row * span, span)
            total = base_ref[at, :].astype(f32) + row_total(refs[: len(inputs)], row, rows_n)
            scale = lax.rsqrt(jnp.mean(total * total, axis=-1, keepdims=True) + EPS_NORM)
            out_ref[at, :] = total
            norm_ref[row] = (total * scale * gain_ref[...]).astype(bf16)

    extra = [base, gain.reshape(1, D)]
    return local_call(
        body,
        "add_and_norm",
        inputs + extra,
        specs + whole_specs(extra),
        [jax.ShapeDtypeStruct((rows_n * span, D), f32), jax.ShapeDtypeStruct((rows_n, span, D), bf16)],
        4_000_000,
    )


def norm_back(terms, base, through, gain, out_dtype, groups=None):
    inputs, specs = term_specs(terms)
    rows_n, _, span, _ = terms[0].shape
    with_rows = groups is None

    def body(*refs):
        base_ref, through_ref, gain_ref = refs[len(inputs) : len(inputs) + 3]
        outs = refs[len(inputs) + 3 :]
        g_gain = jnp.zeros((1, D), f32)
        for row in range(rows_n):
            at = pl.ds(row * span, span)
            d_norm = row_total(refs[: len(inputs)], row, rows_n)
            x = base_ref[at, :].astype(f32)
            scale = lax.rsqrt(jnp.mean(x * x, axis=-1, keepdims=True) + EPS_NORM)
            e = d_norm * gain_ref[...]
            lean = jnp.mean(e * x, axis=-1, keepdims=True)
            total = through_ref[at, :].astype(f32) + scale * e - x * (scale * scale * scale * lean)
            g_gain = g_gain + jnp.sum(d_norm * x * scale, axis=0, keepdims=True)
            if with_rows:
                outs[0][at, :] = total.astype(out_dtype)
                outs[1][row] = total.astype(bf16)
            else:
                outs[0][at, :] = in_order(total, groups).astype(out_dtype)
        outs[-1][...] = g_gain

    extra = [base, through, gain.reshape(1, D)]
    outs = [jax.ShapeDtypeStruct((rows_n * span, D), out_dtype)]
    if with_rows:
        outs.append(jax.ShapeDtypeStruct((rows_n, span, D), bf16))
    return local_call(
        body,
        "norm_back",
        inputs + extra,
        specs + whole_specs(extra),
        outs + [jax.ShapeDtypeStruct((1, D), f32)],
        4_000_000,
    )


def add_in_order(terms, base, groups):
    inputs, specs = term_specs(terms)
    rows_n, _, span, _ = terms[0].shape

    def body(*refs):
        base_ref, out_ref = refs[len(inputs) :]
        for row in range(rows_n):
            at = pl.ds(row * span, span)
            total = base_ref[at, :] + row_total(refs[: len(inputs)], row, rows_n)
            out_ref[at, :] = in_order(total, groups).astype(bf16)

    return local_call(
        body,
        "add_in_order",
        inputs + [base],
        specs + whole_specs([base]),
        [jax.ShapeDtypeStruct((rows_n * span, D), bf16)],
        3_000_000,
    )[0]


ROW_BLOCK = 256


def gated_norm(mixed, proj, gain):
    rows_n, width = mixed.shape
    gate_block = pl.BlockSpec((ROW_BLOCK, width), lambda i: (i, proj.shape[1] // width - 1))

    def body(mixed_ref, gate_ref, gain_ref, out_ref):
        for at in range(0, width, DV):
            x = mixed_ref[:, at : at + DV]
            g = gate_ref[:, at : at + DV]
            scale = lax.rsqrt(jnp.mean(x * x, axis=-1, keepdims=True) + EPS_HEAD)
            out_ref[:, at : at + DV] = (x * scale * gain_ref[...] * (g * jax.nn.sigmoid(g))).astype(bf16)

    block = pl.BlockSpec((ROW_BLOCK, width), lambda i: (i, 0))
    return pl.pallas_call(
        body,
        grid=(rows_n // ROW_BLOCK,),
        in_specs=[block, gate_block, pl.BlockSpec((1, DV), lambda i: (0, 0))],
        out_specs=block,
        out_shape=jax.ShapeDtypeStruct((rows_n, width), bf16),
        cost_estimate=SMALL_COST,
        compiler_params=params(),
        name="gated_norm",
    )(mixed, proj, gain.reshape(1, DV))


def gated_norm_back(mixed, proj, gain, d_out):
    rows_n, width = mixed.shape
    gate_block = pl.BlockSpec((ROW_BLOCK, width), lambda i: (i, proj.shape[1] // width - 1))

    def body(mixed_ref, gate_ref, gain_ref, d_ref, d_mixed_ref, d_gate_ref, g_gain_ref):
        @pl.when(pl.program_id(0) == 0)
        def _():
            g_gain_ref[...] = jnp.zeros_like(g_gain_ref)

        g_gain = jnp.zeros((1, DV), f32)
        for at in range(0, width, DV):
            x = mixed_ref[:, at : at + DV]
            g = gate_ref[:, at : at + DV]
            d = d_ref[:, at : at + DV]
            scale = lax.rsqrt(jnp.mean(x * x, axis=-1, keepdims=True) + EPS_HEAD)
            sig = jax.nn.sigmoid(g)
            through = d * (g * sig)
            unit_x = x * scale
            e = through * gain_ref[...]
            lean = jnp.mean(e * unit_x, axis=-1, keepdims=True)
            d_mixed_ref[:, at : at + DV] = scale * (e - unit_x * lean)
            d_gate_ref[:, at : at + DV] = (
                d * (unit_x * gain_ref[...]) * (sig * (1.0 + g * (1.0 - sig)))
            ).astype(bf16)
            g_gain = g_gain + jnp.sum(through * unit_x, axis=0, keepdims=True)
        g_gain_ref[0:1, :] += g_gain

    block = pl.BlockSpec((ROW_BLOCK, width), lambda i: (i, 0))
    return pl.pallas_call(
        body,
        grid=(rows_n // ROW_BLOCK,),
        in_specs=[block, gate_block, pl.BlockSpec((1, DV), lambda i: (0, 0)), block],
        out_specs=[block, block, pl.BlockSpec((8, DV), lambda i: (0, 0))],
        out_shape=[
            jax.ShapeDtypeStruct((rows_n, width), f32),
            jax.ShapeDtypeStruct((rows_n, width), bf16),
            jax.ShapeDtypeStruct((8, DV), f32),
        ],
        cost_estimate=SMALL_COST,
        compiler_params=params(),
        name="gated_norm_back",
    )(mixed, proj, gain.reshape(1, DV), d_out)


def laid_out(blocks, pieces, total):
    size, rows_n, _ = blocks[0].shape

    def body(*refs):
        out_ref = refs[-1]
        for which, first, width, start in pieces:
            for s in range(size):
                out_ref[:, start + s * width : start + (s + 1) * width] = refs[which][
                    s, :, first : first + width
                ].astype(f32)

    return local_call(
        body, "laid_out", blocks, whole_specs(blocks), [jax.ShapeDtypeStruct((rows_n, total), f32)], 5_000_000
    )[0]


def swap(value, axis, bit):
    return lax.ppermute(value, axis, [(i, i ^ bit) for i in range(lax.axis_size(axis))])


def routes(axis):
    bits = [1 << i for i in range(lax.axis_size(axis).bit_length() - 1)]
    return [bits[1:] + bits[:1], bits[:0:-1] + bits[:1]]


def gather_rows(rows, axis, ordered=True, earlier=None):
    laid = []
    for row, order in zip(rows, routes(axis) * rows.shape[0]):
        held = row[None]
        names = [0]
        parts = []
        for i, bit in enumerate(order[:-1]):
            got = swap(held, axis, bit)
            names = names + [n ^ (bit >> 1) for n in names]
            if i < len(order) - 2:
                held = jnp.concatenate([held, got], axis=0)
            else:
                parts = [held, got]
        if ordered and names != sorted(names):
            place = {name: i for i, name in enumerate(names)}
            size = len(names) // 2
            for n in sorted(names):
                which, at = divmod(place[n], size)
                laid.append(parts[which][at : at + 1])
        else:
            laid.extend(parts)
    even = jnp.concatenate(laid, axis=0).reshape((rows.shape[0], -1) + rows.shape[1:])
    if earlier is not None:
        even, earlier = lax.optimization_barrier((even, earlier))
        return even, swap(even, axis, 1), earlier
    return even, swap(even, axis, 1)


def scatter_rows(keep, send, axis, ordered=True, earlier=()):
    got = after(swap(send, axis, 1), *earlier)
    rows_n, half, span, width = keep.shape
    depth = half.bit_length() - 1
    steps = []
    for row, order in zip(range(rows_n), routes(axis) * rows_n):
        bits = order[:-1]
        axes = sorted(bits, reverse=True) if ordered else bits[::-1]
        shape = (2,) * depth + (span, width)
        terms = [keep[row].reshape(shape), got[row].reshape(shape)]
        mine = []
        for bit in bits[::-1]:
            at = axes.index(bit)
            sent = sum(lax.index_in_dim(t, 1, at, keepdims=False).astype(f32) for t in terms).astype(bf16)
            back = swap(sent, axis, bit)
            terms = [lax.index_in_dim(t, 0, at, keepdims=False) for t in terms] + [back]
            axes = [b for b in axes if b != bit]
            mine.append(back.reshape((-1, span, width)))
        steps.append(mine)
    return keep, got, steps


def joined(halves):
    return jnp.concatenate([h.reshape(-1, h.shape[-1]) for h in halves], axis=0)


def after(value, *earlier):
    return lax.optimization_barrier((value,) + earlier)[0]


def sum_all(value, axes):
    for axis in axes:
        for i in range(lax.axis_size(axis).bit_length() - 1):
            value = value + swap(value, axis, 1 << i)
    return value


def gather_small(value, axis):
    held = value[None]
    size = lax.axis_size(axis)
    for i in range(size.bit_length() - 1):
        held = jnp.concatenate([held, swap(held, axis, 1 << i)], axis=0)
    return held[jnp.arange(size, dtype=jnp.int32) ^ lax.axis_index(axis).astype(jnp.int32)]


def mm(left, right):
    return jnp.dot(left, right, preferred_element_type=f32)


def contract_rows(left, right):
    return lax.dot_general(left, right, (((0,), (0,)), ((), ())), preferred_element_type=f32)


def contract_cols(left, right):
    return lax.dot_general(left, right, (((1,), (1,)), ((), ())), preferred_element_type=f32)


def rms_scale(values, scale_gain):
    return values * lax.rsqrt(jnp.mean(values * values, axis=-1, keepdims=True) + EPS_NORM) * scale_gain


def glu_hidden(gate_half, up_half):
    return jax.nn.silu(gate_half) * up_half


def exchanged(packed):
    return lax.all_to_all(packed, "seq", split_axis=0, concat_axis=0, tiled=True)


def stacked(blocks):
    full = lax.all_gather(blocks, "batch", axis=0, tiled=False)
    return full.reshape(-1, blocks.shape[-1])


def summed(partial_grad):
    own = lax.psum_scatter(partial_grad, "batch", scatter_dimension=0, tiled=True)
    return own.reshape(lax.axis_size("seq"), -1, own.shape[-1])


def shards(
    tokens,
    grad_out,
    resets,
    w_proj,
    w_small,
    w_out,
    w_gu,
    w_down,
    norm_in,
    norm_ff,
    norm_head,
    conv_w,
    a_log,
    dt_bias,
):
    size = lax.axis_size("seq")
    groups = lax.axis_size("batch")
    me = lax.axis_index("seq")
    batch_rows, span_len, _ = tokens.shape
    own_rows = w_proj.shape[0]
    heads = H // size
    ff = FF // size
    key_w, val_w = heads * DK, heads * DV
    conv_cols = 2 * key_w + val_w
    half = batch_rows * size // 2 * span_len
    halves = (batch_rows, size // 2, span_len)
    blocks = (2,) + halves

    def shuffled(array):
        lead = array.shape[:-1]
        return array.reshape(lead + (size, groups, own_rows)).swapaxes(-3, -2).reshape(lead + (D,))

    def restored(array):
        lead = array.shape[:-1]
        return array.reshape(lead + (groups, size, own_rows)).swapaxes(-3, -2).reshape(lead + (D,))

    out_w = lax.all_gather(w_out, "batch", axis=0, tiled=True)
    packed_mix = jnp.concatenate(
        [
            w_proj[:, :KW].reshape(own_rows, size, key_w),
            w_proj[:, KW : 2 * KW].reshape(own_rows, size, key_w),
            w_proj[:, 2 * KW : CW].reshape(own_rows, size, val_w),
            w_proj[:, CW:].reshape(own_rows, size, val_w),
        ],
        axis=-1,
    ).transpose(1, 0, 2)
    moved_mix = exchanged(packed_mix)
    own_in = shuffled(tokens).reshape(-1, D)
    gain_in, gain_ff = shuffled(norm_in), shuffled(norm_ff)
    h_in = joined(gather_rows(rms_scale(own_in.astype(f32), gain_in).astype(bf16).reshape(tokens.shape), "seq"))
    mix_w = stacked(after(moved_mix, out_w, h_in))
    packed_gu, w_small, d_own, own_down = after(
        (
            w_gu.reshape(own_rows, 2, size, ff).transpose(2, 0, 1, 3).reshape(size, own_rows, 2 * ff),
            w_small,
            shuffled(grad_out),
            shuffled(w_down),
        ),
        moved_mix,
    )
    d_halves = gather_rows(d_own, "seq", False)
    small_all = gather_small(gather_small(w_small, "batch"), "seq").swapaxes(0, 1).reshape(D, 2 * H)
    small_w = jnp.pad(
        jnp.concatenate(
            [
                lax.dynamic_slice_in_dim(small_all, me * heads, heads, 1),
                lax.dynamic_slice_in_dim(small_all, H + me * heads, heads, 1),
            ],
            axis=1,
        ),
        ((0, 0), (0, LANES - 2 * heads)),
    )
    out_w = shuffled(out_w)
    moved_gu = exchanged(packed_gu)

    slots = jnp.arange(size, dtype=jnp.int32) ^ me.astype(jnp.int32)
    conv_l = jnp.concatenate(
        [
            lax.dynamic_slice_in_dim(conv_w, me * key_w, key_w, 1),
            lax.dynamic_slice_in_dim(conv_w, KW + me * key_w, key_w, 1),
            lax.dynamic_slice_in_dim(conv_w, 2 * KW + me * val_w, val_w, 1),
        ],
        axis=1,
    )
    at_heads = (heads, LANES - 2 * heads)
    aux = jnp.pad(
        jnp.stack(
            [
                lax.dynamic_slice_in_dim(jnp.exp(a_log), me * heads, heads),
                lax.dynamic_slice_in_dim(dt_bias, me * heads, heads),
            ]
        ),
        ((0, 6), at_heads),
    )

    small = mm(h_in, small_w).reshape(blocks + (LANES,))
    proj = mm(h_in, mix_w)
    down_first = lax.all_gather(own_down[:, : D // 2], "batch", axis=0, tiled=True)
    prepared = mixer_prepare(proj.reshape(blocks + (-1,)), small, slots, resets, conv_l, aux)
    prepared, moved_gu, down_first = lax.optimization_barrier((prepared, moved_gu, down_first))
    down_rest = lax.all_gather(own_down[:, D // 2 :], "batch", axis=0, tiled=True)
    gu_w = stacked(moved_gu)
    mixed, states, invs, deltas = mixer_scan(prepared, slots, batch_rows)
    mixed = mixed.reshape(-1, val_w)
    z_rows = gated_norm(mixed, proj, norm_head)

    def parts(product, left):
        send = product(left[half:]).astype(bf16).reshape(halves + (D,))
        return product(left[:half]).astype(bf16).reshape(halves + (D,)), send

    keep, send = parts(lambda rows: mm(rows, out_w), z_rows)
    d_out = joined(after(d_halves, keep, send))
    residual, normed_ff = add_and_norm(scatter_rows(keep, send, "seq"), own_in, gain_ff)

    even, odd, gu_w = gather_rows(normed_ff, "seq", False, gu_w)
    h_ff = joined((even, odd))
    gate_up = mm(h_ff, gu_w)
    hidden_full, pull_glu = jax.vjp(glu_hidden, gate_up[:, :ff], gate_up[:, ff:])
    hidden = hidden_full.astype(bf16)
    down_grad = contract_rows(d_out, hidden).astype(bf16)
    hidden, down_rest = lax.optimization_barrier((hidden, down_rest))
    down_own = summed(down_grad)
    d_hidden = contract_cols(d_out[:, : D // 2], down_first) + contract_cols(d_out[:, D // 2 :], down_rest)
    down_w = jnp.concatenate([down_first, down_rest], axis=1)
    d_gate_up = jnp.concatenate(pull_glu(d_hidden), axis=1).astype(bf16)
    keep, send = parts(lambda rows: contract_cols(rows, gu_w), d_gate_up)
    terms = scatter_rows(keep, send, "seq", False)
    gu_grad = contract_rows(after(h_ff, keep, send), d_gate_up).astype(bf16)
    gu_own = summed(gu_grad)
    out_parts = parts(lambda rows: mm(rows, down_w), after(hidden, keep, send))
    d_residual, d_branch, g_norm_ff = norm_back(terms, residual, d_own.reshape(-1, D), gain_ff, f32)

    d_branch = joined(gather_rows(after(d_branch, gu_grad, down_own, out_parts), "seq"))
    d_heads = contract_cols(d_branch, out_w)
    d_mixed, d_gate, g_norm_head = gated_norm_back(mixed, proj, norm_head, d_heads)
    out_grad = jnp.concatenate(
        [contract_rows(h_in, d_gate).astype(bf16), contract_rows(d_branch, z_rows).astype(bf16)], axis=1
    )
    d_mixed, out_grad = lax.optimization_barrier((d_mixed, out_grad))
    d_proj, d_small, g_conv_l, g_decay = mixer_backward(
        proj.reshape(blocks + (-1,)), small, d_mixed.reshape(blocks + (val_w,)), slots, resets, conv_l, aux, states, invs, deltas
    )
    d_proj, gu_own = lax.optimization_barrier((d_proj.reshape(-1, conv_cols), gu_own))
    d_small = d_small.reshape(-1, LANES)
    out_own = summed(out_grad)
    mix_grad = contract_rows(h_in, d_proj).astype(bf16)
    mix_moved = lax.all_to_all(
        mix_grad.reshape(groups, size, own_rows, conv_cols), "seq", split_axis=1, concat_axis=1, tiled=True
    )
    d_proj, d_small, g_conv_l, gu_own = after((d_proj, d_small, g_conv_l, gu_own), mix_grad)
    mix_moved, gu_own = lax.optimization_barrier((mix_moved, gu_own))
    mix_grads = lax.psum_scatter(mix_moved, "batch", scatter_dimension=0, tiled=True)[0]
    gu_grads, down_grads = exchanged(gu_own), exchanged(down_own)
    block_out = add_in_order(scatter_rows(*out_parts, "seq", False), residual, (size, groups))
    keep, send = parts(
        lambda rows: contract_cols(rows[:, : conv_cols + val_w], mix_w)
        + contract_cols(rows[:, conv_cols + val_w :], small_w),
        jnp.concatenate([d_proj, d_gate, d_small], axis=1),
    )
    d_tokens, g_norm_in = norm_back(
        scatter_rows(keep, send, "seq"), own_in, after(d_residual, out_own), gain_in, bf16, (size, groups)
    )

    small_grad = contract_rows(d_small, h_in)[: 2 * heads]
    local = jnp.concatenate(
        [g_conv_l[:TAPS].reshape(-1), g_decay[:2, heads : 2 * heads].reshape(-1), small_grad.reshape(-1)]
    )
    shared = gather_small(sum_all(local, ("batch",)), "seq")
    g_conv_all = shared[:, : TAPS * conv_cols].reshape(size, TAPS, conv_cols).transpose(1, 0, 2)
    g_conv = jnp.concatenate(
        [
            g_conv_all[:, :, :key_w].reshape(TAPS, KW),
            g_conv_all[:, :, key_w : 2 * key_w].reshape(TAPS, KW),
            g_conv_all[:, :, 2 * key_w :].reshape(TAPS, VW),
        ],
        axis=1,
    )
    g_alog = shared[:, TAPS * conv_cols : TAPS * conv_cols + heads].reshape(H)
    g_dt = shared[:, TAPS * conv_cols + heads : TAPS * conv_cols + 2 * heads].reshape(H)
    g_small = lax.dynamic_slice_in_dim(
        shared[:, TAPS * conv_cols + 2 * heads :].reshape(size, 2, heads, D),
        (lax.axis_index("batch") * size + me) * own_rows,
        own_rows,
        3,
    )
    g_small = g_small.transpose(3, 1, 0, 2).reshape(own_rows, 2 * H)
    gains = sum_all(jnp.concatenate([g_norm_in[0], g_norm_ff[0], g_norm_head[0]]), ("seq", "batch"))
    gains = jnp.concatenate([restored(gains[: 2 * D].reshape(2, D)).reshape(-1), gains[2 * D :]])

    out_grads = exchanged(out_own)
    g_gu = laid_out([gu_grads], [(0, 0, ff, 0), (0, ff, ff, FF)], 2 * FF)
    g_down = down_grads.astype(f32).transpose(0, 2, 1).reshape(FF, own_rows)
    g_out = out_grads[:, :, val_w:].astype(f32).transpose(0, 2, 1).reshape(VW, own_rows)
    ready = (d_tokens, block_out, out_grads, g_gu, g_down, g_out, gains, g_conv, g_small)
    mix_grads, ready = lax.optimization_barrier((mix_grads, ready))
    d_tokens, block_out, out_grads, g_gu, g_down, g_out, gains, g_conv, g_small = ready
    g_proj = laid_out(
        [mix_grads, out_grads],
        [(0, 0, key_w, 0), (0, key_w, key_w, KW), (0, 2 * key_w, val_w, 2 * KW), (1, 0, val_w, CW)],
        CW + VW,
    )
    return (
        block_out.reshape(tokens.shape),
        d_tokens.reshape(tokens.shape),
        g_proj,
        g_small,
        g_out,
        g_gu,
        g_down,
        gains[:D],
        gains[D : 2 * D],
        gains[2 * D :],
        g_conv,
        g_alog,
        g_dt,
    )


def solution(mesh):
    rows = P(("seq", "batch"), None)
    cols = P(None, ("seq", "batch"))
    act = P("batch", "seq", None)
    in_specs = (act, act, P("batch"), rows, rows, rows, rows, rows) + (P(),) * 6
    out_specs = (act, act, rows, rows, cols, rows, cols) + (P(),) * 6
    return jax.shard_map(shards, mesh=mesh, in_specs=in_specs, out_specs=out_specs, check_vma=False)
```

```python
from functools import partial

import jax
import jax.numpy as jnp
from jax import lax
from jax.experimental import pallas as pl
from jax.experimental.pallas import tpu as pltpu
from jax.sharding import PartitionSpec as P

D = 2048
H = 16
DK = 128
DV = 256
FF = 5632
CH = 64
KW = 2048
VW = 4096
CW = 8192
TAPS = 4
LANES = 128

EPS_NORM = 1e-06
EPS_HEAD = 1e-05
EPS_UNIT = 1e-06
f32 = jnp.float32
bf16 = jnp.bfloat16
VMEM_BYTES = 56 * 1024 * 1024
KERNEL_COST = pl.CostEstimate(flops=30_000_000_000, bytes_accessed=40_000_000, transcendentals=0)


def dot_in(left, right, contract, precision):
    return lax.dot_general(
        left,
        right,
        (((contract[0],), (contract[1],)), ((), ())),
        precision=precision,
        preferred_element_type=f32,
    )


def fine(left, right, contract=(1, 0)):
    return dot_in(left, right, contract, lax.Precision.HIGH)


def coarse(left, right, contract=(1, 0)):
    return dot_in(left, right, contract, lax.Precision.HIGH)


def position_masks(reset, chunk):
    rows = lax.broadcasted_iota(jnp.int32, (CH, CH), 0)
    cols = lax.broadcasted_iota(jnp.int32, (CH, CH), 1)
    time = lax.broadcasted_iota(jnp.int32, (CH, 1), 0)
    offset = reset - chunk * CH
    cut = jnp.where(offset < 0, CH, offset)
    apart = (rows >= cut) & (cols < cut)
    causal = jnp.where((rows >= cols) & ~apart, 1.0, 0.0)
    strict = jnp.where((rows > cols) & ~apart, 1.0, 0.0)
    in_first = jnp.where(time < cut, 1.0, 0.0)
    last_first = jnp.where(CH - 1 < cut, 1.0, 0.0)
    in_last = jnp.where((time >= cut) | (cut > CH - 1), 1.0, 0.0)
    begin = jnp.where(time >= offset, offset, -chunk * CH)
    taps = [jnp.where(time - (TAPS - 1) + j >= begin, 1.0, 0.0) for j in range(TAPS)]
    return causal, strict, in_first, last_first, in_last, taps


def gates(small, aux):
    beta = jax.nn.sigmoid(small)
    shifted = small + aux[1:2]
    soft = jnp.maximum(shifted, 0.0) + jnp.log1p(jnp.exp(-jnp.abs(shifted)))
    return beta, -aux[0:1] * soft, shifted


def running(values, reverse=False):
    rows = lax.broadcasted_iota(jnp.int32, (CH, CH), 0)
    cols = lax.broadcasted_iota(jnp.int32, (CH, CH), 1)
    keep = (cols >= rows) if reverse else (cols <= rows)
    return fine(jnp.where(keep, 1.0, 0.0), values)


def as_rows(total):
    pick_row = lax.broadcasted_iota(jnp.int32, (LANES, LANES), 0)
    pick_col = lax.broadcasted_iota(jnp.int32, (LANES, LANES), 1)
    return fine(jnp.where(pick_row == pick_col, 1.0, 0.0), total, (1, 1))


def inverses_unit_lower(parts):
    size = parts[0].shape[0]
    rows = lax.broadcasted_iota(jnp.int32, (size, size), 0)
    cols = lax.broadcasted_iota(jnp.int32, (size, size), 1)
    eye = jnp.where(rows == cols, 1.0, 0.0)
    block = lambda n: jnp.where((rows & -n) == (cols & -n), 1.0, 0.0)
    inside = {n: block(n) for n in (16, 32, 64)}
    power = [part * inside[16] for part in parts]
    inv = [eye - diag for diag in power]
    for _ in range(3):
        power = [fine(p, p) for p in power]
        more = [fine(i, p) for i, p in zip(inv, power)]
        inv = [i + m for i, m in zip(inv, more)]
    for n in (16, 32):
        ring = inside[2 * n] - inside[n]
        left = [fine(i, part * ring) for i, part in zip(inv, parts)]
        more = [fine(l, i) for l, i in zip(left, inv)]
        inv = [i - m for i, m in zip(inv, more)]
    return inv


def conv_taps(ext_ref, row, conv_w, taps):
    out = None
    for j in range(TAPS):
        part = conv_w[j : j + 1] * (ext_ref[row, 8 - (TAPS - 1) + j : 8 - (TAPS - 1) + j + CH, :] * taps[j])
        out = part if out is None else out + part
    return out


def unit(values):
    return lax.rsqrt(jnp.sum(values * values, axis=-1, keepdims=True) + EPS_UNIT)


def head_parts(active, head, heads):
    q = active[:, head * DK : (head + 1) * DK]
    k = active[:, heads * DK + head * DK : heads * DK + (head + 1) * DK]
    v = active[:, 2 * heads * DK + head * DV : 2 * heads * DK + (head + 1) * DV]
    return q, k, v


def decay_terms(total, total_rows, head, heads, masks):
    causal, strict, in_first, last_first, in_last, _ = masks
    lane = heads + head
    col = total[:, lane : lane + 1]
    row = total_rows[lane : lane + 1, :]
    ratios = jnp.exp(jnp.where(causal > 0, col - row, 0.0)) * causal
    last = col[CH - 1 : CH, :]
    start_fade = jnp.exp(col) * in_first
    start_last = jnp.exp(last) * last_first
    end_fade = jnp.exp(jnp.where(in_last > 0, last - col, 0.0)) * in_last
    return ratios, start_fade, start_last, end_fade


def backward_kernel(
    heads,
    chunks,
    pos_ref,
    reset_ref,
    proj,
    small_ref,
    tail,
    d_out,
    conv_w_ref,
    aux_ref,
    state_ref,
    inv_ref,
    delta_ref,
    d_proj,
    d_small_ref,
    g_conv,
    g_decay,
    ext,
    dext,
    d_state,
):
    step = pl.program_id(0)
    chunk = chunks - 1 - step
    width = heads * (2 * DK + DV)

    @pl.when(step == 0)
    def _():
        dext[...] = jnp.zeros_like(dext)
        d_state[...] = jnp.zeros_like(d_state)
        g_conv[...] = jnp.zeros_like(g_conv)
        g_decay[...] = jnp.zeros_like(g_decay)

    conv_w = conv_w_ref[...]
    aux = aux_ref[...]
    lane_ids = lax.broadcasted_iota(jnp.int32, (CH, LANES), 1)
    last_row = lax.broadcasted_iota(jnp.int32, (CH, 1), 0) == CH - 1
    ones = jnp.ones((CH, LANES), f32)
    rows = range(proj.shape[1])
    units = range(len(rows) * heads)
    row_of = [u // heads for u in units]
    head_of = [u % heads for u in units]
    masks = [position_masks(reset_ref[r], chunk) for r in rows]
    conv = []
    for r in rows:
        ext[r, 0:8, :] = tail[0, r, 0].astype(bf16).astype(f32)
        ext[r, 8:, :] = proj[0, r, 0].astype(bf16).astype(f32)
        conv.append(conv_taps(ext, r, conv_w, masks[r][5]))
    sig = [jax.nn.sigmoid(c) for c in conv]
    active = [c * g for c, g in zip(conv, sig)]
    gated = [gates(small_ref[0, r, 0], aux) for r in rows]
    beta_all = [g[0] for g in gated]
    decay = [g[1] for g in gated]
    shifted = [g[2] for g in gated]
    total = [running(d) for d in decay]
    total_rows = [as_rows(t) for t in total]
    parts = [head_parts(active[row_of[u]], head_of[u], heads) for u in units]
    a_q, a_k, v = ([p[i] for p in parts] for i in range(3))
    q_scale = [unit(a) for a in a_q]
    k_scale = [unit(a) for a in a_k]
    q = [a_q[u] * (q_scale[u] * DK**-0.5) for u in units]
    k = [a_k[u] * k_scale[u] for u in units]
    beta = [beta_all[row_of[u]][:, head_of[u] : head_of[u] + 1] for u in units]
    terms = [
        decay_terms(total[row_of[u]], total_rows[row_of[u]], head_of[u], heads, masks[row_of[u]]) for u in units
    ]
    ratios, start_fade, start_last, end_fade = ([t[i] for t in terms] for i in range(4))
    both = [jnp.concatenate([q[u], k[u]], axis=0) for u in units]
    pair = [fine(both[u], k[u], (1, 1)) for u in units]
    key_key = [p[CH:] for p in pair]
    query_key = [p[:CH] for p in pair]
    old = [state_ref[0, u] for u in units]
    inv = [inv_ref[0, u] for u in units]
    delta = [delta_ref[0, u] for u in units]
    do = [d_out[0, row_of[u], 0, :, head_of[u] * DV : (head_of[u] + 1) * DV] for u in units]
    ds = [d_state[u] for u in units]
    read = [coarse(both[u], old[u]) for u in units]
    readings = [ratios[u] * query_key[u] for u in units]
    faded = [end_fade[u] * k[u] for u in units]
    back_read = [coarse(readings[u], do[u], (0, 0)) for u in units]
    back_state = [coarse(faded[u], ds[u]) for u in units]
    d_right = [coarse(inv[u], back_read[u] + back_state[u], (0, 0)) for u in units]
    d_pair = [coarse(jnp.concatenate([do[u], d_right[u]], axis=0), delta[u], (1, 1)) for u in units]
    d_faded = [coarse(delta[u], ds[u], (1, 1)) for u in units]
    d_read = [
        jnp.concatenate([start_fade[u] * do[u], -(beta[u] * start_fade[u]) * d_right[u]], axis=0) for u in units
    ]
    grown = [coarse(both[u], d_read[u], (0, 0)) for u in units]
    d_both = [coarse(d_read[u], old[u], (1, 1)) for u in units]
    for u in units:
        d_state[u] = start_last[u] * ds[u] + grown[u]
    d_v = [beta[u] * d_right[u] for u in units]
    d_read_pair = [d_pair[u][:CH] * ratios[u] for u in units]
    d_sys = [-d_pair[u][CH:] * (ratios[u] * masks[row_of[u]][1]) for u in units]
    d_key_key = [beta[u] * d_sys[u] for u in units]
    moved = [d_key_key[u] * key_key[u] + d_read_pair[u] * query_key[u] for u in units]
    moved_cols = [fine(m, ones, (0, 0))[:, 0:1] for m in moved]
    q_more = [coarse(d_read_pair[u], k[u]) for u in units]
    k_more = [coarse(jnp.concatenate([d_read_pair[u], d_key_key[u]], axis=0), both[u], (0, 0)) for u in units]
    k_most = [coarse(d_key_key[u], k[u]) for u in units]
    d_beta_all = [jnp.zeros((CH, LANES), f32) for _ in rows]
    d_total = [jnp.zeros((CH, LANES), f32) for _ in rows]
    d_active = []
    for u in units:
        r, head = row_of[u], head_of[u]
        recall = read[u][CH:]
        d_beta = jnp.sum(d_right[u] * (v[u] - start_fade[u] * recall), axis=-1, keepdims=True) + jnp.sum(
            d_sys[u] * key_key[u], axis=-1, keepdims=True
        )
        d_start = jnp.sum(do[u] * read[u][:CH], axis=-1, keepdims=True) - beta[u] * jnp.sum(
            d_right[u] * recall, axis=-1, keepdims=True
        )
        d_end = jnp.sum(d_faded[u] * k[u], axis=-1, keepdims=True) * end_fade[u]
        d_last = jnp.sum(d_end, axis=0, keepdims=True) + start_last[u] * jnp.sum(
            jnp.sum(ds[u] * old[u], axis=-1, keepdims=True), axis=0, keepdims=True
        )
        d_col = (
            jnp.sum(moved[u], axis=-1, keepdims=True)
            - moved_cols[u]
            + d_start * start_fade[u]
            - d_end
            + jnp.where(last_row, d_last, 0.0)
        )
        d_q = d_both[u][:CH] + q_more[u]
        d_k = d_both[u][CH:] + k_more[u] + k_most[u] + end_fade[u] * d_faded[u]
        d_aq = (q_scale[u] * DK**-0.5) * (
            d_q - a_q[u] * (q_scale[u] * q_scale[u] * jnp.sum(a_q[u] * d_q, axis=-1, keepdims=True))
        )
        d_ak = k_scale[u] * (
            d_k - a_k[u] * (k_scale[u] * k_scale[u] * jnp.sum(a_k[u] * d_k, axis=-1, keepdims=True))
        )
        d_active.append((d_aq, d_ak, d_v[u]))
        d_beta_all[r] = jnp.where(lane_ids == head, d_beta, d_beta_all[r])
        d_total[r] = jnp.where(lane_ids == heads + head, d_col, d_total[r])
    d_decay = [running(d, reverse=True) for d in d_total]
    for r in rows:
        taps = masks[r][5]
        d_shift = d_decay[r] * (-aux[0:1]) * jax.nn.sigmoid(shifted[r])
        d_small_ref[0, r, 0] = (d_beta_all[r] * beta_all[r] * (1.0 - beta_all[r]) + d_shift).astype(bf16)
        g_decay[0:1, :] += jnp.sum(d_decay[r] * decay[r], axis=0, keepdims=True)
        g_decay[1:2, :] += jnp.sum(d_shift, axis=0, keepdims=True)
        own = d_active[r * heads : (r + 1) * heads]
        d_act = jnp.concatenate([own[h][i] for i in range(3) for h in range(heads)], axis=1)
        d_conv = d_act * (sig[r] * (1.0 + conv[r] * (1.0 - sig[r])))
        d_in = None
        for j in range(TAPS):
            masked = d_conv * taps[j]
            g_conv[j : j + 1, :] += jnp.sum(
                masked * ext[r, 8 - (TAPS - 1) + j : 8 - (TAPS - 1) + j + CH, :], axis=0, keepdims=True
            )
            dext[r, j, 0:CH, :] = masked
            shift = TAPS - 1 - j
            part = conv_w[j : j + 1] * dext[r, j, shift : shift + CH, :]
            d_in = part if d_in is None else d_in + part
            dext[r, j, CH : CH + 8, :] = masked[0:8]
        d_proj[0, r, 0] = d_in.astype(bf16)


def params():
    return pltpu.CompilerParams(dimension_semantics=("arbitrary",), vmem_limit_bytes=VMEM_BYTES)


def whole(array):
    return pl.BlockSpec(array.shape, lambda c, pos, rst: (0,) * array.ndim)


SMALL_COST = pl.CostEstimate(flops=1_000_000, bytes_accessed=1_000, transcendentals=0)


def slot_spec(rows_n, width, chunk_of):
    return pl.BlockSpec(
        (1, rows_n, 1, CH, width), lambda c, pos, rst: (pos[chunk_of(c)] & 1, 0, pos[chunk_of(c)] >> 1, 0, 0)
    )


def prepare_kernel(
    heads, pos_ref, reset_ref, first, second, tail, small_a, small_b, conv_w_ref, aux_ref, *outs_and_scratch
):
    both_out, value_out, inv_out, read_out, cols_out, ext = outs_and_scratch
    step = pl.program_id(0)
    conv_w = conv_w_ref[...]
    aux = aux_ref[...]
    lane_ids = lax.broadcasted_iota(jnp.int32, (CH, LANES), 1)
    systems = []
    for row in range(first.shape[1]):
        ext[row, 0:8, :] = jnp.where(step > 0, tail[0, row, 0].astype(bf16).astype(f32), 0.0)
        ext[row, 8 : 8 + CH, :] = first[0, row, 0].astype(bf16).astype(f32)
        ext[row, 8 + CH :, :] = second[0, row, 0].astype(bf16).astype(f32)
        for which, small_ref in enumerate((small_a, small_b)):
            masks = position_masks(reset_ref[row], 2 * step + which)
            conv = None
            for j in range(TAPS):
                at = which * CH + 8 - (TAPS - 1) + j
                part = conv_w[j : j + 1] * (ext[row, at : at + CH, :] * masks[5][j])
                conv = part if conv is None else conv + part
            active = conv * jax.nn.sigmoid(conv)
            beta_all, decay, _ = gates(small_ref[0, row, 0], aux)
            total = running(decay)
            total_rows = as_rows(total)
            for head in range(heads):
                at = row * heads + head
                q, k, v = head_parts(active, head, heads)
                q = q * (unit(q) * DK**-0.5)
                k = k * unit(k)
                beta = beta_all[:, head : head + 1]
                ratios, start_fade, start_last, end_fade = decay_terms(total, total_rows, head, heads, masks)
                both = jnp.concatenate([q, k], axis=0)
                pair = fine(both, k, (1, 1))
                both_out[which, at] = both
                value_out[which, at] = v
                systems.append((which, at, beta * (ratios * masks[1] * pair[CH:])))
                read_out[which, at] = ratios * pair[:CH]
                cols_out[which, at] = jnp.where(
                    lane_ids == 0,
                    beta,
                    jnp.where(lane_ids == 1, start_fade, jnp.where(lane_ids == 2, end_fade, start_last)),
                )
    for (which, at, _), inv in zip(systems, inverses_unit_lower([part for _, _, part in systems])):
        inv_out[which, at] = inv


def scan_kernel(heads, pos_ref, both_ref, value_ref, inv_ref, read_ref, cols_ref, outs, state_out, delta_out, state):
    @pl.when(pl.program_id(0) == 0)
    def _():
        state[...] = jnp.zeros_like(state)

    state_out[0] = state[...]
    units = range(state.shape[0])
    old = [state[u] for u in units]
    beta = [cols_ref[0, u, :, 0:1] for u in units]
    start_fade = [cols_ref[0, u, :, 1:2] for u in units]
    end_fade = [cols_ref[0, u, :, 2:3] for u in units]
    start_last = [cols_ref[0, u, 0:1, 3:4] for u in units]
    read = [coarse(both_ref[0, u], old[u]) for u in units]
    right = [beta[u] * (value_ref[0, u] - start_fade[u] * read[u][CH:]) for u in units]
    delta = [coarse(inv_ref[0, u], right[u]) for u in units]
    grown = [coarse(end_fade[u] * both_ref[0, u, CH:, :], delta[u], (0, 0)) for u in units]
    local = [coarse(read_ref[0, u], delta[u]) for u in units]
    for u in units:
        row, head = divmod(u, heads)
        state[u] = start_last[u] * old[u] + grown[u]
        outs[0, row, 0, :, head * DV : (head + 1) * DV] = start_fade[u] * read[u][:CH] + local[u]
        delta_out[0, u] = delta[u]


def mixer_prepare(proj, small, pos, resets, conv_w, aux):
    _, rows_n, half, _, _ = proj.shape
    width = conv_w.shape[1]
    chunks = 2 * half
    heads = width // (2 * DK + DV)
    units = rows_n * heads
    tail = pl.BlockSpec(
        (1, rows_n, 1, 8, width),
        lambda i, pos, rst: (
            pos[jnp.maximum(2 * i - 1, 0)] & 1,
            0,
            pos[jnp.maximum(2 * i - 1, 0)] >> 1,
            CH // 8 - 1,
            0,
        ),
    )
    even = lambda w: slot_spec(rows_n, w, lambda i: 2 * i)
    odd = lambda w: slot_spec(rows_n, w, lambda i: 2 * i + 1)
    shapes = ((2 * CH, DK), (CH, DV), (CH, CH), (CH, CH), (CH, LANES))
    return pl.pallas_call(
        partial(prepare_kernel, heads),
        grid_spec=pltpu.PrefetchScalarGridSpec(
            num_scalar_prefetch=2,
            grid=(half,),
            in_specs=[even(width), odd(width), tail, even(LANES), odd(LANES), whole(conv_w), whole(aux)],
            out_specs=[pl.BlockSpec((2, units) + s, lambda i, pos, rst: (i, 0, 0, 0)) for s in shapes],
            scratch_shapes=[pltpu.VMEM((rows_n, 2 * CH + 8, width), f32)],
        ),
        out_shape=[jax.ShapeDtypeStruct((chunks, units) + s, f32) for s in shapes],
        cost_estimate=KERNEL_COST,
        compiler_params=params(),
        name="delta_prepare",
    )(pos, resets, proj, proj, proj, small, small, conv_w, aux)


def mixer_scan(prepared, pos, rows_n):
    chunks, units = prepared[0].shape[:2]
    heads = units // rows_n
    kept = lambda *s: pl.BlockSpec((1, units) + s, lambda c, pos: (c, 0, 0, 0))
    mixed, states, deltas = pl.pallas_call(
        partial(scan_kernel, heads),
        grid_spec=pltpu.PrefetchScalarGridSpec(
            num_scalar_prefetch=1,
            grid=(chunks,),
            in_specs=[kept(*p.shape[2:]) for p in prepared],
            out_specs=[
                pl.BlockSpec(
                    (1, rows_n, 1, CH, heads * DV), lambda c, pos: (pos[c] & 1, 0, pos[c] >> 1, 0, 0)
                ),
                kept(DK, DV),
                kept(CH, DV),
            ],
            scratch_shapes=[pltpu.VMEM((units, DK, DV), f32)],
        ),
        out_shape=[
            jax.ShapeDtypeStruct((2, rows_n, chunks // 2, CH, heads * DV), f32),
            jax.ShapeDtypeStruct((chunks, units, DK, DV), f32),
            jax.ShapeDtypeStruct((chunks, units, CH, DV), f32),
        ],
        cost_estimate=SMALL_COST,
        compiler_params=params(),
        name="delta_scan",
    )(pos, *prepared)
    return mixed, states, prepared[2], deltas


def mixer_backward(proj, small, d_out, pos, resets, conv_w, aux, states, invs, deltas):
    _, rows_n, half, _, _ = proj.shape
    width = conv_w.shape[1]
    chunks = 2 * half
    heads = width // (2 * DK + DV)
    units = rows_n * heads
    back = lambda c: chunks - 1 - c
    before = lambda c: jnp.maximum(back(c) - 1, 0)
    spec = lambda w: slot_spec(rows_n, w, back)
    tail = pl.BlockSpec(
        (1, rows_n, 1, 8, width),
        lambda c, pos, rst: (pos[before(c)] & 1, 0, pos[before(c)] >> 1, CH // 8 - 1, 0),
    )
    kept = lambda *s: pl.BlockSpec((1, units) + s, lambda c, pos, rst: (back(c), 0, 0, 0))
    return pl.pallas_call(
        partial(backward_kernel, heads, chunks),
        grid_spec=pltpu.PrefetchScalarGridSpec(
            num_scalar_prefetch=2,
            grid=(chunks,),
            in_specs=[spec(width), spec(LANES), tail, spec(heads * DV), whole(conv_w), whole(aux)]
            + [kept(DK, DV), kept(CH, CH), kept(CH, DV)],
            out_specs=[
                spec(width),
                spec(LANES),
                pl.BlockSpec((8, width), lambda c, pos, rst: (0, 0)),
                pl.BlockSpec((8, LANES), lambda c, pos, rst: (0, 0)),
            ],
            scratch_shapes=[
                pltpu.VMEM((rows_n, CH + 8, width), f32),
                pltpu.VMEM((rows_n, TAPS, CH + 8, width), f32),
                pltpu.VMEM((units, DK, DV), f32),
            ],
        ),
        out_shape=[
            jax.ShapeDtypeStruct((2, rows_n, half, CH, width), bf16),
            jax.ShapeDtypeStruct((2, rows_n, half, CH, LANES), bf16),
            jax.ShapeDtypeStruct((8, width), f32),
            jax.ShapeDtypeStruct((8, LANES), f32),
        ],
        cost_estimate=KERNEL_COST,
        compiler_params=params(),
        name="delta_backward",
    )(pos, resets, proj, small, proj, d_out, conv_w, aux, states, invs, deltas)


def local_call(body, name, inputs, specs, outs, bytes_accessed=0):
    return pl.pallas_call(
        body,
        grid=(1,),
        in_specs=specs,
        out_specs=whole_specs(outs),
        out_shape=outs,
        cost_estimate=SMALL_COST,
        compiler_params=pltpu.CompilerParams(vmem_limit_bytes=VMEM_BYTES),
        name=name,
    )(*inputs)


def term_specs(terms):
    kept, got, steps = terms
    rows_n = kept.shape[0]
    first = pl.BlockSpec((rows_n, 1) + kept.shape[2:], lambda i: (0, 0, 0, 0))
    flat = [step for row in steps for step in row]
    return [kept, got] + flat, [first, first] + [pl.BlockSpec((1,) + s.shape[1:], lambda i: (0, 0, 0)) for s in flat]


def row_total(refs, row, rows_n):
    kept, got = refs[0], refs[1]
    each = (len(refs) - 2) // rows_n
    total = kept[row, 0].astype(f32) + got[row, 0].astype(f32)
    for step in refs[2 + row * each : 2 + (row + 1) * each]:
        total = total + step[0].astype(f32)
    return total


def in_order(values, groups):
    size, batches = groups
    own = values.shape[-1] // (size * batches)
    return jnp.concatenate(
        [
            values[:, (b * size + s) * own : (b * size + s + 1) * own]
            for s in range(size)
            for b in range(batches)
        ],
        axis=1,
    )


def whole_specs(arrays):
    zeros = lambda n: lambda i: (0,) * n
    return [pl.BlockSpec(a.shape, zeros(len(a.shape))) for a in arrays]


def add_and_norm(terms, base, gain):
    inputs, specs = term_specs(terms)
    rows_n, _, span, _ = terms[0].shape

    def body(*refs):
        base_ref, gain_ref, out_ref, norm_ref = refs[len(inputs) :]
        for row in range(rows_n):
            at = pl.ds(row * span, span)
            total = base_ref[at, :].astype(f32) + row_total(refs[: len(inputs)], row, rows_n)
            scale = lax.rsqrt(jnp.mean(total * total, axis=-1, keepdims=True) + EPS_NORM)
            out_ref[at, :] = total
            norm_ref[row] = (total * scale * gain_ref[...]).astype(bf16)

    extra = [base, gain.reshape(1, D)]
    return local_call(
        body,
        "add_and_norm",
        inputs + extra,
        specs + whole_specs(extra),
        [jax.ShapeDtypeStruct((rows_n * span, D), f32), jax.ShapeDtypeStruct((rows_n, span, D), bf16)],
        4_000_000,
    )


def norm_back(terms, base, through, gain, out_dtype, groups=None):
    inputs, specs = term_specs(terms)
    rows_n, _, span, _ = terms[0].shape
    with_rows = groups is None

    def body(*refs):
        base_ref, through_ref, gain_ref = refs[len(inputs) : len(inputs) + 3]
        outs = refs[len(inputs) + 3 :]
        g_gain = jnp.zeros((1, D), f32)
        for row in range(rows_n):
            at = pl.ds(row * span, span)
            d_norm = row_total(refs[: len(inputs)], row, rows_n)
            x = base_ref[at, :].astype(f32)
            scale = lax.rsqrt(jnp.mean(x * x, axis=-1, keepdims=True) + EPS_NORM)
            e = d_norm * gain_ref[...]
            lean = jnp.mean(e * x, axis=-1, keepdims=True)
            total = through_ref[at, :].astype(f32) + scale * e - x * (scale * scale * scale * lean)
            g_gain = g_gain + jnp.sum(d_norm * x * scale, axis=0, keepdims=True)
            if with_rows:
                outs[0][at, :] = total.astype(out_dtype)
                outs[1][row] = total.astype(bf16)
            else:
                outs[0][at, :] = in_order(total, groups).astype(out_dtype)
        outs[-1][...] = g_gain

    extra = [base, through, gain.reshape(1, D)]
    outs = [jax.ShapeDtypeStruct((rows_n * span, D), out_dtype)]
    if with_rows:
        outs.append(jax.ShapeDtypeStruct((rows_n, span, D), bf16))
    return local_call(
        body,
        "norm_back",
        inputs + extra,
        specs + whole_specs(extra),
        outs + [jax.ShapeDtypeStruct((1, D), f32)],
        4_000_000,
    )


def add_in_order(terms, base, groups):
    inputs, specs = term_specs(terms)
    rows_n, _, span, _ = terms[0].shape

    def body(*refs):
        base_ref, out_ref = refs[len(inputs) :]
        for row in range(rows_n):
            at = pl.ds(row * span, span)
            total = base_ref[at, :] + row_total(refs[: len(inputs)], row, rows_n)
            out_ref[at, :] = in_order(total, groups).astype(bf16)

    return local_call(
        body,
        "add_in_order",
        inputs + [base],
        specs + whole_specs([base]),
        [jax.ShapeDtypeStruct((rows_n * span, D), bf16)],
        3_000_000,
    )[0]


ROW_BLOCK = 256


def gated_norm(mixed, proj, gain):
    rows_n, width = mixed.shape
    gate_block = pl.BlockSpec((ROW_BLOCK, width), lambda i: (i, proj.shape[1] // width - 1))

    def body(mixed_ref, gate_ref, gain_ref, out_ref):
        for at in range(0, width, DV):
            x = mixed_ref[:, at : at + DV]
            g = gate_ref[:, at : at + DV]
            scale = lax.rsqrt(jnp.mean(x * x, axis=-1, keepdims=True) + EPS_HEAD)
            out_ref[:, at : at + DV] = (x * scale * gain_ref[...] * (g * jax.nn.sigmoid(g))).astype(bf16)

    block = pl.BlockSpec((ROW_BLOCK, width), lambda i: (i, 0))
    return pl.pallas_call(
        body,
        grid=(rows_n // ROW_BLOCK,),
        in_specs=[block, gate_block, pl.BlockSpec((1, DV), lambda i: (0, 0))],
        out_specs=block,
        out_shape=jax.ShapeDtypeStruct((rows_n, width), bf16),
        cost_estimate=SMALL_COST,
        compiler_params=params(),
        name="gated_norm",
    )(mixed, proj, gain.reshape(1, DV))


def gated_norm_back(mixed, proj, gain, d_out):
    rows_n, width = mixed.shape
    gate_block = pl.BlockSpec((ROW_BLOCK, width), lambda i: (i, proj.shape[1] // width - 1))

    def body(mixed_ref, gate_ref, gain_ref, d_ref, d_mixed_ref, d_gate_ref, g_gain_ref):
        @pl.when(pl.program_id(0) == 0)
        def _():
            g_gain_ref[...] = jnp.zeros_like(g_gain_ref)

        g_gain = jnp.zeros((1, DV), f32)
        for at in range(0, width, DV):
            x = mixed_ref[:, at : at + DV]
            g = gate_ref[:, at : at + DV]
            d = d_ref[:, at : at + DV]
            scale = lax.rsqrt(jnp.mean(x * x, axis=-1, keepdims=True) + EPS_HEAD)
            sig = jax.nn.sigmoid(g)
            through = d * (g * sig)
            unit_x = x * scale
            e = through * gain_ref[...]
            lean = jnp.mean(e * unit_x, axis=-1, keepdims=True)
            d_mixed_ref[:, at : at + DV] = scale * (e - unit_x * lean)
            d_gate_ref[:, at : at + DV] = (
                d * (unit_x * gain_ref[...]) * (sig * (1.0 + g * (1.0 - sig)))
            ).astype(bf16)
            g_gain = g_gain + jnp.sum(through * unit_x, axis=0, keepdims=True)
        g_gain_ref[0:1, :] += g_gain

    block = pl.BlockSpec((ROW_BLOCK, width), lambda i: (i, 0))
    return pl.pallas_call(
        body,
        grid=(rows_n // ROW_BLOCK,),
        in_specs=[block, gate_block, pl.BlockSpec((1, DV), lambda i: (0, 0)), block],
        out_specs=[block, block, pl.BlockSpec((8, DV), lambda i: (0, 0))],
        out_shape=[
            jax.ShapeDtypeStruct((rows_n, width), f32),
            jax.ShapeDtypeStruct((rows_n, width), bf16),
            jax.ShapeDtypeStruct((8, DV), f32),
        ],
        cost_estimate=SMALL_COST,
        compiler_params=params(),
        name="gated_norm_back",
    )(mixed, proj, gain.reshape(1, DV), d_out)


def laid_out(blocks, pieces, total):
    size, rows_n, _ = blocks[0].shape

    def body(*refs):
        out_ref = refs[-1]
        for which, first, width, start in pieces:
            for s in range(size):
                out_ref[:, start + s * width : start + (s + 1) * width] = refs[which][
                    s, :, first : first + width
                ].astype(f32)

    return local_call(
        body, "laid_out", blocks, whole_specs(blocks), [jax.ShapeDtypeStruct((rows_n, total), f32)], 5_000_000
    )[0]


def swap(value, axis, bit):
    return lax.ppermute(value, axis, [(i, i ^ bit) for i in range(lax.axis_size(axis))])


def routes(axis):
    bits = [1 << i for i in range(lax.axis_size(axis).bit_length() - 1)]
    return [bits[1:] + bits[:1], bits[:0:-1] + bits[:1]]


def gather_rows(rows, axis, ordered=True, earlier=None):
    laid = []
    for row, order in zip(rows, routes(axis) * rows.shape[0]):
        held = row[None]
        names = [0]
        parts = []
        for i, bit in enumerate(order[:-1]):
            got = swap(held, axis, bit)
            names = names + [n ^ (bit >> 1) for n in names]
            if i < len(order) - 2:
                held = jnp.concatenate([held, got], axis=0)
            else:
                parts = [held, got]
        if ordered and names != sorted(names):
            place = {name: i for i, name in enumerate(names)}
            size = len(names) // 2
            for n in sorted(names):
                which, at = divmod(place[n], size)
                laid.append(parts[which][at : at + 1])
        else:
            laid.extend(parts)
    even = jnp.concatenate(laid, axis=0).reshape((rows.shape[0], -1) + rows.shape[1:])
    if earlier is not None:
        even, earlier = lax.optimization_barrier((even, earlier))
        return even, swap(even, axis, 1), earlier
    return even, swap(even, axis, 1)


def scatter_rows(keep, send, axis, ordered=True, earlier=()):
    got = after(swap(send, axis, 1), *earlier)
    rows_n, half, span, width = keep.shape
    depth = half.bit_length() - 1
    steps = []
    for row, order in zip(range(rows_n), routes(axis) * rows_n):
        bits = order[:-1]
        axes = sorted(bits, reverse=True) if ordered else bits[::-1]
        shape = (2,) * depth + (span, width)
        terms = [keep[row].reshape(shape), got[row].reshape(shape)]
        mine = []
        for bit in bits[::-1]:
            at = axes.index(bit)
            sent = sum(lax.index_in_dim(t, 1, at, keepdims=False).astype(f32) for t in terms).astype(bf16)
            back = swap(sent, axis, bit)
            terms = [lax.index_in_dim(t, 0, at, keepdims=False) for t in terms] + [back]
            axes = [b for b in axes if b != bit]
            mine.append(back.reshape((-1, span, width)))
        steps.append(mine)
    return keep, got, steps


def joined(halves):
    return jnp.concatenate([h.reshape(-1, h.shape[-1]) for h in halves], axis=0)


def after(value, *earlier):
    return lax.optimization_barrier((value,) + earlier)[0]


def sum_all(value, axes):
    for axis in axes:
        for i in range(lax.axis_size(axis).bit_length() - 1):
            value = value + swap(value, axis, 1 << i)
    return value


def gather_small(value, axis):
    held = value[None]
    size = lax.axis_size(axis)
    for i in range(size.bit_length() - 1):
        held = jnp.concatenate([held, swap(held, axis, 1 << i)], axis=0)
    return held[jnp.arange(size, dtype=jnp.int32) ^ lax.axis_index(axis).astype(jnp.int32)]


def mm(left, right):
    return jnp.dot(left, right, preferred_element_type=f32)


def contract_rows(left, right):
    return lax.dot_general(left, right, (((0,), (0,)), ((), ())), preferred_element_type=f32)


def contract_cols(left, right):
    return lax.dot_general(left, right, (((1,), (1,)), ((), ())), preferred_element_type=f32)


def rms_scale(values, scale_gain):
    return values * lax.rsqrt(jnp.mean(values * values, axis=-1, keepdims=True) + EPS_NORM) * scale_gain


def glu_hidden(gate_half, up_half):
    return jax.nn.silu(gate_half) * up_half


def exchanged(packed):
    return lax.all_to_all(packed, "seq", split_axis=0, concat_axis=0, tiled=True)


def stacked(blocks):
    full = lax.all_gather(blocks, "batch", axis=0, tiled=False)
    return full.reshape(-1, blocks.shape[-1])


def summed(partial_grad):
    own = lax.psum_scatter(partial_grad, "batch", scatter_dimension=0, tiled=True)
    return own.reshape(lax.axis_size("seq"), -1, own.shape[-1])


def shards(
    tokens,
    grad_out,
    resets,
    w_proj,
    w_small,
    w_out,
    w_gu,
    w_down,
    norm_in,
    norm_ff,
    norm_head,
    conv_w,
    a_log,
    dt_bias,
):
    size = lax.axis_size("seq")
    groups = lax.axis_size("batch")
    me = lax.axis_index("seq")
    batch_rows, span_len, _ = tokens.shape
    own_rows = w_proj.shape[0]
    heads = H // size
    ff = FF // size
    key_w, val_w = heads * DK, heads * DV
    conv_cols = 2 * key_w + val_w
    half = batch_rows * size // 2 * span_len
    halves = (batch_rows, size // 2, span_len)
    blocks = (2,) + halves

    def shuffled(array):
        lead = array.shape[:-1]
        return array.reshape(lead + (size, groups, own_rows)).swapaxes(-3, -2).reshape(lead + (D,))

    def restored(array):
        lead = array.shape[:-1]
        return array.reshape(lead + (groups, size, own_rows)).swapaxes(-3, -2).reshape(lead + (D,))

    out_w = lax.all_gather(w_out, "batch", axis=0, tiled=True)
    packed_mix = jnp.concatenate(
        [
            w_proj[:, :KW].reshape(own_rows, size, key_w),
            w_proj[:, KW : 2 * KW].reshape(own_rows, size, key_w),
            w_proj[:, 2 * KW : CW].reshape(own_rows, size, val_w),
            w_proj[:, CW:].reshape(own_rows, size, val_w),
        ],
        axis=-1,
    ).transpose(1, 0, 2)
    moved_mix = exchanged(packed_mix)
    own_in = shuffled(tokens).reshape(-1, D)
    gain_in, gain_ff = shuffled(norm_in), shuffled(norm_ff)
    h_in = joined(gather_rows(rms_scale(own_in.astype(f32), gain_in).astype(bf16).reshape(tokens.shape), "seq"))
    mix_w = stacked(after(moved_mix, out_w, h_in))
    packed_gu, w_small, d_own, own_down = after(
        (
            w_gu.reshape(own_rows, 2, size, ff).transpose(2, 0, 1, 3).reshape(size, own_rows, 2 * ff),
            w_small,
            shuffled(grad_out),
            shuffled(w_down),
        ),
        moved_mix,
    )
    d_halves = gather_rows(d_own, "seq", False)
    small_all = gather_small(gather_small(w_small, "batch"), "seq").swapaxes(0, 1).reshape(D, 2 * H)
    small_w = jnp.pad(
        jnp.concatenate(
            [
                lax.dynamic_slice_in_dim(small_all, me * heads, heads, 1),
                lax.dynamic_slice_in_dim(small_all, H + me * heads, heads, 1),
            ],
            axis=1,
        ),
        ((0, 0), (0, LANES - 2 * heads)),
    )
    out_w = shuffled(out_w)
    moved_gu = exchanged(packed_gu)

    slots = jnp.arange(size, dtype=jnp.int32) ^ me.astype(jnp.int32)
    conv_l = jnp.concatenate(
        [
            lax.dynamic_slice_in_dim(conv_w, me * key_w, key_w, 1),
            lax.dynamic_slice_in_dim(conv_w, KW + me * key_w, key_w, 1),
            lax.dynamic_slice_in_dim(conv_w, 2 * KW + me * val_w, val_w, 1),
        ],
        axis=1,
    )
    at_heads = (heads, LANES - 2 * heads)
    aux = jnp.pad(
        jnp.stack(
            [
                lax.dynamic_slice_in_dim(jnp.exp(a_log), me * heads, heads),
                lax.dynamic_slice_in_dim(dt_bias, me * heads, heads),
            ]
        ),
        ((0, 6), at_heads),
    )

    small = mm(h_in, small_w).reshape(blocks + (LANES,))
    proj = mm(h_in, mix_w)
    down_first = lax.all_gather(own_down[:, : D // 2], "batch", axis=0, tiled=True)
    prepared = mixer_prepare(proj.reshape(blocks + (-1,)), small, slots, resets, conv_l, aux)
    prepared, moved_gu = lax.optimization_barrier((prepared, moved_gu))
    down_rest = lax.all_gather(own_down[:, D // 2 :], "batch", axis=0, tiled=True)
    gu_w = stacked(moved_gu)
    mixed, states, invs, deltas = mixer_scan(prepared, slots, batch_rows)
    mixed = mixed.reshape(-1, val_w)
    z_rows = gated_norm(mixed, proj, norm_head)

    def parts(product, left):
        send = product(left[half:]).astype(bf16).reshape(halves + (D,))
        return product(left[:half]).astype(bf16).reshape(halves + (D,)), send

    keep, send = parts(lambda rows: mm(rows, out_w), z_rows)
    d_out = joined(after(d_halves, keep, send))
    residual, normed_ff = add_and_norm(scatter_rows(keep, send, "seq"), own_in, gain_ff)

    even, odd, gu_w = gather_rows(normed_ff, "seq", False, gu_w)
    h_ff = joined((even, odd))
    gate_up = mm(h_ff, gu_w)
    hidden_full, pull_glu = jax.vjp(glu_hidden, gate_up[:, :ff], gate_up[:, ff:])
    hidden = hidden_full.astype(bf16)
    down_grad = contract_rows(d_out, hidden).astype(bf16)
    hidden, down_rest = lax.optimization_barrier((hidden, down_rest))
    down_own = summed(down_grad)
    d_hidden = contract_cols(d_out[:, : D // 2], down_first) + contract_cols(d_out[:, D // 2 :], down_rest)
    down_w = jnp.concatenate([down_first, down_rest], axis=1)
    d_gate_up = jnp.concatenate(pull_glu(d_hidden), axis=1).astype(bf16)
    keep, send = parts(lambda rows: contract_cols(rows, gu_w), d_gate_up)
    terms = scatter_rows(keep, send, "seq", False)
    gu_grad = contract_rows(after(h_ff, keep, send), d_gate_up).astype(bf16)
    gu_own = summed(gu_grad)
    out_parts = parts(lambda rows: mm(rows, down_w), after(hidden, keep, send))
    d_residual, d_branch, g_norm_ff = norm_back(terms, residual, d_own.reshape(-1, D), gain_ff, f32)

    d_branch = joined(gather_rows(after(d_branch, gu_grad, down_own, out_parts), "seq"))
    d_heads = contract_cols(d_branch, out_w)
    d_mixed, d_gate, g_norm_head = gated_norm_back(mixed, proj, norm_head, d_heads)
    out_grad = jnp.concatenate(
        [contract_rows(h_in, d_gate).astype(bf16), contract_rows(d_branch, z_rows).astype(bf16)], axis=1
    )
    d_mixed, out_grad = lax.optimization_barrier((d_mixed, out_grad))
    d_proj, d_small, g_conv_l, g_decay = mixer_backward(
        proj.reshape(blocks + (-1,)), small, d_mixed.reshape(blocks + (val_w,)), slots, resets, conv_l, aux, states, invs, deltas
    )
    d_proj, gu_own = lax.optimization_barrier((d_proj.reshape(-1, conv_cols), gu_own))
    d_small = d_small.reshape(-1, LANES)
    out_own = summed(out_grad)
    mix_grad = contract_rows(h_in, d_proj).astype(bf16)
    mix_moved = lax.all_to_all(
        mix_grad.reshape(groups, size, own_rows, conv_cols), "seq", split_axis=1, concat_axis=1, tiled=True
    )
    d_proj, d_small, g_conv_l, gu_own = after((d_proj, d_small, g_conv_l, gu_own), mix_grad)
    mix_moved, gu_own = lax.optimization_barrier((mix_moved, gu_own))
    mix_grads = lax.psum_scatter(mix_moved, "batch", scatter_dimension=0, tiled=True)[0]
    gu_grads, down_grads = exchanged(gu_own), exchanged(down_own)
    block_out = add_in_order(scatter_rows(*out_parts, "seq", False), residual, (size, groups))
    keep, send = parts(
        lambda rows: contract_cols(rows[:, : conv_cols + val_w], mix_w)
        + contract_cols(rows[:, conv_cols + val_w :], small_w),
        jnp.concatenate([d_proj, d_gate, d_small], axis=1),
    )
    d_tokens, g_norm_in = norm_back(
        scatter_rows(keep, send, "seq"), own_in, after(d_residual, out_own), gain_in, bf16, (size, groups)
    )

    small_grad = contract_rows(d_small, h_in)[: 2 * heads]
    local = jnp.concatenate(
        [g_conv_l[:TAPS].reshape(-1), g_decay[:2, heads : 2 * heads].reshape(-1), small_grad.reshape(-1)]
    )
    shared = gather_small(sum_all(local, ("batch",)), "seq")
    g_conv_all = shared[:, : TAPS * conv_cols].reshape(size, TAPS, conv_cols).transpose(1, 0, 2)
    g_conv = jnp.concatenate(
        [
            g_conv_all[:, :, :key_w].reshape(TAPS, KW),
            g_conv_all[:, :, key_w : 2 * key_w].reshape(TAPS, KW),
            g_conv_all[:, :, 2 * key_w :].reshape(TAPS, VW),
        ],
        axis=1,
    )
    g_alog = shared[:, TAPS * conv_cols : TAPS * conv_cols + heads].reshape(H)
    g_dt = shared[:, TAPS * conv_cols + heads : TAPS * conv_cols + 2 * heads].reshape(H)
    g_small = lax.dynamic_slice_in_dim(
        shared[:, TAPS * conv_cols + 2 * heads :].reshape(size, 2, heads, D),
        (lax.axis_index("batch") * size + me) * own_rows,
        own_rows,
        3,
    )
    g_small = g_small.transpose(3, 1, 0, 2).reshape(own_rows, 2 * H)
    gains = sum_all(jnp.concatenate([g_norm_in[0], g_norm_ff[0], g_norm_head[0]]), ("seq", "batch"))
    gains = jnp.concatenate([restored(gains[: 2 * D].reshape(2, D)).reshape(-1), gains[2 * D :]])

    out_grads = exchanged(out_own)
    g_gu = laid_out([gu_grads], [(0, 0, ff, 0), (0, ff, ff, FF)], 2 * FF)
    g_down = down_grads.astype(f32).transpose(0, 2, 1).reshape(FF, own_rows)
    g_out = out_grads[:, :, val_w:].astype(f32).transpose(0, 2, 1).reshape(VW, own_rows)
    ready = (d_tokens, block_out, out_grads, g_gu, g_down, g_out, gains, g_conv, g_small)
    mix_grads, ready = lax.optimization_barrier((mix_grads, ready))
    d_tokens, block_out, out_grads, g_gu, g_down, g_out, gains, g_conv, g_small = ready
    g_proj = laid_out(
        [mix_grads, out_grads],
        [(0, 0, key_w, 0), (0, key_w, key_w, KW), (0, 2 * key_w, val_w, 2 * KW), (1, 0, val_w, CW)],
        CW + VW,
    )
    return (
        block_out.reshape(tokens.shape),
        d_tokens.reshape(tokens.shape),
        g_proj,
        g_small,
        g_out,
        g_gu,
        g_down,
        gains[:D],
        gains[D : 2 * D],
        gains[2 * D :],
        g_conv,
        g_alog,
        g_dt,
    )


def solution(mesh):
    rows = P(("seq", "batch"), None)
    cols = P(None, ("seq", "batch"))
    act = P("batch", "seq", None)
    in_specs = (act, act, P("batch"), rows, rows, rows, rows, rows) + (P(),) * 6
    out_specs = (act, act, rows, rows, cols, rows, cols) + (P(),) * 6
    return jax.shard_map(shards, mesh=mesh, in_specs=in_specs, out_specs=out_specs, check_vma=False)
```
